32 devices in a mesh: gx: 8 (over z, x), gy: 4 (over y, core).
Axes of the slice: x: 2, y: 2, z: 4, core: 2. Of those that a mesh axis runs over, the one named last changes fastest.
Arguments:
- velocity_guess: float32 [8, 2, 256, 1024], P(None, None, 'gx', 'gy'), may hold values from -6 to 6
- friction: bfloat16 [8, 256, 1024], P(None, 'gx', 'gy'), may hold values from 0.5 to 4
- thickness: float32 [256, 1024], P('gx', 'gy'), may hold values from 0.5 to 4.5
- surface: float32 [256, 1024], P('gx', 'gy'), may hold values from -4 to 324
- ice_mask: int32 [256, 1024], P('gx', 'gy'), may hold values 0 or 1
- grounded_mask: int32 [256, 1024], P('gx', 'gy'), may hold values 0 or 1
Outputs:
- velocity: float32 [8, 2, 256, 1024], P(None, None, 'gx', 'gy')
The draws below stay inside these ranges and needn't reach their ends.
All inputs are finite; a program needn't handle non-finite values. No bound on the sum of `ice_mask` or of `grounded_mask` on one device may be relied on, other than what follows from the above.
Results may differ from the reference program's by a relative error of at most 0.0003.
Values sent between devices are 32-bit elements; how exact they have to be, the bound alone decides.
No kernel may reach another device: no remote copies, remote signals or barrier semaphores. Data moves between devices by JAX's collectives and lax.ppermute only.
A program may use at most 64 MiB of HBM per device.

```python
import math
import jax
import jax.numpy as jnp
from jax import lax

MEMBERS = 8
NX = 256
NY = 1024


def draw_thickness(key, part):
    rows = jnp.arange(NX, dtype=jnp.float32)[:, None] / float(max(NX - 1, 1))
    rough = jax.random.uniform(key, (NX, NY), jnp.float32, 0.5, 1.5)
    trend = 1.0 + 2.0 * rows
    return trend * rough


def draw_surface(key, part):
    rough = jax.random.truncated_normal(key, -4.0, 4.0, (NX, NY), jnp.float32)
    return rough


def plant(entries, own_key, least, top_value):
    index_at = [jax.random.randint(jax.random.fold_in(own_key, axis), (), 0, length) for axis, length in enumerate(entries.shape)]
    widest = entries.shape.index(max(entries.shape))
    beside = index_at[:widest] + [(index_at[widest] + 1) % entries.shape[widest]] + index_at[widest + 1:]
    return entries.at[tuple(index_at)].set(least).at[tuple(beside)].set(top_value)


def level_of(rng, shape, shards, low, largest):
    loudness = 1.0
    for position, parts in shards:
        steps = jax.random.uniform(jax.random.fold_in(jax.random.fold_in(rng, 6), position), (parts,), jnp.float32, low / len(shards), largest / len(shards))
        loudness = loudness * jnp.repeat(jnp.exp(steps), shape[position] // parts).reshape((-1,) + (1,) * (len(shape) - 1 - position))
    return loudness


def scatter_about(key, dims, spread, bound, shards=(), kind=jnp.bfloat16):
    gain = level_of(key, dims, shards, -0.22, 0.18) if shards else 1.0
    entries = jax.random.normal(key, dims, jnp.float32) * spread * gain
    return jnp.minimum(jnp.maximum(entries, -bound), bound).astype(kind)


def setup_inputs(seed: int = 0) -> dict:
    key_list = jax.random.split(jax.random.key(seed), 7)
    return {
        "velocity_guess": scatter_about(key_list[0], (MEMBERS, 2, NX, NY), 1.0, 6.0, ((2, 8), (3, 4)), jnp.float32),
        "friction": jnp.clip(jnp.exp(math.log(4.0) - 2.0794415 * jax.random.uniform(key_list[1], (MEMBERS, NX, NY), jnp.float32) ** level_of(key_list[1], (MEMBERS, NX, NY), ((1, 8), (2, 4)), -0.2, 0.2)), 0.5, 4.0).astype(jnp.bfloat16),
        "thickness": draw_thickness(jax.random.fold_in(key_list[6], 71), 0),
        "surface": draw_surface(jax.random.fold_in(key_list[6], 71), 0),
        "ice_mask": plant((jax.random.randint(key_list[4], (NX, NY), 0, 8) < 7).astype(jnp.int32), jax.random.fold_in(key_list[4], 1), 0, 1),
        "grounded_mask": plant((jax.random.randint(key_list[5], (NX, NY), 0, 2) < 1).astype(jnp.int32), jax.random.fold_in(key_list[5], 1), 0, 1),
    }


strain_floor = 0.1
water_drag = 0.25
flow_power = 1.0 / 3.0


def diff_rows(field):
    padded = jnp.pad(field, ((1, 1), (0, 0)))
    return 0.5 * (padded[2:] - padded[:-2])


def diff_cols(field):
    padded = jnp.pad(field, ((0, 0), (1, 1)))
    return 0.5 * (padded[:, 2:] - padded[:, :-2])


def strains(field_u, field_v):
    return diff_rows(field_u), diff_cols(field_v), diff_cols(field_u) + diff_rows(field_v)


def reference(velocity_guess, friction, thickness, surface, ice_mask, grounded_mask):
    icef = ice_mask.astype(jnp.float32)
    groundf = grounded_mask.astype(jnp.float32)
    force_u = icef * (-(thickness * diff_rows(surface)))
    force_v = icef * (-(thickness * diff_cols(surface)))

    def member(item):
        guess, fric = item
        drag = icef * (groundf * fric.astype(jnp.float32) + water_drag)
        start_u = icef * guess[0]
        start_v = icef * guess[1]
        sa, sb, sc = strains(start_u, start_v)
        nu = icef * 0.5 * thickness * jnp.power(sa * sa + sb * sb + sa * sb + 0.25 * (sc * sc) + strain_floor, -flow_power)
        padnu = jnp.pad(nu, 1)
        near_rows = padnu[2:, 1:-1] + padnu[:-2, 1:-1]
        near_cols = padnu[1:-1, 2:] + padnu[1:-1, :-2]
        prec_u = icef * (near_rows + 0.25 * near_cols + drag) + (1.0 - icef)
        prec_v = icef * (near_cols + 0.25 * near_rows + drag) + (1.0 - icef)

        def operate(part_u, part_v):
            ka, kb, kc = strains(part_u, part_v)
            sxx = nu * (4.0 * ka + 2.0 * kb)
            syy = nu * (2.0 * ka + 4.0 * kb)
            sxy = nu * kc
            return (icef * (drag * part_u - diff_rows(sxx) - diff_cols(sxy)),
                    icef * (drag * part_v - diff_cols(syy) - diff_rows(sxy)))

        vel_u, vel_v = start_u, start_v
        image_u, image_v = operate(start_u, start_v)
        res_u = force_u - image_u
        res_v = force_v - image_v
        pre_u = res_u / prec_u
        pre_v = res_v / prec_v
        dir_u, dir_v = pre_u, pre_v
        norm_now = jnp.sum(res_u * pre_u) + jnp.sum(res_v * pre_v)
        for step in range(2):
            image_u, image_v = operate(dir_u, dir_v)
            alpha = norm_now / (jnp.sum(dir_u * image_u) + jnp.sum(dir_v * image_v))
            vel_u = vel_u + alpha * dir_u
            vel_v = vel_v + alpha * dir_v
            res_u = res_u - alpha * image_u
            res_v = res_v - alpha * image_v
            if step == 0:
                pre_u = res_u / prec_u
                pre_v = res_v / prec_v
                norm_next = jnp.sum(res_u * pre_u) + jnp.sum(res_v * pre_v)
                dir_u = pre_u + (norm_next / norm_now) * dir_u
                dir_v = pre_v + (norm_next / norm_now) * dir_v
                norm_now = norm_next
        return jnp.stack([vel_u, vel_v])

    return lax.map(member, (velocity_guess, friction))
```

```python
import functools

import jax
import jax.numpy as jnp
from jax import lax
from jax.experimental import pallas as pl
from jax.experimental.pallas import tpu as pltpu
from jax.sharding import PartitionSpec as P

strain_floor = 0.1
water_drag = 0.25
flow_power = 1.0 / 3.0

F32 = jnp.float32
DEPTH = 5
SIDE = 8
LANES = 128
PLANES = 4
GROUPS = LANES // SIDE
ROWS_PER_STRIP = GROUPS // PLANES


def vmem(shape):
    return pltpu.VMEM(shape, F32)


def call(kernel, outs, ins, scratch=(), flops=0):
    specs = [pl.BlockSpec(memory_space=pltpu.HBM if space == "hbm" else pltpu.VMEM) for space in ins]
    out_specs = [
        pl.BlockSpec(memory_space=pltpu.HBM if isinstance(o, jax.ShapeDtypeStruct) else pltpu.VMEM) for o in outs
    ]
    return pl.pallas_call(
        kernel,
        out_shape=outs,
        in_specs=specs,
        out_specs=out_specs,
        scratch_shapes=scratch,
        cost_estimate=pl.CostEstimate(flops=flops, bytes_accessed=flops // 8, transcendentals=0),
        compiler_params=pltpu.CompilerParams(vmem_limit_bytes=48 * 1024 * 1024),
    )


def lane_iota(shape):
    return lax.broadcasted_iota(jnp.int32, shape, len(shape) - 1)


def sublane_iota(shape):
    return lax.broadcasted_iota(jnp.int32, shape, len(shape) - 2)


def pack_kernel(
    vel, fric, thick, surf, ice, ground, own, to_left, to_right,
    vel_in, fric_in, thick_in, surf_in, ice_in, ground_in, friction32, sems,
):
    members, rows, cols = fric.shape
    tiles = cols // LANES
    copies = [
        pltpu.make_async_copy(source, target, sems.at[k])
        for k, (source, target) in enumerate(
            [(fric, fric_in), (thick, thick_in), (surf, surf_in), (ice, ice_in), (ground, ground_in)]
            + [(vel.at[:, pl.ds(t * LANES, LANES)], vel_in.at[t]) for t in range(tiles)]
        )
    ]
    for copy in copies:
        copy.start()
    for copy in copies:
        copy.wait()
    for t in range(tiles):
        friction32[t] = fric_in[:, :, t * LANES : (t + 1) * LANES].astype(F32).reshape(members * rows, LANES)
    group = lane_iota((members, LANES)) // SIDE
    sub = sublane_iota((members, LANES))

    def strip(block, carry):
        base = pl.multiple_of(block * 8, 8)
        near = []
        for t in range(tiles):
            part = slice(t * LANES, (t + 1) * LANES)
            icef = ice_in[pl.ds(base, 8), part].astype(F32)
            near.append(
                (
                    icef,
                    icef * ground_in[pl.ds(base, 8), part].astype(F32),
                    icef * thick_in[pl.ds(base, 8), part],
                    surf_in[pl.ds(base, 8), part],
                )
            )
        for half in range(8 // ROWS_PER_STRIP):
            heads = jnp.zeros((members, LANES), F32)
            tails = jnp.zeros((members, LANES), F32)
            for step in range(ROWS_PER_STRIP):
                at = half * ROWS_PER_STRIP + step
                row = base + at
                for t in range(tiles):
                    part = slice(t * LANES, (t + 1) * LANES)
                    icef, grounded, thin, top = (value[at : at + 1, :] for value in near[t])
                    field_u = vel_in[t, pl.ds(row, members, stride=2 * rows), :] * icef
                    field_v = vel_in[t, pl.ds(rows + row, members, stride=2 * rows), :] * icef
                    rough = friction32[t, pl.ds(row, members, stride=rows), :]
                    drag = grounded * rough + water_drag * icef
                    shared = jnp.where(sub == 0, thin, jnp.where(sub == 1, top, jnp.where(sub == 2, icef, 0.0)))
                    for plane, value in enumerate((field_u, field_v, drag, shared)):
                        own[row, plane, :, part] = value
                        place = step * PLANES + plane
                        if t == 0:
                            head = pltpu.roll(value, place * SIDE, 1) if place else value
                            heads = jnp.where(group == place, head, heads)
                        if t == tiles - 1:
                            tail = pltpu.roll(value, (place + 1) * SIDE, 1) if place != GROUPS - 1 else value
                            tails = jnp.where(group == place, tail, tails)
            to_left[block * (8 // ROWS_PER_STRIP) + half] = heads
            to_right[block * (8 // ROWS_PER_STRIP) + half] = tails
        return carry

    lax.fori_loop(0, rows // 8, strip, 0)


def side_tile(from_left, from_right, row, plane, lane):
    block, step = row // ROWS_PER_STRIP, row % ROWS_PER_STRIP
    place = step * PLANES + plane
    right = from_right[block]
    left = from_left[block]
    if place:
        right = pltpu.roll(right, LANES - place * SIDE, 1)
    if place != GROUPS - 1:
        left = pltpu.roll(left, LANES - (place + 1) * SIDE, 1)
    return jnp.where(lane < SIDE, right, jnp.where(lane >= LANES - SIDE, left, 0.0))


def edge_kernel(own, from_left, from_right, to_up, to_down):
    rows, _, members, cols = own.shape
    lane = lane_iota((members, LANES))
    for step in range(DEPTH):
        for target, row in ((to_up, step), (to_down, rows - DEPTH + step)):
            for plane in range(PLANES):
                target[step, plane, :, :cols] = own[row, plane]
                target[step, plane, :, cols:] = side_tile(from_left, from_right, row, plane, lane)


def loop(low, high, block, body, carry=0):
    count = high - low
    whole = count // block

    def step(index, carry):
        return body(low + index * block, block, carry)

    carry = lax.fori_loop(0, whole, step, carry)
    if count % block:
        carry = body(low + whole * block, count % block, carry)
    return carry


def compute_kernel(
    own, from_left, from_right, from_up, from_down, sums, along, across,
    field, visc, sx, sy, sz, rest, inverse,
):
    rows, _, members, cols = own.shape
    wide = cols + LANES
    lane = lane_iota((members, LANES))

    for step in range(DEPTH):
        field[step] = from_up[step]
        field[DEPTH + rows + step] = from_down[step]

    def place(block, carry):
        base = block * ROWS_PER_STRIP
        for step in range(ROWS_PER_STRIP):
            for plane in range(PLANES):
                item = step * PLANES + plane
                right = from_right[block]
                left = from_left[block]
                if item:
                    right = pltpu.roll(right, LANES - item * SIDE, 1)
                if item != GROUPS - 1:
                    left = pltpu.roll(left, LANES - (item + 1) * SIDE, 1)
                field[DEPTH + base + step, plane, :, :cols] = own[base + step, plane]
                field[DEPTH + base + step, plane, :, cols:] = jnp.where(
                    lane < SIDE, right, jnp.where(lane >= LANES - SIDE, left, 0.0)
                )
        return carry

    lax.fori_loop(0, rows // ROWS_PER_STRIP, place, 0)

    def spread(row, sub):
        return jnp.broadcast_to(field[row, 3, pl.ds(sub, 1), :], (members, wide))

    def after(value):
        return pltpu.roll(value, wide - 1, 1)

    def before(value):
        return pltpu.roll(value, 1, 1)

    def stress(row, strain_u, strain_v, strain_c, nu):
        half = 0.5 * nu
        sx[row] = half * (2.0 * strain_u + strain_v)
        sy[row] = half * (strain_u + 2.0 * strain_v)
        sz[row] = half * (0.5 * strain_c)

    def strains(ref_u, ref_v, first, count):
        us = [ref_u(first - 1 + k) for k in range(count + 2)]
        vs = [ref_v(first - 1 + k) for k in range(count + 2)]
        for k in range(count):
            yield (
                first + k,
                us[k + 2] - us[k],
                after(vs[k + 1]) - before(vs[k + 1]),
                (after(us[k + 1]) - before(us[k + 1])) + (vs[k + 2] - vs[k]),
            )

    last = rows + 2 * DEPTH

    def viscosity(first, count, carry):
        for row, su, sv, sc in strains(lambda r: field[r, 0], lambda r: field[r, 1], first, count):
            square = 0.25 * (su * su + sv * sv + su * sv + 0.25 * (sc * sc)) + strain_floor
            nu = (0.5 * spread(row, 0)) * jnp.exp(-flow_power * jnp.log(square))
            visc[row] = nu
            stress(row, su, sv, sc, nu)
        return carry

    loop(1, last - 1, 2, viscosity)

    def divergences(first, count):
        for row in range(count):
            row = first + row
            z = sz[row]
            y = sy[row]
            yield (
                row,
                (sx[row + 1] - sx[row - 1]) + (after(z) - before(z)),
                (after(y) - before(y)) + (sz[row + 1] - sz[row - 1]),
            )

    def residual(first, count, carry):
        for row, div_u, div_v in divergences(first, count):
            drag = field[row, 2]
            thin = spread(row, 0)
            icef = spread(row, 2)
            top = spread(row, 1)
            half = 0.5 * thin
            force_u = half * (spread(row - 1, 1) - spread(row + 1, 1))
            force_v = half * (before(top) - after(top))
            res_u = force_u - (drag * field[row, 0] - icef * div_u)
            res_v = force_v - (drag * field[row, 1] - icef * div_v)
            nu = visc[row]
            near_rows = visc[row + 1] + visc[row - 1]
            near_cols = after(nu) + before(nu)
            diag_u = near_rows + 0.25 * near_cols + drag
            diag_v = near_cols + 0.25 * near_rows + drag
            on = icef > 0.0
            inv_u = 1.0 / jnp.where(on, diag_u, 1.0)
            inv_v = 1.0 / jnp.where(on, diag_v, 1.0)
            rest[row, 0] = res_u
            rest[row, 1] = res_v
            inverse[row, 0] = inv_u
            inverse[row, 1] = inv_v
            along[row, 0] = res_u * inv_u
            along[row, 1] = res_v * inv_v
        return carry

    loop(2, last - 2, 2, residual)

    def direction(first, count, carry):
        for row, su, sv, sc in strains(lambda r: along[r, 0], lambda r: along[r, 1], first, count):
            stress(row, su, sv, sc, visc[row])
        return carry

    loop(3, last - 3, 2, direction)

    def image(first, count, carry):
        for row, div_u, div_v in divergences(first, count):
            drag = field[row, 2]
            icef = spread(row, 2)
            dir_u = along[row, 0]
            dir_v = along[row, 1]
            off_u = drag * dir_u - icef * div_u - rest[row, 0]
            off_v = drag * dir_v - icef * div_v - rest[row, 1]
            across[row, 0] = off_u * inverse[row, 0]
            across[row, 1] = off_v * inverse[row, 1]
        return carry

    loop(4, last - 4, 2, image)

    def energy(first, count, carry):
        norm, cross, square, power = carry
        for row, su, sv, sc in strains(lambda r: across[r, 0], lambda r: across[r, 1], first, count):
            su, sv, sc = su[:, :cols], sv[:, :cols], sc[:, :cols]
            drag = field[row, 2, :, :cols]
            nu = visc[row, :, :cols]
            res_u, res_v = rest[row, 0, :, :cols], rest[row, 1, :, :cols]
            dir_u, dir_v = along[row, 0, :, :cols], along[row, 1, :, :cols]
            off_u, off_v = across[row, 0, :, :cols], across[row, 1, :, :cols]
            norm = norm + (res_u * dir_u + res_v * dir_v)
            cross = cross + (res_u * off_u + res_v * off_v)
            square = square + (off_u * off_u / inverse[row, 0, :, :cols] + off_v * off_v / inverse[row, 1, :, :cols])
            power = power + (
                drag * (off_u * off_u + off_v * off_v)
                + nu * (su * su + su * sv + sv * sv + 0.25 * (sc * sc))
            )
        return norm, cross, square, power

    zero = jnp.zeros((members, cols), F32)
    totals = loop(DEPTH, DEPTH + rows, 2, energy, (zero,) * 4)
    sub = sublane_iota((members, LANES))
    row = jnp.zeros((members, LANES), F32)
    for k, total in enumerate(totals):
        row = row + jnp.where(lane == sub + members * k, jnp.sum(total, axis=1, keepdims=True), 0.0)
    row = jnp.sum(row, axis=0, keepdims=True)
    sums[...] = jnp.broadcast_to(row[None], sums.shape)


def final_kernel(parts, own, along, across, out, out_tiles, sems):
    rows, _, members, cols = own.shape
    total = jnp.sum(parts[...], axis=0)
    spread = jnp.broadcast_to(total, (members, LANES))
    lane = lane_iota((members, LANES))
    sub = sublane_iota((members, LANES))
    norm, cross, square, power = (
        jnp.sum(jnp.where(lane == sub + members * k, spread, 0.0), axis=1, keepdims=True) for k in range(4)
    )
    k1, k2, k3 = cross / norm, square / norm, power / norm
    scale = 1.0 + k1
    first = 1.0 / scale
    beta = (k2 - k1 * k1) * first * first
    curve = (k1 * k1 * scale - 2.0 * k1 * (k1 + k2) + k3) * first * first - beta * beta * scale
    second = jnp.where(curve > 0.0, beta / jnp.where(curve > 0.0, curve, 1.0), 0.0)
    on_along = jnp.broadcast_to(first + second * (k1 * first + beta), (members, LANES))
    on_across = jnp.broadcast_to(second * first, (members, LANES))
    tiles = cols // LANES

    def body(block, carry):
        for step in range(4):
            row = block * 4 + step
            for part in range(2):
                for t in range(tiles):
                    place = slice(t * LANES, (t + 1) * LANES)
                    out_tiles[t, pl.ds(part * rows + row, members, stride=2 * rows), :] = (
                        own[row, part, :, place]
                        + on_along * along[DEPTH + row, part, :, place]
                        - on_across * across[DEPTH + row, part, :, place]
                    )
        return carry

    lax.fori_loop(0, rows // 4, body, 0)
    copies = [
        pltpu.make_async_copy(out_tiles.at[t], out.at[:, pl.ds(t * LANES, LANES)], sems.at[t])
        for t in range(tiles)
    ]
    for copy in copies:
        copy.start()
    for copy in copies:
        copy.wait()


def shifted(axis, array, up):
    count = lax.axis_size(axis)
    pairs = [(i, i + 1) if up else (i + 1, i) for i in range(count - 1)]
    return lax.ppermute(array, axis, pairs)


def per_device(velocity_guess, friction, thickness, surface, ice_mask, grounded_mask):
    members, parts, rows, cols = velocity_guess.shape
    devices = lax.axis_size(("gx", "gy"))
    wide = cols + LANES
    high = rows + 2 * DEPTH
    strips = rows // ROWS_PER_STRIP
    tiles = cols // LANES
    flat = members * parts * rows
    own, to_left, to_right = call(
        pack_kernel,
        [
            vmem((rows, PLANES, members, cols)),
            vmem((strips, members, LANES)),
            vmem((strips, members, LANES)),
        ],
        ["hbm"] * 6,
        [
            pltpu.VMEM((tiles, flat, LANES), F32),
            pltpu.VMEM((members, rows, cols), friction.dtype),
            pltpu.VMEM((rows, cols), F32),
            pltpu.VMEM((rows, cols), F32),
            pltpu.VMEM((rows, cols), jnp.int32),
            pltpu.VMEM((rows, cols), jnp.int32),
            pltpu.VMEM((tiles, members * rows, LANES), F32),
            pltpu.SemaphoreType.DMA((5 + tiles,)),
        ],
    )(velocity_guess.reshape(flat, cols), friction, thickness, surface, ice_mask, grounded_mask)
    from_left = shifted("gy", to_right, True)
    from_right = shifted("gy", to_left, False)
    edge = vmem((DEPTH, PLANES, members, wide))
    to_up, to_down = call(edge_kernel, [edge, edge], ["vmem"] * 3)(own, from_left, from_right)
    from_up = shifted("gx", to_down, True)
    from_down = shifted("gx", to_up, False)
    two = (high, 2, members, wide)
    one = (high, members, wide)
    sums, along, across = call(
        compute_kernel,
        [vmem((devices, 1, LANES)), vmem(two), vmem(two)],
        ["vmem"] * 5,
        [vmem((high, PLANES, members, wide))] + [vmem(one)] * 4 + [vmem(two)] * 2,
    )(own, from_left, from_right, from_up, from_down)
    shares = lax.all_to_all(sums, ("gx", "gy"), 0, 0, tiled=True)
    (out,) = call(
        final_kernel,
        [jax.ShapeDtypeStruct((flat, cols), F32)],
        ["vmem"] * 4,
        [pltpu.VMEM((tiles, flat, LANES), F32), pltpu.SemaphoreType.DMA((tiles,))],
    )(shares, own, along, across)
    return out.reshape(members, parts, rows, cols)


def solution(mesh):
    placed = (
        P(None, None, "gx", "gy"),
        P(None, "gx", "gy"),
        P("gx", "gy"),
        P("gx", "gy"),
        P("gx", "gy"),
        P("gx", "gy"),
    )
    return jax.shard_map(
        per_device, mesh=mesh, in_specs=placed, out_specs=P(None, None, "gx", "gy"), check_vma=False
    )
```

```python
import functools

import jax
import jax.numpy as jnp
from jax import lax
from jax.experimental import pallas as pl
from jax.experimental.pallas import tpu as pltpu
from jax.sharding import PartitionSpec as P

strain_floor = 0.1
water_drag = 0.25
flow_power = 1.0 / 3.0

F32 = jnp.float32
DEPTH = 5
SIDE = 8
LANES = 128
PLANES = 4
GROUPS = LANES // SIDE
ROWS_PER_STRIP = GROUPS // PLANES
MOVING = DEPTH
DRAGGED = DEPTH - 2
SHARED = DEPTH - 1
TOTALS = 4


def vmem(shape):
    return pltpu.VMEM(shape, F32)


def call(kernel, outs, ins, scratch=(), flops=0, limit=24, aliases=None):
    specs = [pl.BlockSpec(memory_space=pltpu.HBM if space == "hbm" else pltpu.VMEM) for space in ins]
    out_specs = [
        pl.BlockSpec(memory_space=pltpu.HBM if isinstance(o, jax.ShapeDtypeStruct) else pltpu.VMEM) for o in outs
    ]
    return pl.pallas_call(
        kernel,
        out_shape=outs,
        in_specs=specs,
        out_specs=out_specs,
        scratch_shapes=scratch,
        input_output_aliases=aliases or {},
        cost_estimate=pl.CostEstimate(flops=flops, bytes_accessed=flops // 8, transcendentals=0),
        compiler_params=pltpu.CompilerParams(vmem_limit_bytes=limit * 1024 * 1024),
    )


def lane_iota(shape):
    return lax.broadcasted_iota(jnp.int32, shape, len(shape) - 1)


def sublane_iota(shape):
    return lax.broadcasted_iota(jnp.int32, shape, len(shape) - 2)


def swaps(axis):
    count = lax.axis_size(axis)
    inner = [(i, i ^ 1) if i ^ 1 < count else (i, i) for i in range(count)]
    if count % 2:
        outer = [(i, i + 1) if i % 2 else (i, i - 1) if i else (i, i) for i in range(count)]
    else:
        outer = [(i, (i + 1) % count) if i % 2 else (i, (i - 1) % count) for i in range(count)]
    return inner, outer


def neighbours(axis):
    index, count = lax.axis_index(axis), lax.axis_size(axis)
    lower = lax.rem(index, 2) == 0
    inner = jnp.logical_or(jnp.logical_not(lower), index + 1 < count)
    outer = jnp.where(lower, index > 0, index + 1 < count)
    return lower, inner, outer


def either(flag, first, second):
    return jnp.where(flag, first, second)


def pack_kernel(
    vel, fric, thick, surf, ice, ground, own, to_inner, to_outer,
    vel_in, fric_in, thick_in, surf_in, ice_in, ground_in, friction32, sems,
):
    members, rows, cols = fric.shape
    tiles = cols // LANES
    copies = [
        pltpu.make_async_copy(source, target, sems.at[k])
        for k, (source, target) in enumerate(
            [(fric, fric_in), (ice, ice_in), (ground, ground_in), (thick, thick_in), (surf, surf_in)]
            + [(vel.at[:, pl.ds(t * LANES, LANES)], vel_in.at[t]) for t in range(tiles)]
        )
    ]
    for copy in copies:
        copy.start()
    lower, _, _ = neighbours("gy")
    group = lane_iota((members, LANES)) // SIDE
    sub = sublane_iota((members, LANES))
    for copy in copies[:5]:
        copy.wait()
    for t in range(tiles):
        friction32[t] = fric_in[:, :, t * LANES : (t + 1) * LANES].astype(F32).reshape(members * rows, LANES)
    for copy in copies[5:]:
        copy.wait()
    near = {}
    for base in range(0, rows, 8):
        for t in range(tiles):
            part = slice(t * LANES, (t + 1) * LANES)
            icef = ice_in[base : base + 8, part].astype(F32)
            near[base, t] = (
                icef,
                icef * ground_in[base : base + 8, part].astype(F32),
                icef * thick_in[base : base + 8, part],
                surf_in[base : base + 8, part],
            )
    for strip in range(rows // ROWS_PER_STRIP):
        heads = jnp.zeros((members, LANES), F32)
        tails = jnp.zeros((members, LANES), F32)
        for step in range(ROWS_PER_STRIP):
            row = strip * ROWS_PER_STRIP + step
            at = row % 8
            for t in range(tiles):
                part = slice(t * LANES, (t + 1) * LANES)
                icef, grounded, thin, top = (value[at : at + 1, :] for value in near[row - at, t])
                field_u = vel_in[t, pl.ds(row, members, stride=2 * rows), :] * icef
                field_v = vel_in[t, pl.ds(rows + row, members, stride=2 * rows), :] * icef
                rough = friction32[t, pl.ds(row, members, stride=rows), :]
                drag = grounded * rough + water_drag * icef
                shared = jnp.where(sub == 0, thin, jnp.where(sub == 1, top, jnp.where(sub == 2, icef, 0.0)))
                for plane, value in enumerate((field_u, field_v, drag, shared)):
                    own[row, plane, :, part] = value
                    place = step * PLANES + plane
                    if t == 0:
                        head = pltpu.roll(value, place * SIDE, 1) if place else value
                        heads = jnp.where(group == place, head, heads)
                    if t == tiles - 1:
                        tail = pltpu.roll(value, (place + 1) * SIDE, 1) if place != GROUPS - 1 else value
                        tails = jnp.where(group == place, tail, tails)
        to_inner[strip] = either(lower, tails, heads)
        to_outer[strip] = either(lower, heads, tails)


def side_strips(from_inner, from_outer):
    lower, has_inner, has_outer = neighbours("gy")

    def strips(strip):
        inner = jnp.where(has_inner, from_inner[strip], 0.0)
        outer = jnp.where(has_outer, from_outer[strip], 0.0)
        return either(lower, outer, inner), either(lower, inner, outer)

    return strips


def unpacked(left, right, place, lane):
    if place:
        right = pltpu.roll(right, LANES - place * SIDE, 1)
    if place != GROUPS - 1:
        left = pltpu.roll(left, LANES - (place + 1) * SIDE, 1)
    return jnp.where(lane < SIDE, right, jnp.where(lane >= LANES - SIDE, left, 0.0))


def edge_items():
    moving = [(plane, k) for k in range(MOVING) for plane in (0, 1)]
    return moving + [(2, k) for k in range(DRAGGED)] + [(3, k) for k in range(0, SHARED, 2)]


def edge_tiles(cols):
    items = len(edge_items())
    per_tile = GROUPS // 2
    return items * (cols // LANES) + -(-items // per_tile)


def edge_kernel(own, from_inner, from_outer, to_inner, to_outer, field):
    rows, _, members, cols = own.shape
    tiles = cols // LANES
    lane = lane_iota((members, LANES))
    sub = sublane_iota((members, LANES))
    strips = side_strips(from_inner, from_outer)
    lower, _, _ = neighbours("gx")
    items = edge_items()
    per_tile = GROUPS // 2

    for first in (0, rows - 2 * ROWS_PER_STRIP):
        for strip in (first // ROWS_PER_STRIP, first // ROWS_PER_STRIP + 1):
            left, right = strips(strip)
            for step in range(ROWS_PER_STRIP):
                for plane in range(PLANES):
                    field[strip * ROWS_PER_STRIP + step, plane] = unpacked(
                        left, right, step * PLANES + plane, lane
                    )

    def tile_of(up, plane, k, t):
        depth = (MOVING, MOVING, DRAGGED, SHARED)[plane]
        row = k if up else rows - depth + k

        def one(row):
            return own[row, plane, :, t * LANES : (t + 1) * LANES] if t < tiles else field[row, plane]

        if plane < 3:
            return one(row)
        return jnp.where(sub < 4, one(row), pltpu.roll(one(row + 1), 4, 0))

    for target, up in ((to_inner, False), (to_outer, True)):
        at = 0
        sides = None
        for j, (plane, k) in enumerate(items):
            for t in range(tiles):
                target[at] = either(lower, tile_of(up, plane, k, t), tile_of(not up, plane, k, t))
                at += 1
            side = either(lower, tile_of(up, plane, k, tiles), tile_of(not up, plane, k, tiles))
            side = pltpu.roll(side, (SIDE + 2 * SIDE * (j % per_tile)) % LANES, 1)
            if j % per_tile == 0:
                sides = side
            else:
                sides = jnp.where(lane // (2 * SIDE) == j % per_tile, side, sides)
            if j % per_tile == per_tile - 1 or j == len(items) - 1:
                target[len(items) * tiles + j // per_tile] = sides


def stages(field, store, rows, members, cols):
    visc, sx, sy, sz, tx, ty, tz, rest, inverse, along, across = store
    wide = cols + LANES

    def spread(row, sub):
        return jnp.broadcast_to(field[row + DEPTH, 3, sub : sub + 1, :], (members, wide))

    def after(value):
        return pltpu.roll(value, wide - 1, 1)

    def before(value):
        return pltpu.roll(value, 1, 1)

    def strains(ref, row):
        row = row + DEPTH
        u, v = ref[row, 0], ref[row, 1]
        return (
            ref[row + 1, 0] - ref[row - 1, 0],
            after(v) - before(v),
            (after(u) - before(u)) + (ref[row + 1, 1] - ref[row - 1, 1]),
        )

    def stress(x, y, z, row, strain_u, strain_v, strain_c, nu):
        half = 0.5 * nu
        x[row + DEPTH] = half * (2.0 * strain_u + strain_v)
        y[row + DEPTH] = half * (strain_u + 2.0 * strain_v)
        z[row + DEPTH] = half * (0.5 * strain_c)

    def divergence(x, y, z, row):
        row = row + DEPTH
        shear, normal = z[row], y[row]
        return (
            (x[row + 1] - x[row - 1]) + (after(shear) - before(shear)),
            (after(normal) - before(normal)) + (z[row + 1] - z[row - 1]),
        )

    def viscosity(row):
        su, sv, sc = strains(field, row)
        square = 0.25 * (su * su + sv * sv + su * sv + 0.25 * (sc * sc)) + strain_floor
        nu = (0.5 * spread(row, 0)) * jnp.exp(-flow_power * jnp.log(square))
        visc[row + DEPTH] = nu
        stress(sx, sy, sz, row, su, sv, sc, nu)

    def reciprocal(value):
        guess = pltpu.reciprocal(value, approx=True)
        return guess * (2.0 - value * guess)

    def residual(row):
        div_u, div_v = divergence(sx, sy, sz, row)
        at = row + DEPTH
        drag = field[at, 2]
        icef = spread(row, 2)
        top = spread(row, 1)
        half = 0.5 * spread(row, 0)
        force_u = half * (spread(row - 1, 1) - spread(row + 1, 1))
        force_v = half * (before(top) - after(top))
        res_u = force_u - (drag * field[at, 0] - icef * div_u)
        res_v = force_v - (drag * field[at, 1] - icef * div_v)
        nu = visc[at]
        near_rows = visc[at + 1] + visc[at - 1]
        near_cols = after(nu) + before(nu)
        on = icef > 0.0
        inv_u = reciprocal(jnp.where(on, near_rows + 0.25 * near_cols + drag, 1.0))
        inv_v = reciprocal(jnp.where(on, near_cols + 0.25 * near_rows + drag, 1.0))
        rest[at, 0] = res_u
        rest[at, 1] = res_v
        inverse[at, 0] = inv_u
        inverse[at, 1] = inv_v
        along[at, 0] = res_u * inv_u
        along[at, 1] = res_v * inv_v

    def direction(row):
        su, sv, sc = strains(along, row)
        stress(tx, ty, tz, row, su, sv, sc, visc[row + DEPTH])

    def image(row, totals):
        div_u, div_v = divergence(tx, ty, tz, row)
        at = row + DEPTH
        drag = field[at, 2]
        icef = spread(row, 2)
        dir_u, dir_v = along[at, 0], along[at, 1]
        res_u, res_v = rest[at, 0], rest[at, 1]
        off_u = drag * dir_u - icef * div_u - res_u
        off_v = drag * dir_v - icef * div_v - res_v
        new_u = off_u * inverse[at, 0]
        new_v = off_v * inverse[at, 1]
        across[at, 0] = new_u
        across[at, 1] = new_v
        if 0 <= row < rows:
            totals[0] += (res_u * dir_u + res_v * dir_v)[:, :cols]
            totals[1] += (res_u * new_u + res_v * new_v)[:, :cols]
            totals[2] += (off_u * new_u + off_v * new_v)[:, :cols]

    def energy(row, totals):
        su, sv, sc = strains(across, row)
        at = row + DEPTH
        u, v = across[at, 0], across[at, 1]
        power = field[at, 2] * (u * u + v * v) + visc[at] * (su * su + su * sv + sv * sv + 0.25 * (sc * sc))
        totals[3] += power[:, :cols]

    return viscosity, residual, direction, image, energy


def run(steps, totals, ranges):
    viscosity, residual, direction, image, energy = steps
    for step, over in zip((viscosity, residual, direction), ranges[:3], strict=True):
        for row in over:
            step(row)
    for step, over in zip((image, energy), ranges[3:], strict=True):
        for row in over:
            step(row, totals)


def inner_ranges(rows):
    return [range(k, rows - k) for k in range(1, 6)]


def inner_kernel(own, from_inner, from_outer, field, *rest):
    store, totals_ref = rest[:11], rest[11]
    rows, _, members, cols = own.shape
    lane = lane_iota((members, LANES))
    strips = side_strips(from_inner, from_outer)
    for strip in range(rows // ROWS_PER_STRIP):
        left, right = strips(strip)
        for step in range(ROWS_PER_STRIP):
            row = strip * ROWS_PER_STRIP + step
            for plane in range(PLANES):
                field[row + DEPTH, plane, :, :cols] = own[row, plane]
                field[row + DEPTH, plane, :, cols:] = unpacked(left, right, step * PLANES + plane, lane)
    totals = [jnp.zeros((members, cols), F32) for _ in range(TOTALS)]
    run(stages(field, store, rows, members, cols), totals, inner_ranges(rows))
    for k, total in enumerate(totals):
        totals_ref[k] = total


def outer_kernel(from_inner, from_outer, totals_ref, *refs):
    sums, field, store = refs[12], refs[13], refs[14:25]
    high, _, members, wide = field.shape
    rows, cols = high - 2 * DEPTH, wide - LANES
    tiles = cols // LANES
    lane = lane_iota((members, LANES))
    items = edge_items()
    per_tile = GROUPS // 2
    lower, has_inner, has_outer = neighbours("gx")

    def both(k):
        inner = jnp.where(has_inner, from_inner[k], 0.0)
        outer = jnp.where(has_outer, from_outer[k], 0.0)
        return either(lower, outer, inner), either(lower, inner, outer)

    sides = [both(len(items) * tiles + k) for k in range(-(-len(items) // per_tile))]
    for j, (plane, k) in enumerate(items):
        depth = (MOVING, MOVING, DRAGGED, SHARED)[plane]
        ups = [DEPTH - depth + k]
        downs = [DEPTH + rows + k]
        if plane == 3:
            ups, downs = [ups[0], ups[0] + 1], [downs[0], downs[0] + 1]
        values = [both(j * tiles + t) for t in range(tiles)]
        shift = (LANES - (SIDE + 2 * SIDE * (j % per_tile))) % LANES
        ends = []
        for side in sides[j // per_tile]:
            side = pltpu.roll(side, shift, 1) if shift else side
            ends.append(jnp.where((lane < SIDE) | (lane >= LANES - SIDE), side, 0.0))
        values.append(tuple(ends))
        for t, pair in enumerate(values):
            for value, places in zip(pair, (ups, downs), strict=True):
                for n, place in enumerate(places):
                    field[place, plane, :, t * LANES : (t + 1) * LANES] = (
                        pltpu.roll(value, 4, 0) if n else value
                    )
    inner = inner_ranges(rows)
    ranges = [
        [row for row in range(k, rows - k) if row not in inner[k + 4]] for k in range(-4, 1)
    ]
    totals = [totals_ref[k] for k in range(TOTALS)]
    run(stages(field, store, rows, members, cols), totals, ranges)
    sub = sublane_iota((members, LANES))
    row = jnp.zeros((members, LANES), F32)
    for k, total in enumerate(totals):
        row = row + jnp.where(lane == sub + members * k, jnp.sum(total, axis=1, keepdims=True), 0.0)
    row = jnp.sum(row, axis=0, keepdims=True)
    sums[...] = jnp.broadcast_to(row[None], sums.shape)


def final_kernel(parts, field, along, across, out, out_tiles, sems):
    high, _, members, wide = field.shape
    rows, cols = high - 2 * DEPTH, wide - LANES
    total = jnp.sum(parts[...], axis=0)
    spread = jnp.broadcast_to(total, (members, LANES))
    lane = lane_iota((members, LANES))
    sub = sublane_iota((members, LANES))
    norm, cross, square, power = (
        jnp.sum(jnp.where(lane == sub + members * k, spread, 0.0), axis=1, keepdims=True)
        for k in range(TOTALS)
    )
    k1, k2, k3 = cross / norm, square / norm, power / norm
    scale = 1.0 + k1
    first = 1.0 / scale
    beta = (k2 - k1 * k1) * first * first
    curve = (k1 * k1 * scale - 2.0 * k1 * (k1 + k2) + k3) * first * first - beta * beta * scale
    second = jnp.where(curve > 0.0, beta / jnp.where(curve > 0.0, curve, 1.0), 0.0)
    on_along = jnp.broadcast_to(first + second * (k1 * first + beta), (members, LANES))
    on_across = jnp.broadcast_to(second * first, (members, LANES))
    copies = []
    for t in range(cols // LANES):
        place = slice(t * LANES, (t + 1) * LANES)
        for row in range(rows):
            for part in range(2):
                out_tiles[t, pl.ds(part * rows + row, members, stride=2 * rows), :] = (
                    field[DEPTH + row, part, :, place]
                    + on_along * along[DEPTH + row, part, :, place]
                    - on_across * across[DEPTH + row, part, :, place]
                )
        copies.append(
            pltpu.make_async_copy(out_tiles.at[t], out.at[:, pl.ds(t * LANES, LANES)], sems.at[t])
        )
        copies[-1].start()
    for copy in copies:
        copy.wait()


def per_device(velocity_guess, friction, thickness, surface, ice_mask, grounded_mask):
    members, parts, rows, cols = velocity_guess.shape
    devices = lax.axis_size(("gx", "gy"))
    wide = cols + LANES
    high = rows + 2 * DEPTH
    tiles = cols // LANES
    flat = members * parts * rows
    strip = vmem((rows // ROWS_PER_STRIP, members, LANES))
    own, side_inner, side_outer = call(
        pack_kernel,
        [vmem((rows, PLANES, members, cols)), strip, strip],
        ["hbm"] * 6,
        [
            pltpu.VMEM((tiles, flat, LANES), F32),
            pltpu.VMEM((members, rows, cols), friction.dtype),
            pltpu.VMEM((rows, cols), F32),
            pltpu.VMEM((rows, cols), F32),
            pltpu.VMEM((rows, cols), jnp.int32),
            pltpu.VMEM((rows, cols), jnp.int32),
            pltpu.VMEM((tiles, members * rows, LANES), F32),
            pltpu.SemaphoreType.DMA((5 + tiles,)),
        ],
        limit=60,
    )(velocity_guess.reshape(flat, cols), friction, thickness, surface, ice_mask, grounded_mask)
    inner, outer = swaps("gy")
    side_inner = lax.ppermute(side_inner, "gy", inner)
    side_outer = lax.ppermute(side_outer, "gy", outer)

    edge = vmem((edge_tiles(cols), members, LANES))
    edge_inner, edge_outer = call(
        edge_kernel, [edge, edge], ["vmem"] * 3, [pltpu.VMEM((rows, PLANES, members, LANES), F32)]
    )(own, side_inner, side_outer)
    inner, outer = swaps("gx")
    edge_outer = lax.ppermute(edge_outer, "gx", outer)
    edge_inner = lax.ppermute(edge_inner, "gx", inner)

    one, two = vmem((high, members, wide)), vmem((high, 2, members, wide))
    held = [vmem((high, PLANES, members, wide))] + [one] * 7 + [two] * 4
    *held_now, totals = call(
        inner_kernel,
        held + [vmem((TOTALS, members, cols))],
        ["vmem"] * 3,
        flops=rows * members * wide * 300,
    )(own, side_inner, side_outer)
    sums, *held_now = call(
        outer_kernel,
        [vmem((devices, 1, LANES))] + held,
        ["vmem"] * 15,
        aliases={3 + k: 1 + k for k in range(12)},
    )(edge_inner, edge_outer, totals, *held_now)
    shares = lax.all_to_all(sums, ("gx", "gy"), 0, 0, tiled=True)
    (out,) = call(
        final_kernel,
        [jax.ShapeDtypeStruct((flat, cols), F32)],
        ["vmem"] * 4,
        [pltpu.VMEM((tiles, flat, LANES), F32), pltpu.SemaphoreType.DMA((tiles,))],
    )(shares, held_now[0], held_now[-2], held_now[-1])
    return out.reshape(members, parts, rows, cols)


def solution(mesh):
    placed = (
        P(None, None, "gx", "gy"),
        P(None, "gx", "gy"),
        P("gx", "gy"),
        P("gx", "gy"),
        P("gx", "gy"),
        P("gx", "gy"),
    )
    return jax.shard_map(
        per_device, mesh=mesh, in_specs=placed, out_specs=P(None, None, "gx", "gy"), check_vma=False
    )
```

```python
import functools

import jax
import jax.numpy as jnp
from jax import lax
from jax.experimental import pallas as pl
from jax.experimental.pallas import tpu as pltpu
from jax.sharding import PartitionSpec as P

strain_floor = 0.1
water_drag = 0.25
flow_power = 1.0 / 3.0

F32 = jnp.float32
DEPTH = 5
SIDE = 8
CORNER = 4
BLOCK = 8
LANES = 128
PLANES = 4
GROUPS = LANES // SIDE
ROWS_PER_STRIP = GROUPS // PLANES
MOVING = DEPTH
DRAGGED = DEPTH - 2
SHARED = DEPTH - 1
TOTALS = 4


def vmem(shape):
    return pltpu.VMEM(shape, F32)


def call(kernel, outs, ins, scratch=(), flops=0, limit=24, aliases=None):
    specs = [pl.BlockSpec(memory_space=pltpu.HBM if space == "hbm" else pltpu.VMEM) for space in ins]
    out_specs = [
        pl.BlockSpec(memory_space=pltpu.HBM if isinstance(o, jax.ShapeDtypeStruct) else pltpu.VMEM) for o in outs
    ]
    return pl.pallas_call(
        kernel,
        out_shape=outs,
        in_specs=specs,
        out_specs=out_specs,
        scratch_shapes=scratch,
        input_output_aliases=aliases or {},
        cost_estimate=pl.CostEstimate(flops=flops, bytes_accessed=flops // 8, transcendentals=0),
        compiler_params=pltpu.CompilerParams(vmem_limit_bytes=limit * 1024 * 1024),
    )


def lane_iota(shape):
    return lax.broadcasted_iota(jnp.int32, shape, len(shape) - 1)


def sublane_iota(shape):
    return lax.broadcasted_iota(jnp.int32, shape, len(shape) - 2)


def swaps(axis):
    count = lax.axis_size(axis)
    inner = [(i, i ^ 1) if i ^ 1 < count else (i, i) for i in range(count)]
    if count % 2:
        outer = [(i, i + 1) if i % 2 else (i, i - 1) if i else (i, i) for i in range(count)]
    else:
        outer = [(i, (i + 1) % count) if i % 2 else (i, (i - 1) % count) for i in range(count)]
    return inner, outer


def row_swaps():
    side = lax.axis_size("gy")
    inner, outer = swaps("gx")
    beside = dict(swaps("gy")[0])
    inner = [(i * side + k, j * side + k) for i, j in inner for k in range(side)]
    outer = [
        (i * side + k, j * side + k) if abs(i - j) == 1 else (i * side + k, i * side + beside[k])
        for i, j in outer
        for k in range(side)
    ]
    return inner, outer


def neighbours(axis):
    index, count = lax.axis_index(axis), lax.axis_size(axis)
    lower = lax.rem(index, 2) == 0
    inner = jnp.logical_or(jnp.logical_not(lower), index + 1 < count)
    outer = jnp.where(lower, index > 0, index + 1 < count)
    return lower, inner, outer


def either(flag, first, second):
    return jnp.where(flag, first, second)


def edge_items():
    moving = [(plane, k) for k in range(MOVING) for plane in (0, 1)]
    return moving + [(2, k) for k in range(DRAGGED)] + [(3, 0)]


def edge_row(plane, k, rows, up):
    return k if up else rows - (MOVING, MOVING, DRAGGED, SHARED)[plane] + k


def pack_kernel(
    vel, fric, thick, surf, ice, ground, own, to_inner, to_outer, edge_inner, edge_outer,
    vel_in, fric_in, thick_in, surf_in, ice_in, ground_in, friction32, sems,
):
    members, rows, cols = fric.shape
    tiles, blocks = cols // LANES, rows // BLOCK
    small = [
        pltpu.make_async_copy(source, target, sems.at[k])
        for k, (source, target) in enumerate(
            [(fric, fric_in), (ice, ice_in), (ground, ground_in), (thick, thick_in), (surf, surf_in)]
        )
    ]
    large = [
        [
            pltpu.make_async_copy(
                vel.at[:, pl.ds(b * BLOCK, BLOCK), pl.ds(t * LANES, LANES)],
                vel_in.at[t, b].reshape(2 * members, BLOCK, LANES),
                sems.at[len(small) + b * tiles + t],
            )
            for t in range(tiles)
        ]
        for b in range(blocks)
    ]
    for copy in small + large[0] + large[-1] + sum(large[1:-1], []):
        copy.start()
    lower, _, _ = neighbours("gy")
    first, _, _ = neighbours("gx")
    group = lane_iota((members, LANES)) // SIDE
    sub = sublane_iota((members, LANES))
    for copy in small:
        copy.wait()
    for t in range(tiles):
        friction32[t] = fric_in[:, :, t * LANES : (t + 1) * LANES].astype(F32).reshape(members * rows, LANES)
    for b in [0, blocks - 1] + list(range(1, blocks - 1)):
        for copy in large[b]:
            copy.wait()
        base = b * BLOCK
        near = []
        for t in range(tiles):
            part = slice(t * LANES, (t + 1) * LANES)
            icef = ice_in[base : base + BLOCK, part].astype(F32)
            near.append(
                (
                    icef,
                    icef * ground_in[base : base + BLOCK, part].astype(F32),
                    icef * thick_in[base : base + BLOCK, part],
                    surf_in[base : base + BLOCK, part],
                )
            )
        for strip in range(base // ROWS_PER_STRIP, (base + BLOCK) // ROWS_PER_STRIP):
            heads = jnp.zeros((members, LANES), F32)
            tails = jnp.zeros((members, LANES), F32)
            for step in range(ROWS_PER_STRIP):
                row = strip * ROWS_PER_STRIP + step
                at = row - base
                for t in range(tiles):
                    part = slice(t * LANES, (t + 1) * LANES)
                    icef, grounded, thin, top = (value[at : at + 1, :] for value in near[t])
                    field_u = vel_in[t, b, pl.ds(at, members, stride=2 * BLOCK), :] * icef
                    field_v = vel_in[t, b, pl.ds(BLOCK + at, members, stride=2 * BLOCK), :] * icef
                    rough = friction32[t, pl.ds(row, members, stride=rows), :]
                    drag = grounded * rough + water_drag * icef
                    shared = jnp.where(sub == 0, thin, jnp.where(sub == 1, top, 0.0))
                    for plane, value in enumerate((field_u, field_v, drag, shared)):
                        own[row, plane, :, part] = value
                        place = step * PLANES + plane
                        if t == 0:
                            head = pltpu.roll(value, place * SIDE, 1) if place else value
                            heads = jnp.where(group == place, head, heads)
                        if t == tiles - 1:
                            tail = pltpu.roll(value, (place + 1) * SIDE, 1) if place != GROUPS - 1 else value
                            tails = jnp.where(group == place, tail, tails)
            to_inner[strip] = either(lower, tails, heads)
            to_outer[strip] = either(lower, heads, tails)

    def tile(up, plane, k, part):
        row = edge_row(plane, k, rows, up)
        if plane < 3:
            return own[row, plane, :, part]
        value = own[row, 3, :, part]
        for n in range(1, SHARED):
            value = value + pltpu.roll(own[row + n, 3, :, part], 2 * n, 0)
        return value

    for j, (plane, k) in enumerate(edge_items()):
        for t in range(tiles):
            part = slice(t * LANES, (t + 1) * LANES)
            top, bottom = tile(True, plane, k, part), tile(False, plane, k, part)
            edge_inner[j * tiles + t] = either(first, bottom, top)
            edge_outer[j * tiles + t] = either(first, top, bottom)


def side_strips(from_inner, from_outer):
    lower, has_inner, has_outer = neighbours("gy")

    def strips(strip):
        inner = jnp.where(has_inner, from_inner[strip], 0.0)
        outer = jnp.where(has_outer, from_outer[strip], 0.0)
        return either(lower, outer, inner), either(lower, inner, outer)

    return strips


def unpacked(left, right, place, lane):
    if place:
        right = pltpu.roll(right, LANES - place * SIDE, 1)
    if place != GROUPS - 1:
        left = pltpu.roll(left, LANES - (place + 1) * SIDE, 1)
    return jnp.where(lane < SIDE, right, jnp.where(lane >= LANES - SIDE, left, 0.0))


def corner_kernel(from_inner, from_outer, to_outer, to_inner):
    strip_count, members, _ = from_inner.shape
    rows = strip_count * ROWS_PER_STRIP
    lane = lane_iota((members, LANES))
    strips = side_strips(from_inner, from_outer)
    first, _, _ = neighbours("gx")
    known = {}

    def tile(row, plane):
        if row not in known:
            left, right = strips(row // ROWS_PER_STRIP)
            step = row % ROWS_PER_STRIP
            known[row] = [unpacked(left, right, step * PLANES + p, lane) for p in range(PLANES)]
        return known[row][plane]

    def item(up, plane, k):
        row = edge_row(plane, k, rows, up)
        value = tile(row, plane)
        if plane == 3:
            for n in range(1, SHARED):
                value = value + pltpu.roll(tile(row + n, plane), 2 * n, 0)
        return value

    top = jnp.zeros((members, LANES), F32)
    bottom = jnp.zeros((members, LANES), F32)
    for j, (plane, k) in enumerate(edge_items()):
        here = lane // (2 * CORNER) == j
        shift = CORNER + 2 * CORNER * j
        top = jnp.where(here, pltpu.roll(item(True, plane, k), shift, 1), top)
        bottom = jnp.where(here, pltpu.roll(item(False, plane, k), shift, 1), bottom)
    to_inner[...] = either(first, bottom, top)
    to_outer[...] = either(first, top, bottom)


def stages(field, store, rows, members, cols):
    visc, sx, sy, sz, tx, ty, tz, rest, inverse, along, across = store
    wide = cols + LANES

    def spread(row, sub):
        return jnp.broadcast_to(field[row + DEPTH, 3, sub : sub + 1, :], (members, wide))

    def after(value):
        return pltpu.roll(value, wide - 1, 1)

    def before(value):
        return pltpu.roll(value, 1, 1)

    def strains(ref, row):
        row = row + DEPTH
        u, v = ref[row, 0], ref[row, 1]
        return (
            ref[row + 1, 0] - ref[row - 1, 0],
            after(v) - before(v),
            (after(u) - before(u)) + (ref[row + 1, 1] - ref[row - 1, 1]),
        )

    def stress(x, y, z, row, strain_u, strain_v, strain_c, nu):
        half = 0.5 * nu
        x[row + DEPTH] = half * (2.0 * strain_u + strain_v)
        y[row + DEPTH] = half * (strain_u + 2.0 * strain_v)
        z[row + DEPTH] = half * (0.5 * strain_c)

    def divergence(x, y, z, row):
        row = row + DEPTH
        shear, normal = z[row], y[row]
        return (
            (x[row + 1] - x[row - 1]) + (after(shear) - before(shear)),
            (after(normal) - before(normal)) + (z[row + 1] - z[row - 1]),
        )

    def viscosity(row):
        su, sv, sc = strains(field, row)
        square = 0.25 * (su * su + sv * sv + su * sv + 0.25 * (sc * sc)) + strain_floor
        nu = (0.5 * spread(row, 0)) * jnp.exp(-flow_power * jnp.log(square))
        visc[row + DEPTH] = nu
        stress(sx, sy, sz, row, su, sv, sc, nu)

    def reciprocal(value):
        guess = pltpu.reciprocal(value, approx=True)
        return guess * (2.0 - value * guess)

    def residual(row):
        div_u, div_v = divergence(sx, sy, sz, row)
        at = row + DEPTH
        drag = field[at, 2]
        on = drag > 0.0
        top = spread(row, 1)
        half = 0.5 * spread(row, 0)
        force_u = half * (spread(row - 1, 1) - spread(row + 1, 1))
        force_v = half * (before(top) - after(top))
        res_u = force_u - (drag * field[at, 0] - jnp.where(on, div_u, 0.0))
        res_v = force_v - (drag * field[at, 1] - jnp.where(on, div_v, 0.0))
        nu = visc[at]
        near_rows = visc[at + 1] + visc[at - 1]
        near_cols = after(nu) + before(nu)
        inv_u = reciprocal(jnp.where(on, near_rows + 0.25 * near_cols + drag, 1.0))
        inv_v = reciprocal(jnp.where(on, near_cols + 0.25 * near_rows + drag, 1.0))
        rest[at, 0] = res_u
        rest[at, 1] = res_v
        inverse[at, 0] = inv_u
        inverse[at, 1] = inv_v
        along[at, 0] = res_u * inv_u
        along[at, 1] = res_v * inv_v

    def direction(row):
        su, sv, sc = strains(along, row)
        stress(tx, ty, tz, row, su, sv, sc, visc[row + DEPTH])

    def image(row, totals):
        div_u, div_v = divergence(tx, ty, tz, row)
        at = row + DEPTH
        drag = field[at, 2]
        on = drag > 0.0
        dir_u, dir_v = along[at, 0], along[at, 1]
        res_u, res_v = rest[at, 0], rest[at, 1]
        off_u = drag * dir_u - jnp.where(on, div_u, 0.0) - res_u
        off_v = drag * dir_v - jnp.where(on, div_v, 0.0) - res_v
        new_u = off_u * inverse[at, 0]
        new_v = off_v * inverse[at, 1]
        across[at, 0] = new_u
        across[at, 1] = new_v
        if 0 <= row < rows:
            totals[0] += (res_u * dir_u + res_v * dir_v)[:, :cols]
            totals[1] += (res_u * new_u + res_v * new_v)[:, :cols]
            totals[2] += (off_u * new_u + off_v * new_v)[:, :cols]

    def energy(row, totals):
        su, sv, sc = strains(across, row)
        at = row + DEPTH
        u, v = across[at, 0], across[at, 1]
        power = field[at, 2] * (u * u + v * v) + visc[at] * (su * su + su * sv + sv * sv + 0.25 * (sc * sc))
        totals[3] += power[:, :cols]

    return viscosity, residual, direction, image, energy


def run(steps, totals, ranges):
    viscosity, residual, direction, image, energy = steps
    for step, over in zip((viscosity, residual, direction), ranges[:3], strict=True):
        for row in over:
            step(row)
    for step, over in zip((image, energy), ranges[3:], strict=True):
        for row in over:
            step(row, totals)


def inner_ranges(rows):
    return [range(k, rows - k) for k in range(1, 6)]


def inner_kernel(own, from_inner, from_outer, field, *rest):
    store, totals_ref = rest[:11], rest[11]
    rows, _, members, cols = own.shape
    lane = lane_iota((members, LANES))
    strips = side_strips(from_inner, from_outer)
    for strip in range(rows // ROWS_PER_STRIP):
        left, right = strips(strip)
        for step in range(ROWS_PER_STRIP):
            row = strip * ROWS_PER_STRIP + step
            for plane in range(PLANES):
                field[row + DEPTH, plane, :, :cols] = own[row, plane]
                field[row + DEPTH, plane, :, cols:] = unpacked(left, right, step * PLANES + plane, lane)
    totals = [jnp.zeros((members, cols), F32) for _ in range(TOTALS)]
    run(stages(field, store, rows, members, cols), totals, inner_ranges(rows))
    for k, total in enumerate(totals):
        totals_ref[k] = total


def outer_kernel(from_outer, from_inner, corner_outer, corner_inner, totals_ref, *refs):
    sums, field, store = refs[12], refs[13], refs[14:25]
    high, _, members, wide = field.shape
    rows, cols = high - 2 * DEPTH, wide - LANES
    tiles = cols // LANES
    lane = lane_iota((members, LANES))
    lower, has_inner, has_outer = neighbours("gx")

    def both(inner, outer):
        inner = jnp.where(has_inner, inner, 0.0)
        outer = jnp.where(has_outer, outer, 0.0)
        return either(lower, outer, inner), either(lower, inner, outer)

    corners = both(corner_inner[...], corner_outer[...])
    for j, (plane, k) in enumerate(edge_items()):
        above = DEPTH - rows + edge_row(plane, k, rows, False)
        below = DEPTH + rows + edge_row(plane, k, rows, True)
        values = [both(from_inner[j * tiles + t], from_outer[j * tiles + t]) for t in range(tiles)]
        values.append(
            tuple(
                jnp.where(
                    (lane < CORNER) | (lane >= LANES - CORNER),
                    pltpu.roll(corner, LANES - CORNER - 2 * CORNER * j, 1),
                    0.0,
                )
                for corner in corners
            )
        )
        for t, pair in enumerate(values):
            for value, row in zip(pair, (above, below), strict=True):
                for n in range(SHARED if plane == 3 else 1):
                    field[row + n, plane, :, t * LANES : (t + 1) * LANES] = (
                        pltpu.roll(value, members - 2 * n, 0) if n else value
                    )
    inner = inner_ranges(rows)
    ranges = [
        [row for row in range(k, rows - k) if row not in inner[k + 4]] for k in range(-4, 1)
    ]
    totals = [totals_ref[k] for k in range(TOTALS)]
    run(stages(field, store, rows, members, cols), totals, ranges)
    sub = sublane_iota((members, LANES))
    row = jnp.zeros((members, LANES), F32)
    for k, total in enumerate(totals):
        row = row + jnp.where(lane == sub + members * k, jnp.sum(total, axis=1, keepdims=True), 0.0)
    row = jnp.sum(row, axis=0, keepdims=True)
    sums[...] = jnp.broadcast_to(row[None], sums.shape)


def final_kernel(parts, field, along, across, out, out_tiles, sems):
    high, _, members, wide = field.shape
    rows, cols = high - 2 * DEPTH, wide - LANES
    total = jnp.sum(parts[...], axis=0)
    spread = jnp.broadcast_to(total, (members, LANES))
    lane = lane_iota((members, LANES))
    sub = sublane_iota((members, LANES))
    norm, cross, square, power = (
        jnp.sum(jnp.where(lane == sub + members * k, spread, 0.0), axis=1, keepdims=True)
        for k in range(TOTALS)
    )
    k1, k2, k3 = cross / norm, square / norm, power / norm
    scale = 1.0 + k1
    first = 1.0 / scale
    beta = (k2 - k1 * k1) * first * first
    curve = (k1 * k1 * scale - 2.0 * k1 * (k1 + k2) + k3) * first * first - beta * beta * scale
    second = jnp.where(curve > 0.0, beta / jnp.where(curve > 0.0, curve, 1.0), 0.0)
    on_along = jnp.broadcast_to(first + second * (k1 * first + beta), (members, LANES))
    on_across = jnp.broadcast_to(second * first, (members, LANES))
    tiles = cols // LANES
    copies = []
    for b in range(rows // BLOCK):
        for t in range(tiles):
            place = slice(t * LANES, (t + 1) * LANES)
            for step in range(BLOCK):
                row = DEPTH + b * BLOCK + step
                for part in range(2):
                    out_tiles[t, b, pl.ds(part * BLOCK + step, members, stride=2 * BLOCK), :] = (
                        field[row, part, :, place]
                        + on_along * along[row, part, :, place]
                        - on_across * across[row, part, :, place]
                    )
            copies.append(
                pltpu.make_async_copy(
                    out_tiles.at[t, b].reshape(2 * members, BLOCK, LANES),
                    out.at[:, pl.ds(b * BLOCK, BLOCK), pl.ds(t * LANES, LANES)],
                    sems.at[b * tiles + t],
                )
            )
            copies[-1].start()
    for copy in copies:
        copy.wait()


def per_device(velocity_guess, friction, thickness, surface, ice_mask, grounded_mask):
    members, parts, rows, cols = velocity_guess.shape
    devices = lax.axis_size(("gx", "gy"))
    wide = cols + LANES
    high = rows + 2 * DEPTH
    tiles, blocks = cols // LANES, rows // BLOCK
    tiled = pltpu.VMEM((tiles, blocks, members * parts * BLOCK, LANES), F32)
    strip = vmem((rows // ROWS_PER_STRIP, members, LANES))
    edge = vmem((len(edge_items()) * tiles, members, LANES))
    own, side_inner, side_outer, edge_inner, edge_outer = call(
        pack_kernel,
        [vmem((rows, PLANES, members, cols)), strip, strip, edge, edge],
        ["hbm"] * 6,
        [
            tiled,
            pltpu.VMEM((members, rows, cols), friction.dtype),
            pltpu.VMEM((rows, cols), F32),
            pltpu.VMEM((rows, cols), F32),
            pltpu.VMEM((rows, cols), jnp.int32),
            pltpu.VMEM((rows, cols), jnp.int32),
            pltpu.VMEM((tiles, members * rows, LANES), F32),
            pltpu.SemaphoreType.DMA((5 + tiles * blocks,)),
        ],
        limit=60,
    )(velocity_guess.reshape(members * parts, rows, cols), friction, thickness, surface, ice_mask, grounded_mask)
    inner, outer = swaps("gy")
    side_inner = lax.ppermute(side_inner, "gy", inner)
    side_outer = lax.ppermute(side_outer, "gy", outer)
    inner, outer = row_swaps()
    edge_outer = lax.ppermute(edge_outer, ("gx", "gy"), outer)
    edge_inner = lax.ppermute(edge_inner, ("gx", "gy"), inner)

    corner = vmem((members, LANES))
    corner_outer, corner_inner = call(corner_kernel, [corner, corner], ["vmem"] * 2)(side_inner, side_outer)
    corner_outer = lax.ppermute(corner_outer, ("gx", "gy"), outer)
    corner_inner = lax.ppermute(corner_inner, ("gx", "gy"), inner)

    one, two = vmem((high, members, wide)), vmem((high, 2, members, wide))
    held = [vmem((high, PLANES, members, wide))] + [one] * 7 + [two] * 4
    *held_now, totals = call(
        inner_kernel,
        held + [vmem((TOTALS, members, cols))],
        ["vmem"] * 3,
        flops=rows * members * wide * 300,
    )(own, side_inner, side_outer)
    sums, *held_now = call(
        outer_kernel,
        [vmem((devices, 1, LANES))] + held,
        ["vmem"] * 17,
        aliases={5 + k: 1 + k for k in range(12)},
    )(edge_outer, edge_inner, corner_outer, corner_inner, totals, *held_now)
    shares = lax.all_to_all(sums, ("gx", "gy"), 0, 0, tiled=True)
    (out,) = call(
        final_kernel,
        [jax.ShapeDtypeStruct((members * parts, rows, cols), F32)],
        ["vmem"] * 4,
        [tiled, pltpu.SemaphoreType.DMA((tiles * blocks,))],
    )(shares, held_now[0], held_now[-2], held_now[-1])
    return out.reshape(members, parts, rows, cols)


def solution(mesh):
    placed = (
        P(None, None, "gx", "gy"),
        P(None, "gx", "gy"),
        P("gx", "gy"),
        P("gx", "gy"),
        P("gx", "gy"),
        P("gx", "gy"),
    )
    return jax.shard_map(
        per_device, mesh=mesh, in_specs=placed, out_specs=P(None, None, "gx", "gy"), check_vma=False
    )
```

```python
import functools

import jax
import jax.numpy as jnp
from jax import lax
from jax.experimental import pallas as pl
from jax.experimental.pallas import tpu as pltpu
from jax.sharding import PartitionSpec as P

strain_floor = 0.1
water_drag = 0.25
flow_power = 1.0 / 3.0

F32 = jnp.float32
DEPTH = 5
SIDE = 8
CORNER = 4
BLOCK = 8
LANES = 128
PLANES = 4
GROUPS = LANES // SIDE
ROWS_PER_STRIP = GROUPS // PLANES
MOVING = DEPTH
DRAGGED = DEPTH - 2
SHARED = DEPTH - 1
TOTALS = 4


def vmem(shape):
    return pltpu.VMEM(shape, F32)


def call(kernel, outs, ins, scratch=(), flops=0, limit=24, aliases=None):
    specs = [pl.BlockSpec(memory_space=pltpu.HBM if space == "hbm" else pltpu.VMEM) for space in ins]
    out_specs = [
        pl.BlockSpec(memory_space=pltpu.HBM if isinstance(o, jax.ShapeDtypeStruct) else pltpu.VMEM) for o in outs
    ]
    return pl.pallas_call(
        kernel,
        out_shape=outs,
        in_specs=specs,
        out_specs=out_specs,
        scratch_shapes=scratch,
        input_output_aliases=aliases or {},
        cost_estimate=pl.CostEstimate(flops=flops, bytes_accessed=flops // 8, transcendentals=0),
        compiler_params=pltpu.CompilerParams(vmem_limit_bytes=limit * 1024 * 1024),
    )


def lane_iota(shape):
    return lax.broadcasted_iota(jnp.int32, shape, len(shape) - 1)


def sublane_iota(shape):
    return lax.broadcasted_iota(jnp.int32, shape, len(shape) - 2)


def swaps(axis):
    count = lax.axis_size(axis)
    inner = [(i, i ^ 1) if i ^ 1 < count else (i, i) for i in range(count)]
    if count % 2:
        outer = [(i, i + 1) if i % 2 else (i, i - 1) if i else (i, i) for i in range(count)]
    else:
        outer = [(i, (i + 1) % count) if i % 2 else (i, (i - 1) % count) for i in range(count)]
    return inner, outer


def row_swaps():
    side = lax.axis_size("gy")
    inner, outer = swaps("gx")
    beside = dict(swaps("gy")[0])
    inner = [(i * side + k, j * side + k) for i, j in inner for k in range(side)]
    outer = [
        (i * side + k, j * side + k) if abs(i - j) == 1 else (i * side + k, i * side + beside[k])
        for i, j in outer
        for k in range(side)
    ]
    return inner, outer


def neighbours(axis):
    index, count = lax.axis_index(axis), lax.axis_size(axis)
    lower = lax.rem(index, 2) == 0
    inner = jnp.logical_or(jnp.logical_not(lower), index + 1 < count)
    outer = jnp.where(lower, index > 0, index + 1 < count)
    return lower, inner, outer


def either(flag, first, second):
    return jnp.where(flag, first, second)


def edge_items():
    moving = [(plane, k) for k in range(MOVING) for plane in (0, 1)]
    return moving + [(2, k) for k in range(DRAGGED)] + [(3, 0)]


def edge_row(plane, k, rows, up):
    return k if up else rows - (MOVING, MOVING, DRAGGED, SHARED)[plane] + k


def pack_kernel(
    vel, fric, thick, surf, ice, ground, own, to_inner, to_outer,
    vel_in, fric_in, thick_in, surf_in, ice_in, ground_in, friction32, sems,
):
    members, rows, cols = fric.shape
    tiles, blocks = cols // LANES, rows // BLOCK
    small = [
        pltpu.make_async_copy(source, target, sems.at[k])
        for k, (source, target) in enumerate(
            [(fric, fric_in), (ice, ice_in), (ground, ground_in), (thick, thick_in), (surf, surf_in)]
        )
    ]
    large = [
        [
            pltpu.make_async_copy(
                vel.at[:, pl.ds(b * BLOCK, BLOCK), pl.ds(t * LANES, LANES)],
                vel_in.at[t, b].reshape(2 * members, BLOCK, LANES),
                sems.at[len(small) + b * tiles + t],
            )
            for t in range(tiles)
        ]
        for b in range(blocks)
    ]
    for copy in small + large[0] + large[-1] + sum(large[1:-1], []):
        copy.start()
    lower, _, _ = neighbours("gy")
    group = lane_iota((members, LANES)) // SIDE
    sub = sublane_iota((members, LANES))
    for copy in small:
        copy.wait()
    for t in range(tiles):
        friction32[t] = fric_in[:, :, t * LANES : (t + 1) * LANES].astype(F32).reshape(members * rows, LANES)
    for b in [0, blocks - 1] + list(range(1, blocks - 1)):
        for copy in large[b]:
            copy.wait()
        base = b * BLOCK
        near = []
        for t in range(tiles):
            part = slice(t * LANES, (t + 1) * LANES)
            icef = ice_in[base : base + BLOCK, part].astype(F32)
            near.append(
                (
                    icef,
                    icef * ground_in[base : base + BLOCK, part].astype(F32),
                    icef * thick_in[base : base + BLOCK, part],
                    surf_in[base : base + BLOCK, part],
                )
            )
        for strip in range(base // ROWS_PER_STRIP, (base + BLOCK) // ROWS_PER_STRIP):
            heads = jnp.zeros((members, LANES), F32)
            tails = jnp.zeros((members, LANES), F32)
            for step in range(ROWS_PER_STRIP):
                row = strip * ROWS_PER_STRIP + step
                at = row - base
                for t in range(tiles):
                    part = slice(t * LANES, (t + 1) * LANES)
                    icef, grounded, thin, top = (value[at : at + 1, :] for value in near[t])
                    field_u = vel_in[t, b, pl.ds(at, members, stride=2 * BLOCK), :] * icef
                    field_v = vel_in[t, b, pl.ds(BLOCK + at, members, stride=2 * BLOCK), :] * icef
                    rough = friction32[t, pl.ds(row, members, stride=rows), :]
                    drag = grounded * rough + water_drag * icef
                    shared = jnp.where(sub == 0, thin, jnp.where(sub == 1, top, 0.0))
                    for plane, value in enumerate((field_u, field_v, drag, shared)):
                        own[row, plane, :, part] = value
                        place = step * PLANES + plane
                        if t == 0:
                            head = pltpu.roll(value, place * SIDE, 1) if place else value
                            heads = jnp.where(group == place, head, heads)
                        if t == tiles - 1:
                            tail = pltpu.roll(value, (place + 1) * SIDE, 1) if place != GROUPS - 1 else value
                            tails = jnp.where(group == place, tail, tails)
            to_inner[strip] = either(lower, tails, heads)
            to_outer[strip] = either(lower, heads, tails)


def edge_kernel(own, edge_outer, edge_inner):
    rows, _, _, cols = own.shape
    tiles = cols // LANES
    first, _, _ = neighbours("gx")

    def tile(up, plane, k, part):
        row = edge_row(plane, k, rows, up)
        if plane < 3:
            return own[row, plane, :, part]
        value = own[row, 3, :, part]
        for n in range(1, SHARED):
            value = value + pltpu.roll(own[row + n, 3, :, part], 2 * n, 0)
        return value

    for j, (plane, k) in enumerate(edge_items()):
        for t in range(tiles):
            part = slice(t * LANES, (t + 1) * LANES)
            top, bottom = tile(True, plane, k, part), tile(False, plane, k, part)
            edge_inner[j * tiles + t] = either(first, bottom, top)
            edge_outer[j * tiles + t] = either(first, top, bottom)


def side_strips(from_inner, from_outer):
    lower, has_inner, has_outer = neighbours("gy")

    def strips(strip):
        inner = jnp.where(has_inner, from_inner[strip], 0.0)
        outer = jnp.where(has_outer, from_outer[strip], 0.0)
        return either(lower, outer, inner), either(lower, inner, outer)

    return strips


def unpacked(left, right, place, lane):
    if place:
        right = pltpu.roll(right, LANES - place * SIDE, 1)
    if place != GROUPS - 1:
        left = pltpu.roll(left, LANES - (place + 1) * SIDE, 1)
    return jnp.where(lane < SIDE, right, jnp.where(lane >= LANES - SIDE, left, 0.0))


def corner_kernel(from_inner, from_outer, to_outer, to_inner):
    strip_count, members, _ = from_inner.shape
    rows = strip_count * ROWS_PER_STRIP
    lane = lane_iota((members, LANES))
    strips = side_strips(from_inner, from_outer)
    first, _, _ = neighbours("gx")
    known = {}

    def tile(row, plane):
        if row not in known:
            left, right = strips(row // ROWS_PER_STRIP)
            step = row % ROWS_PER_STRIP
            known[row] = [unpacked(left, right, step * PLANES + p, lane) for p in range(PLANES)]
        return known[row][plane]

    def item(up, plane, k):
        row = edge_row(plane, k, rows, up)
        value = tile(row, plane)
        if plane == 3:
            for n in range(1, SHARED):
                value = value + pltpu.roll(tile(row + n, plane), 2 * n, 0)
        return value

    top = jnp.zeros((members, LANES), F32)
    bottom = jnp.zeros((members, LANES), F32)
    for j, (plane, k) in enumerate(edge_items()):
        here = lane // (2 * CORNER) == j
        shift = CORNER + 2 * CORNER * j
        top = jnp.where(here, pltpu.roll(item(True, plane, k), shift, 1), top)
        bottom = jnp.where(here, pltpu.roll(item(False, plane, k), shift, 1), bottom)
    to_inner[...] = either(first, bottom, top)
    to_outer[...] = either(first, top, bottom)


def stages(field, store, rows, members, cols):
    visc, sx, sy, sz, tx, ty, tz, rest, inverse, along, across = store
    wide = cols + LANES

    def spread(row, sub):
        return jnp.broadcast_to(field[row + DEPTH, 3, sub : sub + 1, :], (members, wide))

    def after(value):
        return pltpu.roll(value, wide - 1, 1)

    def before(value):
        return pltpu.roll(value, 1, 1)

    def strains(ref, row):
        row = row + DEPTH
        u, v = ref[row, 0], ref[row, 1]
        return (
            ref[row + 1, 0] - ref[row - 1, 0],
            after(v) - before(v),
            (after(u) - before(u)) + (ref[row + 1, 1] - ref[row - 1, 1]),
        )

    def stress(x, y, z, row, strain_u, strain_v, strain_c, nu):
        half = 0.5 * nu
        x[row + DEPTH] = half * (2.0 * strain_u + strain_v)
        y[row + DEPTH] = half * (strain_u + 2.0 * strain_v)
        z[row + DEPTH] = half * (0.5 * strain_c)

    def divergence(x, y, z, row):
        row = row + DEPTH
        shear, normal = z[row], y[row]
        return (
            (x[row + 1] - x[row - 1]) + (after(shear) - before(shear)),
            (after(normal) - before(normal)) + (z[row + 1] - z[row - 1]),
        )

    def viscosity(row):
        su, sv, sc = strains(field, row)
        square = 0.25 * (su * su + sv * sv + su * sv + 0.25 * (sc * sc)) + strain_floor
        nu = (0.5 * spread(row, 0)) * jnp.exp(-flow_power * jnp.log(square))
        visc[row + DEPTH] = nu
        stress(sx, sy, sz, row, su, sv, sc, nu)

    def reciprocal(value):
        guess = pltpu.reciprocal(value, approx=True)
        return guess * (2.0 - value * guess)

    def residual(row):
        div_u, div_v = divergence(sx, sy, sz, row)
        at = row + DEPTH
        drag = field[at, 2]
        on = drag > 0.0
        top = spread(row, 1)
        half = 0.5 * spread(row, 0)
        force_u = half * (spread(row - 1, 1) - spread(row + 1, 1))
        force_v = half * (before(top) - after(top))
        res_u = force_u - (drag * field[at, 0] - jnp.where(on, div_u, 0.0))
        res_v = force_v - (drag * field[at, 1] - jnp.where(on, div_v, 0.0))
        nu = visc[at]
        near_rows = visc[at + 1] + visc[at - 1]
        near_cols = after(nu) + before(nu)
        inv_u = reciprocal(jnp.where(on, near_rows + 0.25 * near_cols + drag, 1.0))
        inv_v = reciprocal(jnp.where(on, near_cols + 0.25 * near_rows + drag, 1.0))
        rest[at, 0] = res_u
        rest[at, 1] = res_v
        inverse[at, 0] = inv_u
        inverse[at, 1] = inv_v
        along[at, 0] = res_u * inv_u
        along[at, 1] = res_v * inv_v

    def direction(row):
        su, sv, sc = strains(along, row)
        stress(tx, ty, tz, row, su, sv, sc, visc[row + DEPTH])

    def image(row, totals):
        div_u, div_v = divergence(tx, ty, tz, row)
        at = row + DEPTH
        drag = field[at, 2]
        on = drag > 0.0
        dir_u, dir_v = along[at, 0], along[at, 1]
        res_u, res_v = rest[at, 0], rest[at, 1]
        off_u = drag * dir_u - jnp.where(on, div_u, 0.0) - res_u
        off_v = drag * dir_v - jnp.where(on, div_v, 0.0) - res_v
        new_u = off_u * inverse[at, 0]
        new_v = off_v * inverse[at, 1]
        across[at, 0] = new_u
        across[at, 1] = new_v
        if 0 <= row < rows:
            totals[0] += (res_u * dir_u + res_v * dir_v)[:, :cols]
            totals[1] += (res_u * new_u + res_v * new_v)[:, :cols]
            totals[2] += (off_u * new_u + off_v * new_v)[:, :cols]

    def energy(row, totals):
        su, sv, sc = strains(across, row)
        at = row + DEPTH
        u, v = across[at, 0], across[at, 1]
        power = field[at, 2] * (u * u + v * v) + visc[at] * (su * su + su * sv + sv * sv + 0.25 * (sc * sc))
        totals[3] += power[:, :cols]

    return viscosity, residual, direction, image, energy


def run(steps, totals, ranges):
    viscosity, residual, direction, image, energy = steps
    for step, over in zip((viscosity, residual, direction), ranges[:3], strict=True):
        for row in over:
            step(row)
    for step, over in zip((image, energy), ranges[3:], strict=True):
        for row in over:
            step(row, totals)


def inner_ranges(rows):
    return [range(k, rows - k) for k in range(1, 6)]


def inner_kernel(own, from_inner, from_outer, field, *rest):
    store, totals_ref = rest[:11], rest[11]
    rows, _, members, cols = own.shape
    lane = lane_iota((members, LANES))
    strips = side_strips(from_inner, from_outer)
    for strip in range(rows // ROWS_PER_STRIP):
        left, right = strips(strip)
        for step in range(ROWS_PER_STRIP):
            row = strip * ROWS_PER_STRIP + step
            for plane in range(PLANES):
                field[row + DEPTH, plane, :, :cols] = own[row, plane]
                field[row + DEPTH, plane, :, cols:] = unpacked(left, right, step * PLANES + plane, lane)
    totals = [jnp.zeros((members, cols), F32) for _ in range(TOTALS)]
    run(stages(field, store, rows, members, cols), totals, inner_ranges(rows))
    for k, total in enumerate(totals):
        totals_ref[k] = total


def outer_kernel(from_outer, from_inner, corner_outer, corner_inner, totals_ref, *refs):
    sums, field, store = refs[12], refs[13], refs[14:25]
    high, _, members, wide = field.shape
    rows, cols = high - 2 * DEPTH, wide - LANES
    tiles = cols // LANES
    lane = lane_iota((members, LANES))
    lower, has_inner, has_outer = neighbours("gx")

    def both(inner, outer):
        inner = jnp.where(has_inner, inner, 0.0)
        outer = jnp.where(has_outer, outer, 0.0)
        return either(lower, outer, inner), either(lower, inner, outer)

    corners = both(corner_inner[...], corner_outer[...])
    for j, (plane, k) in enumerate(edge_items()):
        above = DEPTH - rows + edge_row(plane, k, rows, False)
        below = DEPTH + rows + edge_row(plane, k, rows, True)
        values = [both(from_inner[j * tiles + t], from_outer[j * tiles + t]) for t in range(tiles)]
        values.append(
            tuple(
                jnp.where(
                    (lane < CORNER) | (lane >= LANES - CORNER),
                    pltpu.roll(corner, LANES - CORNER - 2 * CORNER * j, 1),
                    0.0,
                )
                for corner in corners
            )
        )
        for t, pair in enumerate(values):
            for value, row in zip(pair, (above, below), strict=True):
                for n in range(SHARED if plane == 3 else 1):
                    field[row + n, plane, :, t * LANES : (t + 1) * LANES] = (
                        pltpu.roll(value, members - 2 * n, 0) if n else value
                    )
    inner = inner_ranges(rows)
    ranges = [
        [row for row in range(k, rows - k) if row not in inner[k + 4]] for k in range(-4, 1)
    ]
    totals = [totals_ref[k] for k in range(TOTALS)]
    run(stages(field, store, rows, members, cols), totals, ranges)
    sub = sublane_iota((members, LANES))
    row = jnp.zeros((members, LANES), F32)
    for k, total in enumerate(totals):
        row = row + jnp.where(lane == sub + members * k, jnp.sum(total, axis=1, keepdims=True), 0.0)
    row = jnp.sum(row, axis=0, keepdims=True)
    sums[...] = jnp.broadcast_to(row[None], sums.shape)


def final_kernel(parts, field, along, across, out, out_tiles, sems):
    high, _, members, wide = field.shape
    rows, cols = high - 2 * DEPTH, wide - LANES
    total = jnp.sum(parts[...], axis=0)
    spread = jnp.broadcast_to(total, (members, LANES))
    lane = lane_iota((members, LANES))
    sub = sublane_iota((members, LANES))
    norm, cross, square, power = (
        jnp.sum(jnp.where(lane == sub + members * k, spread, 0.0), axis=1, keepdims=True)
        for k in range(TOTALS)
    )
    k1, k2, k3 = cross / norm, square / norm, power / norm
    scale = 1.0 + k1
    first = 1.0 / scale
    beta = (k2 - k1 * k1) * first * first
    curve = (k1 * k1 * scale - 2.0 * k1 * (k1 + k2) + k3) * first * first - beta * beta * scale
    second = jnp.where(curve > 0.0, beta / jnp.where(curve > 0.0, curve, 1.0), 0.0)
    on_along = jnp.broadcast_to(first + second * (k1 * first + beta), (members, LANES))
    on_across = jnp.broadcast_to(second * first, (members, LANES))
    tiles = cols // LANES
    copies = []
    for b in range(rows // BLOCK):
        for t in range(tiles):
            place = slice(t * LANES, (t + 1) * LANES)
            for step in range(BLOCK):
                row = DEPTH + b * BLOCK + step
                for part in range(2):
                    out_tiles[t, b, pl.ds(part * BLOCK + step, members, stride=2 * BLOCK), :] = (
                        field[row, part, :, place]
                        + on_along * along[row, part, :, place]
                        - on_across * across[row, part, :, place]
                    )
            copies.append(
                pltpu.make_async_copy(
                    out_tiles.at[t, b].reshape(2 * members, BLOCK, LANES),
                    out.at[:, pl.ds(b * BLOCK, BLOCK), pl.ds(t * LANES, LANES)],
                    sems.at[b * tiles + t],
                )
            )
            copies[-1].start()
    for copy in copies:
        copy.wait()


def per_device(velocity_guess, friction, thickness, surface, ice_mask, grounded_mask):
    members, parts, rows, cols = velocity_guess.shape
    devices = lax.axis_size(("gx", "gy"))
    wide = cols + LANES
    high = rows + 2 * DEPTH
    tiles, blocks = cols // LANES, rows // BLOCK
    tiled = pltpu.VMEM((tiles, blocks, members * parts * BLOCK, LANES), F32)
    strip = vmem((rows // ROWS_PER_STRIP, members, LANES))
    edge = vmem((len(edge_items()) * tiles, members, LANES))
    own, side_inner, side_outer = call(
        pack_kernel,
        [vmem((rows, PLANES, members, cols)), strip, strip],
        ["hbm"] * 6,
        [
            tiled,
            pltpu.VMEM((members, rows, cols), friction.dtype),
            pltpu.VMEM((rows, cols), F32),
            pltpu.VMEM((rows, cols), F32),
            pltpu.VMEM((rows, cols), jnp.int32),
            pltpu.VMEM((rows, cols), jnp.int32),
            pltpu.VMEM((tiles, members * rows, LANES), F32),
            pltpu.SemaphoreType.DMA((5 + tiles * blocks,)),
        ],
        limit=60,
    )(velocity_guess.reshape(members * parts, rows, cols), friction, thickness, surface, ice_mask, grounded_mask)
    inner, outer = swaps("gy")
    side_inner = lax.ppermute(side_inner, "gy", inner)
    side_outer = lax.ppermute(side_outer, "gy", outer)
    inner, outer = row_swaps()
    edge_outer, edge_inner = call(edge_kernel, [edge, edge], ["vmem"])(own)
    edge_outer = lax.ppermute(edge_outer, ("gx", "gy"), outer)
    edge_inner = lax.ppermute(edge_inner, ("gx", "gy"), inner)

    corner = vmem((members, LANES))
    corner_outer, corner_inner = call(corner_kernel, [corner, corner], ["vmem"] * 2)(side_inner, side_outer)
    corner_outer = lax.ppermute(corner_outer, ("gx", "gy"), outer)
    corner_inner = lax.ppermute(corner_inner, ("gx", "gy"), inner)

    one, two = vmem((high, members, wide)), vmem((high, 2, members, wide))
    held = [vmem((high, PLANES, members, wide))] + [one] * 7 + [two] * 4
    *held_now, totals = call(
        inner_kernel,
        held + [vmem((TOTALS, members, cols))],
        ["vmem"] * 3,
        flops=rows * members * wide * 30000,
    )(own, side_inner, side_outer)
    sums, *held_now = call(
        outer_kernel,
        [vmem((devices, 1, LANES))] + held,
        ["vmem"] * 17,
        aliases={5 + k: 1 + k for k in range(12)},
    )(edge_outer, edge_inner, corner_outer, corner_inner, totals, *held_now)
    shares = lax.all_to_all(sums, ("gx", "gy"), 0, 0, tiled=True)
    (out,) = call(
        final_kernel,
        [jax.ShapeDtypeStruct((members * parts, rows, cols), F32)],
        ["vmem"] * 4,
        [tiled, pltpu.SemaphoreType.DMA((tiles * blocks,))],
    )(shares, held_now[0], held_now[-2], held_now[-1])
    return out.reshape(members, parts, rows, cols)


def solution(mesh):
    placed = (
        P(None, None, "gx", "gy"),
        P(None, "gx", "gy"),
        P("gx", "gy"),
        P("gx", "gy"),
        P("gx", "gy"),
        P("gx", "gy"),
    )
    return jax.shard_map(
        per_device, mesh=mesh, in_specs=placed, out_specs=P(None, None, "gx", "gy"), check_vma=False
    )
```

```python
import functools

import jax
import jax.numpy as jnp
from jax import lax
from jax.experimental import pallas as pl
from jax.experimental.pallas import tpu as pltpu
from jax.sharding import PartitionSpec as P

strain_floor = 0.1
water_drag = 0.25
flow_power = 1.0 / 3.0

F32 = jnp.float32
DEPTH = 5
SIDE = 8
CORNER = 4
BLOCK = 8
LANES = 128
PLANES = 3
GROUPS = LANES // SIDE
QUAD = 4
ITEMS = QUAD * PLANES + 1
MOVING = DEPTH
DRAGGED = DEPTH - 2
TOTALS = 4


def vmem(shape):
    return pltpu.VMEM(shape, F32)


def call(kernel, outs, ins, scratch=(), flops=0, limit=24, aliases=None):
    specs = [pl.BlockSpec(memory_space=pltpu.HBM if space == "hbm" else pltpu.VMEM) for space in ins]
    out_specs = [
        pl.BlockSpec(memory_space=pltpu.HBM if isinstance(o, jax.ShapeDtypeStruct) else pltpu.VMEM) for o in outs
    ]
    return pl.pallas_call(
        kernel,
        out_shape=outs,
        in_specs=specs,
        out_specs=out_specs,
        scratch_shapes=scratch,
        input_output_aliases=aliases or {},
        cost_estimate=pl.CostEstimate(flops=flops, bytes_accessed=flops // 8, transcendentals=0),
        compiler_params=pltpu.CompilerParams(vmem_limit_bytes=limit * 1024 * 1024),
    )


def lane_iota(shape):
    return lax.broadcasted_iota(jnp.int32, shape, len(shape) - 1)


def sublane_iota(shape):
    return lax.broadcasted_iota(jnp.int32, shape, len(shape) - 2)


def swaps(axis):
    count = lax.axis_size(axis)
    inner = [(i, i ^ 1) if i ^ 1 < count else (i, i) for i in range(count)]
    if count % 2:
        outer = [(i, i + 1) if i % 2 else (i, i - 1) if i else (i, i) for i in range(count)]
    else:
        outer = [(i, (i + 1) % count) if i % 2 else (i, (i - 1) % count) for i in range(count)]
    return inner, outer


def row_swaps():
    side = lax.axis_size("gy")
    inner, outer = swaps("gx")
    beside = dict(swaps("gy")[0])
    inner = [(i * side + k, j * side + k) for i, j in inner for k in range(side)]
    outer = [
        (i * side + k, j * side + k) if abs(i - j) == 1 else (i * side + k, i * side + beside[k])
        for i, j in outer
        for k in range(side)
    ]
    return inner, outer


def neighbours(axis):
    index, count = lax.axis_index(axis), lax.axis_size(axis)
    lower = lax.rem(index, 2) == 0
    inner = jnp.logical_or(jnp.logical_not(lower), index + 1 < count)
    outer = jnp.where(lower, index > 0, index + 1 < count)
    return lower, inner, outer


def either(flag, first, second):
    return jnp.where(flag, first, second)


def edge_items():
    moving = [(plane, k) for k in range(MOVING) for plane in (0, 1)]
    return moving + [(2, k) for k in range(DRAGGED)] + [(PLANES, 0)]


def edge_row(plane, k, rows, up):
    return k if up else rows - (MOVING, MOVING, DRAGGED, QUAD)[plane] + k


def pack_kernel(
    vel, fric, thick, surf, ice, ground, own, own_shared, to_inner, to_outer,
    vel_in, fric_in, thick_in, surf_in, ice_in, ground_in, friction32, sems,
):
    members, rows, cols = fric.shape
    tiles, blocks = cols // LANES, rows // BLOCK
    small = [
        pltpu.make_async_copy(source, target, sems.at[k])
        for k, (source, target) in enumerate(
            [(fric, fric_in), (ice, ice_in), (ground, ground_in), (thick, thick_in), (surf, surf_in)]
        )
    ]
    large = [
        [
            pltpu.make_async_copy(
                vel.at[:, pl.ds(b * BLOCK, BLOCK), pl.ds(t * LANES, LANES)],
                vel_in.at[t, b].reshape(2 * members, BLOCK, LANES),
                sems.at[len(small) + b * tiles + t],
            )
            for t in range(tiles)
        ]
        for b in range(blocks)
    ]
    for copy in small + sum(large, []):
        copy.start()
    lower, _, _ = neighbours("gy")
    group = lane_iota((members, LANES)) // SIDE
    sub = sublane_iota((members, LANES))
    for copy in small:
        copy.wait()
    for t in range(tiles):
        friction32[t] = fric_in[:, :, t * LANES : (t + 1) * LANES].astype(F32).reshape(members * rows, LANES)
    near = {}
    for b in range(blocks):
        for t in range(tiles):
            at = (slice(b * BLOCK, (b + 1) * BLOCK), slice(t * LANES, (t + 1) * LANES))
            icef = ice_in[at].astype(F32)
            near[b, t] = (icef, icef * ground_in[at].astype(F32), icef * thick_in[at], surf_in[at])
    strips = [[jnp.zeros((members, LANES), F32)] * 2 for _ in range(rows // QUAD)]

    def place(strip, item, t, value):
        if t == 0:
            head = pltpu.roll(value, item * SIDE, 1) if item else value
            strips[strip][0] = jnp.where(group == item, head, strips[strip][0])
        if t == tiles - 1:
            tail = pltpu.roll(value, (item + 1) * SIDE % LANES, 1)
            strips[strip][1] = jnp.where(group == item, tail, strips[strip][1])

    for strip in range(rows // QUAD):
        b, first = divmod(strip * QUAD, BLOCK)
        for t in range(tiles):
            part = slice(t * LANES, (t + 1) * LANES)
            icef, grounded, thin, top = near[b, t]
            shared = jnp.zeros((members, LANES), F32)
            for step in range(QUAD):
                row = strip * QUAD + step
                at = slice(first + step, first + step + 1)
                shared = jnp.where(sub == 2 * step, thin[at], jnp.where(sub == 2 * step + 1, top[at], shared))
                rough = friction32[t, pl.ds(row, members, stride=rows), :]
                drag = grounded[at] * rough + water_drag * icef[at]
                own[row, 2, :, part] = drag
                place(strip, step * PLANES + 2, t, drag)
            own_shared[strip, :, part] = shared
            place(strip, ITEMS - 1, t, shared)
    for copy in sum(large, []):
        copy.wait()
    for b in range(blocks):
        for row in range(b * BLOCK, (b + 1) * BLOCK):
            strip, step = divmod(row, QUAD)
            at = row - b * BLOCK
            for t in range(tiles):
                icef = near[b, t][0][at : at + 1, :]
                for plane in range(2):
                    value = vel_in[t, b, pl.ds(plane * BLOCK + at, members, stride=2 * BLOCK), :] * icef
                    own[row, plane, :, t * LANES : (t + 1) * LANES] = value
                    place(strip, step * PLANES + plane, t, value)
            if step == QUAD - 1:
                heads, tails = strips[strip]
                to_inner[strip] = either(lower, tails, heads)
                to_outer[strip] = either(lower, heads, tails)


def edge_kernel(own, own_shared, edge_outer, edge_inner):
    rows, _, _, cols = own.shape
    tiles = cols // LANES
    first, _, _ = neighbours("gx")

    def tile(up, plane, k, part):
        if plane == PLANES:
            return own_shared[0 if up else rows // QUAD - 1, :, part]
        return own[edge_row(plane, k, rows, up), plane, :, part]

    for j, (plane, k) in enumerate(edge_items()):
        for t in range(tiles):
            part = slice(t * LANES, (t + 1) * LANES)
            top, bottom = tile(True, plane, k, part), tile(False, plane, k, part)
            edge_inner[j * tiles + t] = either(first, bottom, top)
            edge_outer[j * tiles + t] = either(first, top, bottom)


def side_strips(from_inner, from_outer):
    lower, has_inner, has_outer = neighbours("gy")

    def strips(strip):
        inner = jnp.where(has_inner, from_inner[strip], 0.0)
        outer = jnp.where(has_outer, from_outer[strip], 0.0)
        return either(lower, outer, inner), either(lower, inner, outer)

    return strips


def unpacked(left, right, place, lane):
    if place:
        right = pltpu.roll(right, LANES - place * SIDE, 1)
    if place != GROUPS - 1:
        left = pltpu.roll(left, LANES - (place + 1) * SIDE, 1)
    return jnp.where(lane < SIDE, right, jnp.where(lane >= LANES - SIDE, left, 0.0))


def corner_kernel(from_inner, from_outer, to_outer, to_inner):
    strip_count, members, _ = from_inner.shape
    rows = strip_count * QUAD
    lane = lane_iota((members, LANES))
    strips = side_strips(from_inner, from_outer)
    first, _, _ = neighbours("gx")

    def item(up, plane, k):
        strip, step = divmod(edge_row(plane, k, rows, up), QUAD)
        left, right = strips(strip)
        return unpacked(left, right, ITEMS - 1 if plane == PLANES else step * PLANES + plane, lane)

    top = jnp.zeros((members, LANES), F32)
    bottom = jnp.zeros((members, LANES), F32)
    for j, (plane, k) in enumerate(edge_items()):
        here = lane // (2 * CORNER) == j
        shift = CORNER + 2 * CORNER * j
        top = jnp.where(here, pltpu.roll(item(True, plane, k), shift, 1), top)
        bottom = jnp.where(here, pltpu.roll(item(False, plane, k), shift, 1), bottom)
    to_inner[...] = either(first, bottom, top)
    to_outer[...] = either(first, top, bottom)


def stages(field, shared, slope, store, rows, members, cols):
    visc, sx, sy, sz, tx, ty, tz, rest, inverse, along, across = store
    wide = cols + LANES

    def spread(ref, row, sub):
        strip, step = divmod(row + QUAD, QUAD)
        at = 2 * step + sub
        return jnp.broadcast_to(ref[strip, at : at + 1, :], (members, wide))

    lane = lane_iota((members, LANES))
    count = wide // LANES

    def split(value):
        return [value[:, t * LANES : (t + 1) * LANES] for t in range(count)]

    def after(value):
        parts = split(value)
        return jnp.concatenate(
            [
                pltpu.roll(jnp.where(lane == 0, parts[(t + 1) % count], parts[t]), LANES - 1, 1)
                for t in range(count)
            ],
            axis=1,
        )

    def before(value):
        parts = split(value)
        return jnp.concatenate(
            [
                pltpu.roll(jnp.where(lane == LANES - 1, parts[t - 1], parts[t]), 1, 1)
                for t in range(count)
            ],
            axis=1,
        )

    def incline(strip):
        value = shared[strip]
        slope[strip] = before(value) - after(value)

    def strains(ref, row):
        row = row + DEPTH
        u, v = ref[row, 0], ref[row, 1]
        return (
            ref[row + 1, 0] - ref[row - 1, 0],
            after(v) - before(v),
            (after(u) - before(u)) + (ref[row + 1, 1] - ref[row - 1, 1]),
        )

    def stress(x, y, z, row, strain_u, strain_v, strain_c, nu):
        half = 0.5 * nu
        x[row + DEPTH] = half * (2.0 * strain_u + strain_v)
        y[row + DEPTH] = half * (strain_u + 2.0 * strain_v)
        z[row + DEPTH] = half * (0.5 * strain_c)

    def divergence(x, y, z, row):
        row = row + DEPTH
        shear, normal = z[row], y[row]
        return (
            (x[row + 1] - x[row - 1]) + (after(shear) - before(shear)),
            (after(normal) - before(normal)) + (z[row + 1] - z[row - 1]),
        )

    def viscosity(row):
        su, sv, sc = strains(field, row)
        square = 0.25 * (su * su + sv * sv + su * sv + 0.25 * (sc * sc)) + strain_floor
        nu = (0.5 * spread(shared, row, 0)) * jnp.exp(-flow_power * jnp.log(square))
        visc[row + DEPTH] = nu
        stress(sx, sy, sz, row, su, sv, sc, nu)

    def reciprocal(value):
        guess = pltpu.reciprocal(value, approx=True)
        return guess * (2.0 - value * guess)

    def residual(row):
        div_u, div_v = divergence(sx, sy, sz, row)
        at = row + DEPTH
        drag = field[at, 2]
        on = drag > 0.0
        half = 0.5 * spread(shared, row, 0)
        force_u = half * (spread(shared, row - 1, 1) - spread(shared, row + 1, 1))
        force_v = half * spread(slope, row, 1)
        res_u = force_u - (drag * field[at, 0] - jnp.where(on, div_u, 0.0))
        res_v = force_v - (drag * field[at, 1] - jnp.where(on, div_v, 0.0))
        nu = visc[at]
        near_rows = visc[at + 1] + visc[at - 1]
        near_cols = after(nu) + before(nu)
        inv_u = reciprocal(jnp.where(on, near_rows + 0.25 * near_cols + drag, 1.0))
        inv_v = reciprocal(jnp.where(on, near_cols + 0.25 * near_rows + drag, 1.0))
        rest[at, 0] = res_u
        rest[at, 1] = res_v
        inverse[at, 0] = inv_u
        inverse[at, 1] = inv_v
        along[at, 0] = res_u * inv_u
        along[at, 1] = res_v * inv_v

    def direction(row):
        su, sv, sc = strains(along, row)
        stress(tx, ty, tz, row, su, sv, sc, visc[row + DEPTH])

    def image(row, totals):
        div_u, div_v = divergence(tx, ty, tz, row)
        at = row + DEPTH
        drag = field[at, 2]
        on = drag > 0.0
        dir_u, dir_v = along[at, 0], along[at, 1]
        res_u, res_v = rest[at, 0], rest[at, 1]
        off_u = drag * dir_u - jnp.where(on, div_u, 0.0) - res_u
        off_v = drag * dir_v - jnp.where(on, div_v, 0.0) - res_v
        new_u = off_u * inverse[at, 0]
        new_v = off_v * inverse[at, 1]
        across[at, 0] = new_u
        across[at, 1] = new_v
        if 0 <= row < rows:
            totals[0] += (res_u * dir_u + res_v * dir_v)[:, :cols]
            totals[1] += (res_u * new_u + res_v * new_v)[:, :cols]
            totals[2] += (off_u * new_u + off_v * new_v)[:, :cols]

    def energy(row, totals):
        su, sv, sc = strains(across, row)
        at = row + DEPTH
        u, v = across[at, 0], across[at, 1]
        power = field[at, 2] * (u * u + v * v) + visc[at] * (su * su + su * sv + sv * sv + 0.25 * (sc * sc))
        totals[3] += power[:, :cols]

    return incline, viscosity, residual, direction, image, energy


def run(steps, totals, strips, ranges):
    incline, viscosity, residual, direction, image, energy = steps
    for strip in strips:
        incline(strip)
    for step, over in zip((viscosity, residual, direction), ranges[:3], strict=True):
        for row in over:
            step(row)
    for step, over in zip((image, energy), ranges[3:], strict=True):
        for row in over:
            step(row, totals)


def inner_ranges(rows):
    return [range(k, rows - k) for k in range(1, 6)]


def inner_kernel(own, own_shared, from_inner, from_outer, field, shared, slope, *rest):
    store, totals_ref = rest[:11], rest[11]
    rows, _, members, cols = own.shape
    lane = lane_iota((members, LANES))
    strips = side_strips(from_inner, from_outer)
    for strip in range(rows // QUAD):
        left, right = strips(strip)
        shared[strip + 1, :, :cols] = own_shared[strip]
        shared[strip + 1, :, cols:] = unpacked(left, right, ITEMS - 1, lane)
        for step in range(QUAD):
            row = strip * QUAD + step
            for plane in range(PLANES):
                field[row + DEPTH, plane, :, :cols] = own[row, plane]
                field[row + DEPTH, plane, :, cols:] = unpacked(left, right, step * PLANES + plane, lane)
    totals = [jnp.zeros((members, cols), F32) for _ in range(TOTALS)]
    strips = range(1, rows // QUAD + 1)
    run(stages(field, shared, slope, store, rows, members, cols), totals, strips, inner_ranges(rows))
    for k, total in enumerate(totals):
        totals_ref[k] = total


def outer_kernel(from_outer, from_inner, corner_outer, corner_inner, totals_ref, *refs):
    sums, field, shared, slope, store = refs[14], refs[15], refs[16], refs[17], refs[18:29]
    high, _, members, wide = field.shape
    rows, cols = high - 2 * DEPTH, wide - LANES
    tiles = cols // LANES
    lane = lane_iota((members, LANES))
    lower, has_inner, has_outer = neighbours("gx")

    def both(inner, outer):
        inner = jnp.where(has_inner, inner, 0.0)
        outer = jnp.where(has_outer, outer, 0.0)
        return either(lower, outer, inner), either(lower, inner, outer)

    corners = both(corner_inner[...], corner_outer[...])
    for j, (plane, k) in enumerate(edge_items()):
        above = DEPTH - rows + edge_row(plane, k, rows, False)
        below = DEPTH + rows + edge_row(plane, k, rows, True)
        values = [both(from_inner[j * tiles + t], from_outer[j * tiles + t]) for t in range(tiles)]
        values.append(
            tuple(
                jnp.where(
                    (lane < CORNER) | (lane >= LANES - CORNER),
                    pltpu.roll(corner, LANES - CORNER - 2 * CORNER * j, 1),
                    0.0,
                )
                for corner in corners
            )
        )
        for t, pair in enumerate(values):
            part = slice(t * LANES, (t + 1) * LANES)
            for value, row, strip in zip(pair, (above, below), (0, rows // QUAD + 1), strict=True):
                if plane == PLANES:
                    shared[strip, :, part] = value
                else:
                    field[row, plane, :, part] = value
    inner = inner_ranges(rows)
    ranges = [
        [row for row in range(k, rows - k) if row not in inner[k + 4]] for k in range(-4, 1)
    ]
    totals = [totals_ref[k] for k in range(TOTALS)]
    strips = (0, rows // QUAD + 1)
    run(stages(field, shared, slope, store, rows, members, cols), totals, strips, ranges)
    sub = sublane_iota((members, LANES))
    row = jnp.zeros((members, LANES), F32)
    for k, total in enumerate(totals):
        row = row + jnp.where(lane == sub + members * k, jnp.sum(total, axis=1, keepdims=True), 0.0)
    row = jnp.sum(row, axis=0, keepdims=True)
    sums[...] = jnp.broadcast_to(row[None], sums.shape)


def final_kernel(parts, field, along, across, out, out_tiles, sems):
    high, _, members, wide = field.shape
    rows, cols = high - 2 * DEPTH, wide - LANES
    total = jnp.sum(parts[...], axis=0)
    spread = jnp.broadcast_to(total, (members, LANES))
    lane = lane_iota((members, LANES))
    sub = sublane_iota((members, LANES))
    norm, cross, square, power = (
        jnp.sum(jnp.where(lane == sub + members * k, spread, 0.0), axis=1, keepdims=True)
        for k in range(TOTALS)
    )
    k1, k2, k3 = cross / norm, square / norm, power / norm
    scale = 1.0 + k1
    first = 1.0 / scale
    beta = (k2 - k1 * k1) * first * first
    curve = (k1 * k1 * scale - 2.0 * k1 * (k1 + k2) + k3) * first * first - beta * beta * scale
    second = jnp.where(curve > 0.0, beta / jnp.where(curve > 0.0, curve, 1.0), 0.0)
    on_along = jnp.broadcast_to(first + second * (k1 * first + beta), (members, LANES))
    on_across = jnp.broadcast_to(second * first, (members, LANES))
    tiles = cols // LANES
    copies = []
    for b in range(rows // BLOCK):
        for t in range(tiles):
            place = slice(t * LANES, (t + 1) * LANES)
            for step in range(BLOCK):
                row = DEPTH + b * BLOCK + step
                for part in range(2):
                    out_tiles[t, b, pl.ds(part * BLOCK + step, members, stride=2 * BLOCK), :] = (
                        field[row, part, :, place]
                        + on_along * along[row, part, :, place]
                        - on_across * across[row, part, :, place]
                    )
            copies.append(
                pltpu.make_async_copy(
                    out_tiles.at[t, b].reshape(2 * members, BLOCK, LANES),
                    out.at[:, pl.ds(b * BLOCK, BLOCK), pl.ds(t * LANES, LANES)],
                    sems.at[b * tiles + t],
                )
            )
            copies[-1].start()
    for copy in copies:
        copy.wait()


def per_device(velocity_guess, friction, thickness, surface, ice_mask, grounded_mask):
    members, parts, rows, cols = velocity_guess.shape
    devices = lax.axis_size(("gx", "gy"))
    wide = cols + LANES
    high = rows + 2 * DEPTH
    tiles, blocks = cols // LANES, rows // BLOCK
    tiled = pltpu.VMEM((tiles, blocks, members * parts * BLOCK, LANES), F32)
    strip = vmem((rows // QUAD, members, LANES))
    edge = vmem((len(edge_items()) * tiles, members, LANES))
    own, own_shared, side_inner, side_outer = call(
        pack_kernel,
        [vmem((rows, PLANES, members, cols)), vmem((rows // QUAD, members, cols)), strip, strip],
        ["hbm"] * 6,
        [
            tiled,
            pltpu.VMEM((members, rows, cols), friction.dtype),
            pltpu.VMEM((rows, cols), F32),
            pltpu.VMEM((rows, cols), F32),
            pltpu.VMEM((rows, cols), jnp.int32),
            pltpu.VMEM((rows, cols), jnp.int32),
            pltpu.VMEM((tiles, members * rows, LANES), F32),
            pltpu.SemaphoreType.DMA((5 + tiles * blocks,)),
        ],
        limit=60,
    )(velocity_guess.reshape(members * parts, rows, cols), friction, thickness, surface, ice_mask, grounded_mask)
    inner, outer = swaps("gy")
    side_inner = lax.ppermute(side_inner, "gy", inner)
    side_outer = lax.ppermute(side_outer, "gy", outer)
    inner, outer = row_swaps()
    edge_outer, edge_inner = call(edge_kernel, [edge, edge], ["vmem"] * 2)(own, own_shared)
    edge_outer = lax.ppermute(edge_outer, ("gx", "gy"), outer)
    edge_inner = lax.ppermute(edge_inner, ("gx", "gy"), inner)

    corner = vmem((members, LANES))
    corner_outer, corner_inner = call(corner_kernel, [corner, corner], ["vmem"] * 2)(side_inner, side_outer)
    corner_outer = lax.ppermute(corner_outer, ("gx", "gy"), outer)
    corner_inner = lax.ppermute(corner_inner, ("gx", "gy"), inner)

    one, two = vmem((high, members, wide)), vmem((high, 2, members, wide))
    quads = vmem((rows // QUAD + 2, members, wide))
    held = [vmem((high, PLANES, members, wide)), quads, quads] + [one] * 7 + [two] * 4
    *held_now, totals = call(
        inner_kernel,
        held + [vmem((TOTALS, members, cols))],
        ["vmem"] * 4,
        flops=rows * members * wide * 30000,
    )(own, own_shared, side_inner, side_outer)
    sums, *held_now = call(
        outer_kernel,
        [vmem((devices, 1, LANES))] + held,
        ["vmem"] * 19,
        aliases={5 + k: 1 + k for k in range(14)},
    )(edge_outer, edge_inner, corner_outer, corner_inner, totals, *held_now)
    shares = lax.all_to_all(sums, ("gx", "gy"), 0, 0, tiled=True)
    (out,) = call(
        final_kernel,
        [jax.ShapeDtypeStruct((members * parts, rows, cols), F32)],
        ["vmem"] * 4,
        [tiled, pltpu.SemaphoreType.DMA((tiles * blocks,))],
    )(shares, held_now[0], held_now[-2], held_now[-1])
    return out.reshape(members, parts, rows, cols)


def solution(mesh):
    placed = (
        P(None, None, "gx", "gy"),
        P(None, "gx", "gy"),
        P("gx", "gy"),
        P("gx", "gy"),
        P("gx", "gy"),
        P("gx", "gy"),
    )
    return jax.shard_map(
        per_device, mesh=mesh, in_specs=placed, out_specs=P(None, None, "gx", "gy"), check_vma=False
    )
```

```python
import functools

import jax
import jax.numpy as jnp
from jax import lax
from jax.experimental import pallas as pl
from jax.experimental.pallas import tpu as pltpu
from jax.sharding import PartitionSpec as P

strain_floor = 0.1
water_drag = 0.25
flow_power = 1.0 / 3.0

most_step = 1.0 + 2.5 * 2.25 * strain_floor**-flow_power / water_drag

F32 = jnp.float32
DEPTH = 5
SIDE = 8
CORNER = 4
BLOCK = 8
LANES = 128
PLANES = 3
GROUPS = LANES // SIDE
QUAD = 4
ITEMS = QUAD * PLANES + 1
MOVING = DEPTH
DRAGGED = DEPTH - 2
TOTALS = 4


def vmem(shape):
    return pltpu.VMEM(shape, F32)


def call(kernel, outs, ins, scratch=(), flops=0, limit=24, aliases=None):
    specs = [pl.BlockSpec(memory_space=pltpu.HBM if space == "hbm" else pltpu.VMEM) for space in ins]
    out_specs = [
        pl.BlockSpec(memory_space=pltpu.HBM if isinstance(o, jax.ShapeDtypeStruct) else pltpu.VMEM) for o in outs
    ]
    return pl.pallas_call(
        kernel,
        out_shape=outs,
        in_specs=specs,
        out_specs=out_specs,
        scratch_shapes=scratch,
        input_output_aliases=aliases or {},
        cost_estimate=pl.CostEstimate(flops=flops, bytes_accessed=flops // 8, transcendentals=0),
        compiler_params=pltpu.CompilerParams(vmem_limit_bytes=limit * 1024 * 1024),
    )


def lane_iota(shape):
    return lax.broadcasted_iota(jnp.int32, shape, len(shape) - 1)


def sublane_iota(shape):
    return lax.broadcasted_iota(jnp.int32, shape, len(shape) - 2)


def swaps(axis):
    count = lax.axis_size(axis)
    inner = [(i, i ^ 1) if i ^ 1 < count else (i, i) for i in range(count)]
    if count % 2:
        outer = [(i, i + 1) if i % 2 else (i, i - 1) if i else (i, i) for i in range(count)]
    else:
        outer = [(i, (i + 1) % count) if i % 2 else (i, (i - 1) % count) for i in range(count)]
    return inner, outer


def row_swaps():
    side = lax.axis_size("gy")
    inner, outer = swaps("gx")
    beside = dict(swaps("gy")[0])
    inner = [(i * side + k, j * side + k) for i, j in inner for k in range(side)]
    outer = [
        (i * side + k, j * side + k) if abs(i - j) == 1 else (i * side + k, i * side + beside[k])
        for i, j in outer
        for k in range(side)
    ]
    return inner, outer


def neighbours(axis):
    index, count = lax.axis_index(axis), lax.axis_size(axis)
    lower = lax.rem(index, 2) == 0
    inner = jnp.logical_or(jnp.logical_not(lower), index + 1 < count)
    outer = jnp.where(lower, index > 0, index + 1 < count)
    return lower, inner, outer


def either(flag, first, second):
    return jnp.where(flag, first, second)


def edge_items():
    moving = [(plane, k) for k in range(MOVING) for plane in (0, 1)]
    return moving + [(2, k) for k in range(DRAGGED)] + [(PLANES, 0)]


def edge_row(plane, k, rows, up):
    return k if up else rows - (MOVING, MOVING, DRAGGED, QUAD)[plane] + k


def pack_kernel(
    vel, fric, thick, surf, ice, ground, own, own_shared, to_inner, to_outer,
    vel_in, fric_in, thick_in, surf_in, ice_in, ground_in, friction32, sems,
):
    members, rows, cols = fric.shape
    tiles, blocks = cols // LANES, rows // BLOCK
    small = [
        pltpu.make_async_copy(source, target, sems.at[k])
        for k, (source, target) in enumerate(
            [(fric, fric_in), (ice, ice_in), (ground, ground_in), (thick, thick_in), (surf, surf_in)]
        )
    ]
    large = [
        [
            pltpu.make_async_copy(
                vel.at[:, pl.ds(b * BLOCK, BLOCK), pl.ds(t * LANES, LANES)],
                vel_in.at[t, b].reshape(2 * members, BLOCK, LANES),
                sems.at[len(small) + b * tiles + t],
            )
            for t in range(tiles)
        ]
        for b in range(blocks)
    ]
    for copy in small + sum(large, []):
        copy.start()
    lower, _, _ = neighbours("gy")
    group = lane_iota((members, LANES)) // SIDE
    sub = sublane_iota((members, LANES))
    for copy in small:
        copy.wait()
    for t in range(tiles):
        friction32[t] = fric_in[:, :, t * LANES : (t + 1) * LANES].astype(F32).reshape(members * rows, LANES)
    near = {}
    for b in range(blocks):
        for t in range(tiles):
            at = (slice(b * BLOCK, (b + 1) * BLOCK), slice(t * LANES, (t + 1) * LANES))
            icef = ice_in[at].astype(F32)
            near[b, t] = (icef, icef * ground_in[at].astype(F32), icef * thick_in[at], surf_in[at])
    strips = [[jnp.zeros((members, LANES), F32)] * 2 for _ in range(rows // QUAD)]

    def place(strip, item, t, value):
        if t == 0:
            head = pltpu.roll(value, item * SIDE, 1) if item else value
            strips[strip][0] = jnp.where(group == item, head, strips[strip][0])
        if t == tiles - 1:
            tail = pltpu.roll(value, (item + 1) * SIDE % LANES, 1)
            strips[strip][1] = jnp.where(group == item, tail, strips[strip][1])

    for strip in range(rows // QUAD):
        b, first = divmod(strip * QUAD, BLOCK)
        for t in range(tiles):
            part = slice(t * LANES, (t + 1) * LANES)
            icef, grounded, thin, top = near[b, t]
            shared = jnp.zeros((members, LANES), F32)
            for step in range(QUAD):
                row = strip * QUAD + step
                at = slice(first + step, first + step + 1)
                shared = jnp.where(sub == 2 * step, thin[at], jnp.where(sub == 2 * step + 1, top[at], shared))
                rough = friction32[t, pl.ds(row, members, stride=rows), :]
                drag = grounded[at] * rough + water_drag * icef[at]
                own[row, 2, :, part] = drag
                place(strip, step * PLANES + 2, t, drag)
            own_shared[strip, :, part] = shared
            place(strip, ITEMS - 1, t, shared)
    for copy in sum(large, []):
        copy.wait()
    for b in range(blocks):
        for row in range(b * BLOCK, (b + 1) * BLOCK):
            strip, step = divmod(row, QUAD)
            at = row - b * BLOCK
            for t in range(tiles):
                icef = near[b, t][0][at : at + 1, :]
                for plane in range(2):
                    value = vel_in[t, b, pl.ds(plane * BLOCK + at, members, stride=2 * BLOCK), :] * icef
                    own[row, plane, :, t * LANES : (t + 1) * LANES] = value
                    place(strip, step * PLANES + plane, t, value)
            if step == QUAD - 1:
                heads, tails = strips[strip]
                to_inner[strip] = either(lower, tails, heads)
                to_outer[strip] = either(lower, heads, tails)


def edge_kernel(own, own_shared, edge_outer, edge_inner):
    rows, _, _, cols = own.shape
    tiles = cols // LANES
    first, _, _ = neighbours("gx")

    def tile(up, plane, k, part):
        if plane == PLANES:
            return own_shared[0 if up else rows // QUAD - 1, :, part]
        return own[edge_row(plane, k, rows, up), plane, :, part]

    for j, (plane, k) in enumerate(edge_items()):
        for t in range(tiles):
            part = slice(t * LANES, (t + 1) * LANES)
            top, bottom = tile(True, plane, k, part), tile(False, plane, k, part)
            edge_inner[j * tiles + t] = either(first, bottom, top)
            edge_outer[j * tiles + t] = either(first, top, bottom)


def side_strips(from_inner, from_outer):
    lower, has_inner, has_outer = neighbours("gy")

    def strips(strip):
        inner = jnp.where(has_inner, from_inner[strip], 0.0)
        outer = jnp.where(has_outer, from_outer[strip], 0.0)
        return either(lower, outer, inner), either(lower, inner, outer)

    return strips


def unpacked(left, right, place, lane):
    if place:
        right = pltpu.roll(right, LANES - place * SIDE, 1)
    if place != GROUPS - 1:
        left = pltpu.roll(left, LANES - (place + 1) * SIDE, 1)
    return jnp.where(lane < SIDE, right, jnp.where(lane >= LANES - SIDE, left, 0.0))


def corner_kernel(from_inner, from_outer, to_outer, to_inner):
    strip_count, members, _ = from_inner.shape
    rows = strip_count * QUAD
    lane = lane_iota((members, LANES))
    strips = side_strips(from_inner, from_outer)
    first, _, _ = neighbours("gx")

    def item(up, plane, k):
        strip, step = divmod(edge_row(plane, k, rows, up), QUAD)
        left, right = strips(strip)
        return unpacked(left, right, ITEMS - 1 if plane == PLANES else step * PLANES + plane, lane)

    top = jnp.zeros((members, LANES), F32)
    bottom = jnp.zeros((members, LANES), F32)
    for j, (plane, k) in enumerate(edge_items()):
        here = lane // (2 * CORNER) == j
        shift = CORNER + 2 * CORNER * j
        top = jnp.where(here, pltpu.roll(item(True, plane, k), shift, 1), top)
        bottom = jnp.where(here, pltpu.roll(item(False, plane, k), shift, 1), bottom)
    to_inner[...] = either(first, bottom, top)
    to_outer[...] = either(first, top, bottom)


def stages(field, shared, slope, store, rows, members, cols):
    visc, sx, sy, sz, tx, ty, tz, rest, inverse, along, across = store
    wide = cols + LANES

    def spread(ref, row, sub):
        strip, step = divmod(row + QUAD, QUAD)
        at = 2 * step + sub
        return jnp.broadcast_to(ref[strip, at : at + 1, :], (members, wide))

    lane = lane_iota((members, LANES))
    count = wide // LANES

    def split(value):
        return [value[:, t * LANES : (t + 1) * LANES] for t in range(count)]

    def after(value):
        parts = split(value)
        return jnp.concatenate(
            [
                pltpu.roll(jnp.where(lane == 0, parts[(t + 1) % count], parts[t]), LANES - 1, 1)
                for t in range(count)
            ],
            axis=1,
        )

    def before(value):
        parts = split(value)
        return jnp.concatenate(
            [
                pltpu.roll(jnp.where(lane == LANES - 1, parts[t - 1], parts[t]), 1, 1)
                for t in range(count)
            ],
            axis=1,
        )

    def incline(strip):
        value = shared[strip]
        slope[strip] = before(value) - after(value)

    def strains(ref, row):
        row = row + DEPTH
        u, v = ref[row, 0], ref[row, 1]
        return (
            ref[row + 1, 0] - ref[row - 1, 0],
            after(v) - before(v),
            (after(u) - before(u)) + (ref[row + 1, 1] - ref[row - 1, 1]),
        )

    def stress(x, y, z, row, strain_u, strain_v, strain_c, nu):
        half = 0.5 * nu
        x[row + DEPTH] = half * (2.0 * strain_u + strain_v)
        y[row + DEPTH] = half * (strain_u + 2.0 * strain_v)
        z[row + DEPTH] = half * (0.5 * strain_c)

    def divergence(x, y, z, row):
        row = row + DEPTH
        shear, normal = z[row], y[row]
        return (
            (x[row + 1] - x[row - 1]) + (after(shear) - before(shear)),
            (after(normal) - before(normal)) + (z[row + 1] - z[row - 1]),
        )

    def viscosity(row):
        su, sv, sc = strains(field, row)
        square = 0.25 * (su * su + sv * sv + su * sv + 0.25 * (sc * sc)) + strain_floor
        nu = (0.5 * spread(shared, row, 0)) * jnp.exp(-flow_power * jnp.log(square))
        visc[row + DEPTH] = nu
        stress(sx, sy, sz, row, su, sv, sc, nu)

    def reciprocal(value):
        guess = pltpu.reciprocal(value, approx=True)
        return guess * (2.0 - value * guess)

    def residual(row):
        div_u, div_v = divergence(sx, sy, sz, row)
        at = row + DEPTH
        drag = field[at, 2]
        on = drag > 0.0
        half = 0.5 * spread(shared, row, 0)
        force_u = half * (spread(shared, row - 1, 1) - spread(shared, row + 1, 1))
        force_v = half * spread(slope, row, 1)
        res_u = force_u - (drag * field[at, 0] - jnp.where(on, div_u, 0.0))
        res_v = force_v - (drag * field[at, 1] - jnp.where(on, div_v, 0.0))
        nu = visc[at]
        near_rows = visc[at + 1] + visc[at - 1]
        near_cols = after(nu) + before(nu)
        inv_u = reciprocal(jnp.where(on, near_rows + 0.25 * near_cols + drag, 1.0))
        inv_v = reciprocal(jnp.where(on, near_cols + 0.25 * near_rows + drag, 1.0))
        rest[at, 0] = res_u
        rest[at, 1] = res_v
        inverse[at, 0] = inv_u
        inverse[at, 1] = inv_v
        along[at, 0] = res_u * inv_u
        along[at, 1] = res_v * inv_v

    def direction(row):
        su, sv, sc = strains(along, row)
        stress(tx, ty, tz, row, su, sv, sc, visc[row + DEPTH])

    def image(row, totals):
        div_u, div_v = divergence(tx, ty, tz, row)
        at = row + DEPTH
        drag = field[at, 2]
        on = drag > 0.0
        dir_u, dir_v = along[at, 0], along[at, 1]
        res_u, res_v = rest[at, 0], rest[at, 1]
        off_u = drag * dir_u - jnp.where(on, div_u, 0.0) - res_u
        off_v = drag * dir_v - jnp.where(on, div_v, 0.0) - res_v
        new_u = off_u * inverse[at, 0]
        new_v = off_v * inverse[at, 1]
        across[at, 0] = new_u
        across[at, 1] = new_v
        if 0 <= row < rows:
            totals[0] += (res_u * dir_u + res_v * dir_v)[:, :cols]
            totals[1] += (res_u * new_u + res_v * new_v)[:, :cols]
            totals[2] += (off_u * new_u + off_v * new_v)[:, :cols]

    def energy(row, totals):
        su, sv, sc = strains(across, row)
        at = row + DEPTH
        u, v = across[at, 0], across[at, 1]
        power = field[at, 2] * (u * u + v * v) + visc[at] * (su * su + su * sv + sv * sv + 0.25 * (sc * sc))
        totals[3] += power[:, :cols]

    return incline, viscosity, residual, direction, image, energy


def run(steps, totals, strips, ranges):
    incline, viscosity, residual, direction, image, energy = steps
    for strip in strips:
        incline(strip)
    for step, over in zip((viscosity, residual, direction), ranges[:3], strict=True):
        for row in over:
            step(row)
    for step, over in zip((image, energy), ranges[3:], strict=True):
        for row in over:
            step(row, totals)


def inner_ranges(rows):
    return [range(k, rows - k) for k in range(1, 6)]


def inner_kernel(own, own_shared, from_inner, from_outer, field, shared, slope, *rest):
    store, totals_ref = rest[:11], rest[11]
    rows, _, members, cols = own.shape
    lane = lane_iota((members, LANES))
    strips = side_strips(from_inner, from_outer)
    for strip in range(rows // QUAD):
        left, right = strips(strip)
        shared[strip + 1, :, :cols] = own_shared[strip]
        shared[strip + 1, :, cols:] = unpacked(left, right, ITEMS - 1, lane)
        for step in range(QUAD):
            row = strip * QUAD + step
            for plane in range(PLANES):
                field[row + DEPTH, plane, :, :cols] = own[row, plane]
                field[row + DEPTH, plane, :, cols:] = unpacked(left, right, step * PLANES + plane, lane)
    totals = [jnp.zeros((members, cols), F32) for _ in range(TOTALS)]
    strips = range(1, rows // QUAD + 1)
    run(stages(field, shared, slope, store, rows, members, cols), totals, strips, inner_ranges(rows))
    for k, total in enumerate(totals):
        totals_ref[k] = total


def land(received, valid, below, field, shared):
    high, _, _, wide = field.shape
    rows, tiles = high - 2 * DEPTH, wide // LANES - 1
    for j, (plane, k) in enumerate(edge_items()):
        above = DEPTH - rows + edge_row(plane, k, rows, False)
        row = jnp.where(below, DEPTH + rows + edge_row(plane, k, rows, True), above)
        strip = jnp.where(below, rows // QUAD + 1, 0)
        for t in range(tiles):
            part = slice(t * LANES, (t + 1) * LANES)
            value = jnp.where(valid, received[j * tiles + t], 0.0)
            if plane == PLANES:
                shared[strip, :, part] = value
            else:
                field[row, plane, :, part] = value


def land_kernel(from_inner, _, __, field, shared):
    lower, has_inner, _ = neighbours("gx")
    land(from_inner, has_inner, lower, field, shared)


def outer_kernel(from_outer, corner_outer, corner_inner, totals_ref, *refs):
    sums, field, shared, slope, store = refs[14], refs[15], refs[16], refs[17], refs[18:29]
    high, _, members, wide = field.shape
    rows, cols = high - 2 * DEPTH, wide - LANES
    lane = lane_iota((members, LANES))
    lower, has_inner, has_outer = neighbours("gx")
    land(from_outer, has_outer, jnp.logical_not(lower), field, shared)
    inner = jnp.where(has_inner, corner_inner[...], 0.0)
    outer = jnp.where(has_outer, corner_outer[...], 0.0)
    corners = (either(lower, outer, inner), either(lower, inner, outer))
    for j, (plane, k) in enumerate(edge_items()):
        above = DEPTH - rows + edge_row(plane, k, rows, False)
        below = DEPTH + rows + edge_row(plane, k, rows, True)
        for corner, row, strip in zip(corners, (above, below), (0, rows // QUAD + 1), strict=True):
            value = pltpu.roll(corner, LANES - CORNER - 2 * CORNER * j, 1)
            value = jnp.where((lane < CORNER) | (lane >= LANES - CORNER), value, 0.0)
            if plane == PLANES:
                shared[strip, :, cols:] = value
            else:
                field[row, plane, :, cols:] = value
    inner = inner_ranges(rows)
    ranges = [
        [row for row in range(k, rows - k) if row not in inner[k + 4]] for k in range(-4, 1)
    ]
    totals = [totals_ref[k] for k in range(TOTALS)]
    strips = (0, rows // QUAD + 1)
    run(stages(field, shared, slope, store, rows, members, cols), totals, strips, ranges)
    sub = sublane_iota((members, LANES))
    row = jnp.zeros((members, LANES), F32)
    for k, total in enumerate(totals):
        row = row + jnp.where(lane == sub + members * k, jnp.sum(total, axis=1, keepdims=True), 0.0)
    row = jnp.sum(row, axis=0, keepdims=True)
    sums[...] = jnp.broadcast_to(row[None], sums.shape)


def final_kernel(parts, field, along, across, out, out_tiles, sems):
    high, _, members, wide = field.shape
    rows, cols = high - 2 * DEPTH, wide - LANES
    total = jnp.sum(parts[...], axis=0)
    spread = jnp.broadcast_to(total, (members, LANES))
    lane = lane_iota((members, LANES))
    sub = sublane_iota((members, LANES))
    norm, cross, square, power = (
        jnp.sum(jnp.where(lane == sub + members * k, spread, 0.0), axis=1, keepdims=True)
        for k in range(TOTALS)
    )
    k1, k2, k3 = cross / norm, square / norm, power / norm
    scale = 1.0 + k1
    first = 1.0 / scale
    beta = (k2 - k1 * k1) * first * first
    curve = (k1 * k1 * scale - 2.0 * k1 * (k1 + k2) + k3) * first * first - beta * beta * scale
    second = jnp.where(curve > 0.0, beta / jnp.where(curve > 0.0, curve, 1.0), 0.0)
    second = jnp.clip(second, 0.0, most_step)
    on_along = jnp.broadcast_to(first + second * (k1 * first + beta), (members, LANES))
    on_across = jnp.broadcast_to(second * first, (members, LANES))
    tiles = cols // LANES
    copies = []
    for b in range(rows // BLOCK):
        for t in range(tiles):
            place = slice(t * LANES, (t + 1) * LANES)
            for step in range(BLOCK):
                row = DEPTH + b * BLOCK + step
                for part in range(2):
                    out_tiles[t, b, pl.ds(part * BLOCK + step, members, stride=2 * BLOCK), :] = (
                        field[row, part, :, place]
                        + on_along * along[row, part, :, place]
                        - on_across * across[row, part, :, place]
                    )
            copies.append(
                pltpu.make_async_copy(
                    out_tiles.at[t, b].reshape(2 * members, BLOCK, LANES),
                    out.at[:, pl.ds(b * BLOCK, BLOCK), pl.ds(t * LANES, LANES)],
                    sems.at[b * tiles + t],
                )
            )
            copies[-1].start()
    for copy in copies:
        copy.wait()


def per_device(velocity_guess, friction, thickness, surface, ice_mask, grounded_mask):
    members, parts, rows, cols = velocity_guess.shape
    devices = lax.axis_size(("gx", "gy"))
    wide = cols + LANES
    high = rows + 2 * DEPTH
    tiles, blocks = cols // LANES, rows // BLOCK
    tiled = pltpu.VMEM((tiles, blocks, members * parts * BLOCK, LANES), F32)
    strip = vmem((rows // QUAD, members, LANES))
    edge = vmem((len(edge_items()) * tiles, members, LANES))
    own, own_shared, side_inner, side_outer = call(
        pack_kernel,
        [vmem((rows, PLANES, members, cols)), vmem((rows // QUAD, members, cols)), strip, strip],
        ["hbm"] * 6,
        [
            tiled,
            pltpu.VMEM((members, rows, cols), friction.dtype),
            pltpu.VMEM((rows, cols), F32),
            pltpu.VMEM((rows, cols), F32),
            pltpu.VMEM((rows, cols), jnp.int32),
            pltpu.VMEM((rows, cols), jnp.int32),
            pltpu.VMEM((tiles, members * rows, LANES), F32),
            pltpu.SemaphoreType.DMA((5 + tiles * blocks,)),
        ],
        limit=60,
    )(velocity_guess.reshape(members * parts, rows, cols), friction, thickness, surface, ice_mask, grounded_mask)
    inner, outer = swaps("gy")
    side_inner = lax.ppermute(side_inner, "gy", inner)
    side_outer = lax.ppermute(side_outer, "gy", outer)
    inner, outer = row_swaps()
    edge_outer, edge_inner = call(edge_kernel, [edge, edge], ["vmem"] * 2)(own, own_shared)
    edge_outer = lax.ppermute(edge_outer, ("gx", "gy"), outer)
    edge_inner = lax.ppermute(edge_inner, ("gx", "gy"), inner)

    corner = vmem((members, LANES))
    corner_outer, corner_inner = call(corner_kernel, [corner, corner], ["vmem"] * 2)(side_inner, side_outer)
    corner_outer = lax.ppermute(corner_outer, ("gx", "gy"), outer)
    corner_inner = lax.ppermute(corner_inner, ("gx", "gy"), inner)

    one, two = vmem((high, members, wide)), vmem((high, 2, members, wide))
    quads = vmem((rows // QUAD + 2, members, wide))
    held = [vmem((high, PLANES, members, wide)), quads, quads] + [one] * 7 + [two] * 4
    *held_now, totals = call(
        inner_kernel,
        held + [vmem((TOTALS, members, cols))],
        ["vmem"] * 4,
        flops=rows * members * wide * 10000,
    )(own, own_shared, side_inner, side_outer)
    held_now[:2] = call(
        land_kernel,
        held[:2],
        ["vmem"] * 3,
        flops=rows * members * wide * 10000,
        aliases={1: 0, 2: 1},
    )(edge_inner, *held_now[:2])
    sums, *held_now = call(
        outer_kernel,
        [vmem((devices, 1, LANES))] + held,
        ["vmem"] * 18,
        aliases={4 + k: 1 + k for k in range(14)},
    )(edge_outer, corner_outer, corner_inner, totals, *held_now)
    shares = lax.all_to_all(sums, ("gx", "gy"), 0, 0, tiled=True)
    (out,) = call(
        final_kernel,
        [jax.ShapeDtypeStruct((members * parts, rows, cols), F32)],
        ["vmem"] * 4,
        [tiled, pltpu.SemaphoreType.DMA((tiles * blocks,))],
    )(shares, held_now[0], held_now[-2], held_now[-1])
    return out.reshape(members, parts, rows, cols)


def solution(mesh):
    placed = (
        P(None, None, "gx", "gy"),
        P(None, "gx", "gy"),
        P("gx", "gy"),
        P("gx", "gy"),
        P("gx", "gy"),
        P("gx", "gy"),
    )
    return jax.shard_map(
        per_device, mesh=mesh, in_specs=placed, out_specs=P(None, None, "gx", "gy"), check_vma=False
    )
```

```python
import functools

import jax
import jax.numpy as jnp
from jax import lax
from jax.experimental import pallas as pl
from jax.experimental.pallas import tpu as pltpu
from jax.sharding import PartitionSpec as P

strain_floor = 0.1
water_drag = 0.25
flow_power = 1.0 / 3.0

most_step = 1.0 + 2.5 * 2.25 * strain_floor**-flow_power / water_drag

F32 = jnp.float32
DEPTH = 5
SIDE = 8
CORNER = 4
BLOCK = 8
LANES = 128
PLANES = 3
GROUPS = LANES // SIDE
QUAD = 4
ITEMS = QUAD * PLANES + 1
MOVING = DEPTH
DRAGGED = DEPTH - 2
TOTALS = 4


def vmem(shape):
    return pltpu.VMEM(shape, F32)


def call(kernel, outs, ins, scratch=(), flops=0, limit=24, aliases=None):
    specs = [pl.BlockSpec(memory_space=pltpu.HBM if space == "hbm" else pltpu.VMEM) for space in ins]
    out_specs = [
        pl.BlockSpec(memory_space=pltpu.HBM if isinstance(o, jax.ShapeDtypeStruct) else pltpu.VMEM) for o in outs
    ]
    return pl.pallas_call(
        kernel,
        out_shape=outs,
        in_specs=specs,
        out_specs=out_specs,
        scratch_shapes=scratch,
        input_output_aliases=aliases or {},
        cost_estimate=pl.CostEstimate(flops=flops, bytes_accessed=flops // 8, transcendentals=0),
        compiler_params=pltpu.CompilerParams(vmem_limit_bytes=limit * 1024 * 1024),
    )


def lane_iota(shape):
    return lax.broadcasted_iota(jnp.int32, shape, len(shape) - 1)


def sublane_iota(shape):
    return lax.broadcasted_iota(jnp.int32, shape, len(shape) - 2)


def swaps(axis):
    count = lax.axis_size(axis)
    inner = [(i, i ^ 1) if i ^ 1 < count else (i, i) for i in range(count)]
    if count % 2:
        outer = [(i, i + 1) if i % 2 else (i, i - 1) if i else (i, i) for i in range(count)]
    else:
        outer = [(i, (i + 1) % count) if i % 2 else (i, (i - 1) % count) for i in range(count)]
    return inner, outer


def row_swaps():
    side = lax.axis_size("gy")
    inner, outer = swaps("gx")
    beside = dict(swaps("gy")[0])
    inner = [(i * side + k, j * side + k) for i, j in inner for k in range(side)]
    outer = [
        (i * side + k, j * side + k) if abs(i - j) == 1 else (i * side + k, i * side + beside[k])
        for i, j in outer
        for k in range(side)
    ]
    return inner, outer


def neighbours(axis):
    index, count = lax.axis_index(axis), lax.axis_size(axis)
    lower = lax.rem(index, 2) == 0
    inner = jnp.logical_or(jnp.logical_not(lower), index + 1 < count)
    outer = jnp.where(lower, index > 0, index + 1 < count)
    return lower, inner, outer


def either(flag, first, second):
    return jnp.where(flag, first, second)


def edge_items():
    moving = [(plane, k) for k in range(MOVING) for plane in (0, 1)]
    return moving + [(2, k) for k in range(DRAGGED)] + [(PLANES, 0)]


def edge_row(plane, k, rows, up):
    return k if up else rows - (MOVING, MOVING, DRAGGED, QUAD)[plane] + k


def pack_kernel(
    vel, fric, thick, surf, ice, ground, own, own_shared, to_inner, to_outer,
    vel_in, fric_in, thick_in, surf_in, ice_in, ground_in, friction32, sems,
):
    members, rows, cols = fric.shape
    tiles, blocks = cols // LANES, rows // BLOCK
    small = [
        pltpu.make_async_copy(source, target, sems.at[k])
        for k, (source, target) in enumerate(
            [(fric, fric_in), (ice, ice_in), (ground, ground_in), (thick, thick_in), (surf, surf_in)]
        )
    ]
    large = [
        [
            pltpu.make_async_copy(
                vel.at[:, pl.ds(b * BLOCK, BLOCK), pl.ds(t * LANES, LANES)],
                vel_in.at[t, b].reshape(2 * members, BLOCK, LANES),
                sems.at[len(small) + b * tiles + t],
            )
            for t in range(tiles)
        ]
        for b in range(blocks)
    ]
    for copy in small + sum(large, []):
        copy.start()
    lower, _, _ = neighbours("gy")
    group = lane_iota((members, LANES)) // SIDE
    sub = sublane_iota((members, LANES))
    for copy in small:
        copy.wait()
    for t in range(tiles):
        friction32[t] = fric_in[:, :, t * LANES : (t + 1) * LANES].astype(F32).reshape(members * rows, LANES)
    near = {}
    for b in range(blocks):
        for t in range(tiles):
            at = (slice(b * BLOCK, (b + 1) * BLOCK), slice(t * LANES, (t + 1) * LANES))
            icef = ice_in[at].astype(F32)
            near[b, t] = (icef, icef * ground_in[at].astype(F32), icef * thick_in[at], surf_in[at])
    strips = [[jnp.zeros((members, LANES), F32)] * 2 for _ in range(rows // QUAD)]

    def place(strip, item, t, value):
        if t == 0:
            head = pltpu.roll(value, item * SIDE, 1) if item else value
            strips[strip][0] = jnp.where(group == item, head, strips[strip][0])
        if t == tiles - 1:
            tail = pltpu.roll(value, (item + 1) * SIDE % LANES, 1)
            strips[strip][1] = jnp.where(group == item, tail, strips[strip][1])

    for strip in range(rows // QUAD):
        b, first = divmod(strip * QUAD, BLOCK)
        for t in range(tiles):
            part = slice(t * LANES, (t + 1) * LANES)
            icef, grounded, thin, top = near[b, t]
            shared = jnp.zeros((members, LANES), F32)
            for step in range(QUAD):
                row = strip * QUAD + step
                at = slice(first + step, first + step + 1)
                shared = jnp.where(sub == 2 * step, thin[at], jnp.where(sub == 2 * step + 1, top[at], shared))
                rough = friction32[t, pl.ds(row, members, stride=rows), :]
                drag = grounded[at] * rough + water_drag * icef[at]
                own[row + DEPTH, 2, :, part] = drag
                place(strip, step * PLANES + 2, t, drag)
            own_shared[strip + 1, :, part] = shared
            place(strip, ITEMS - 1, t, shared)
    for copy in sum(large, []):
        copy.wait()
    for b in range(blocks):
        for row in range(b * BLOCK, (b + 1) * BLOCK):
            strip, step = divmod(row, QUAD)
            at = row - b * BLOCK
            for t in range(tiles):
                icef = near[b, t][0][at : at + 1, :]
                for plane in range(2):
                    value = vel_in[t, b, pl.ds(plane * BLOCK + at, members, stride=2 * BLOCK), :] * icef
                    own[row + DEPTH, plane, :, t * LANES : (t + 1) * LANES] = value
                    place(strip, step * PLANES + plane, t, value)
            if step == QUAD - 1:
                heads, tails = strips[strip]
                to_inner[strip] = either(lower, tails, heads)
                to_outer[strip] = either(lower, heads, tails)


def edge_kernel(own, own_shared, edge_outer, edge_inner):
    high, _, _, wide = own.shape
    rows, tiles = high - 2 * DEPTH, wide // LANES - 1
    first, _, _ = neighbours("gx")

    def tile(up, plane, k, part):
        if plane == PLANES:
            return own_shared[1 if up else rows // QUAD, :, part]
        return own[edge_row(plane, k, rows, up) + DEPTH, plane, :, part]

    for j, (plane, k) in enumerate(edge_items()):
        for t in range(tiles):
            part = slice(t * LANES, (t + 1) * LANES)
            top, bottom = tile(True, plane, k, part), tile(False, plane, k, part)
            edge_inner[j * tiles + t] = either(first, bottom, top)
            edge_outer[j * tiles + t] = either(first, top, bottom)


def side_strips(from_inner, from_outer):
    lower, has_inner, has_outer = neighbours("gy")

    def strips(strip):
        inner = jnp.where(has_inner, from_inner[strip], 0.0)
        outer = jnp.where(has_outer, from_outer[strip], 0.0)
        return either(lower, outer, inner), either(lower, inner, outer)

    return strips


def unpacked(left, right, place, lane):
    if place:
        right = pltpu.roll(right, LANES - place * SIDE, 1)
    if place != GROUPS - 1:
        left = pltpu.roll(left, LANES - (place + 1) * SIDE, 1)
    return jnp.where(lane < SIDE, right, jnp.where(lane >= LANES - SIDE, left, 0.0))


def corner_kernel(from_inner, from_outer, to_outer, to_inner):
    strip_count, members, _ = from_inner.shape
    rows = strip_count * QUAD
    lane = lane_iota((members, LANES))
    strips = side_strips(from_inner, from_outer)
    first, _, _ = neighbours("gx")

    def item(up, plane, k, target):
        strip, step = divmod(edge_row(plane, k, rows, up), QUAD)
        left, right = strips(strip)
        place = SIDE * (ITEMS - 1 if plane == PLANES else step * PLANES + plane)
        left = pltpu.roll(left, (target - place - SIDE + CORNER) % LANES, 1)
        right = pltpu.roll(right, (target - place + CORNER) % LANES, 1)
        return jnp.where(lane % (2 * CORNER) < CORNER, left, right)

    top = jnp.zeros((members, LANES), F32)
    bottom = jnp.zeros((members, LANES), F32)
    for j, (plane, k) in enumerate(edge_items()):
        here = lane // (2 * CORNER) == j
        top = jnp.where(here, item(True, plane, k, 2 * CORNER * j), top)
        bottom = jnp.where(here, item(False, plane, k, 2 * CORNER * j), bottom)
    to_inner[...] = either(first, bottom, top)
    to_outer[...] = either(first, top, bottom)


def stages(field, shared, slope, store, rows, members, cols):
    visc, sx, sy, sz, tx, ty, tz, rest, inverse, along, across = store
    wide = cols + LANES

    def spread(ref, row, sub):
        strip, step = divmod(row + QUAD, QUAD)
        at = 2 * step + sub
        return jnp.broadcast_to(ref[strip, at : at + 1, :], (members, wide))

    lane = lane_iota((members, LANES))
    count = wide // LANES

    def split(value):
        return [value[:, t * LANES : (t + 1) * LANES] for t in range(count)]

    def after(value):
        parts = split(value)
        return jnp.concatenate(
            [
                pltpu.roll(jnp.where(lane == 0, parts[(t + 1) % count], parts[t]), LANES - 1, 1)
                for t in range(count)
            ],
            axis=1,
        )

    def before(value):
        parts = split(value)
        return jnp.concatenate(
            [
                pltpu.roll(jnp.where(lane == LANES - 1, parts[t - 1], parts[t]), 1, 1)
                for t in range(count)
            ],
            axis=1,
        )

    def incline(strip):
        value = shared[strip]
        slope[strip] = before(value) - after(value)

    def strains(ref, row):
        row = row + DEPTH
        u, v = ref[row, 0], ref[row, 1]
        return (
            ref[row + 1, 0] - ref[row - 1, 0],
            after(v) - before(v),
            (after(u) - before(u)) + (ref[row + 1, 1] - ref[row - 1, 1]),
        )

    def stress(x, y, z, row, strain_u, strain_v, strain_c, nu):
        half = 0.5 * nu
        x[row + DEPTH] = half * (2.0 * strain_u + strain_v)
        y[row + DEPTH] = half * (strain_u + 2.0 * strain_v)
        z[row + DEPTH] = half * (0.5 * strain_c)

    def divergence(x, y, z, row):
        row = row + DEPTH
        shear, normal = z[row], y[row]
        return (
            (x[row + 1] - x[row - 1]) + (after(shear) - before(shear)),
            (after(normal) - before(normal)) + (z[row + 1] - z[row - 1]),
        )

    def viscosity(row):
        su, sv, sc = strains(field, row)
        square = 0.25 * (su * su + sv * sv + su * sv + 0.25 * (sc * sc)) + strain_floor
        nu = (0.5 * spread(shared, row, 0)) * jnp.exp(-flow_power * jnp.log(square))
        visc[row + DEPTH] = nu
        stress(sx, sy, sz, row, su, sv, sc, nu)

    def reciprocal(value):
        guess = pltpu.reciprocal(value, approx=True)
        return guess * (2.0 - value * guess)

    def residual(row):
        div_u, div_v = divergence(sx, sy, sz, row)
        at = row + DEPTH
        drag = field[at, 2]
        on = drag > 0.0
        half = 0.5 * spread(shared, row, 0)
        force_u = half * (spread(shared, row - 1, 1) - spread(shared, row + 1, 1))
        force_v = half * spread(slope, row, 1)
        res_u = force_u - (drag * field[at, 0] - jnp.where(on, div_u, 0.0))
        res_v = force_v - (drag * field[at, 1] - jnp.where(on, div_v, 0.0))
        nu = visc[at]
        near_rows = visc[at + 1] + visc[at - 1]
        near_cols = after(nu) + before(nu)
        inv_u = reciprocal(jnp.where(on, near_rows + 0.25 * near_cols + drag, 1.0))
        inv_v = reciprocal(jnp.where(on, near_cols + 0.25 * near_rows + drag, 1.0))
        rest[at, 0] = res_u
        rest[at, 1] = res_v
        inverse[at, 0] = inv_u
        inverse[at, 1] = inv_v
        along[at, 0] = res_u * inv_u
        along[at, 1] = res_v * inv_v

    def direction(row):
        su, sv, sc = strains(along, row)
        stress(tx, ty, tz, row, su, sv, sc, visc[row + DEPTH])

    def image(row, totals):
        div_u, div_v = divergence(tx, ty, tz, row)
        at = row + DEPTH
        drag = field[at, 2]
        on = drag > 0.0
        dir_u, dir_v = along[at, 0], along[at, 1]
        res_u, res_v = rest[at, 0], rest[at, 1]
        off_u = drag * dir_u - jnp.where(on, div_u, 0.0) - res_u
        off_v = drag * dir_v - jnp.where(on, div_v, 0.0) - res_v
        new_u = off_u * inverse[at, 0]
        new_v = off_v * inverse[at, 1]
        across[at, 0] = new_u
        across[at, 1] = new_v
        if 0 <= row < rows:
            totals[0] += (res_u * dir_u + res_v * dir_v)[:, :cols]
            totals[1] += (res_u * new_u + res_v * new_v)[:, :cols]
            totals[2] += (off_u * new_u + off_v * new_v)[:, :cols]

    def energy(row, totals):
        su, sv, sc = strains(across, row)
        at = row + DEPTH
        u, v = across[at, 0], across[at, 1]
        power = field[at, 2] * (u * u + v * v) + visc[at] * (su * su + su * sv + sv * sv + 0.25 * (sc * sc))
        totals[3] += power[:, :cols]

    return incline, viscosity, residual, direction, image, energy


def run(steps, totals, strips, ranges):
    incline, viscosity, residual, direction, image, energy = steps
    for strip in strips:
        incline(strip)
    for step, over in zip((viscosity, residual, direction), ranges[:3], strict=True):
        for row in over:
            step(row)
    for step, over in zip((image, energy), ranges[3:], strict=True):
        for row in over:
            step(row, totals)


def inner_ranges(rows):
    return [range(k, rows - k) for k in range(1, 6)]


def inner_kernel(from_inner, from_outer, _, __, field, shared, slope, *rest):
    store, totals_ref = rest[:11], rest[11]
    high, _, members, wide = field.shape
    rows, cols = high - 2 * DEPTH, wide - LANES
    lane = lane_iota((members, LANES))
    strips = side_strips(from_inner, from_outer)
    for strip in range(rows // QUAD):
        left, right = strips(strip)
        shared[strip + 1, :, cols:] = unpacked(left, right, ITEMS - 1, lane)
        for step in range(QUAD):
            row = strip * QUAD + step
            for plane in range(PLANES):
                field[row + DEPTH, plane, :, cols:] = unpacked(left, right, step * PLANES + plane, lane)
    totals = [jnp.zeros((members, cols), F32) for _ in range(TOTALS)]
    strips = range(1, rows // QUAD + 1)
    run(stages(field, shared, slope, store, rows, members, cols), totals, strips, inner_ranges(rows))
    for k, total in enumerate(totals):
        totals_ref[k] = total


def land(received, valid, below, field, shared):
    high, _, _, wide = field.shape
    rows, tiles = high - 2 * DEPTH, wide // LANES - 1
    for j, (plane, k) in enumerate(edge_items()):
        above = DEPTH - rows + edge_row(plane, k, rows, False)
        row = jnp.where(below, DEPTH + rows + edge_row(plane, k, rows, True), above)
        strip = jnp.where(below, rows // QUAD + 1, 0)
        for t in range(tiles):
            part = slice(t * LANES, (t + 1) * LANES)
            value = jnp.where(valid, received[j * tiles + t], 0.0)
            if plane == PLANES:
                shared[strip, :, part] = value
            else:
                field[row, plane, :, part] = value


def land_kernel(from_inner, _, __, field, shared):
    lower, has_inner, _ = neighbours("gx")
    land(from_inner, has_inner, lower, field, shared)


def outer_kernel(from_outer, corner_outer, corner_inner, totals_ref, *refs):
    sums, field, shared, slope, store = refs[14], refs[15], refs[16], refs[17], refs[18:29]
    high, _, members, wide = field.shape
    rows, cols = high - 2 * DEPTH, wide - LANES
    lane = lane_iota((members, LANES))
    lower, has_inner, has_outer = neighbours("gx")
    land(from_outer, has_outer, jnp.logical_not(lower), field, shared)
    inner = jnp.where(has_inner, corner_inner[...], 0.0)
    outer = jnp.where(has_outer, corner_outer[...], 0.0)
    corners = (either(lower, outer, inner), either(lower, inner, outer))
    for j, (plane, k) in enumerate(edge_items()):
        above = DEPTH - rows + edge_row(plane, k, rows, False)
        below = DEPTH + rows + edge_row(plane, k, rows, True)
        for corner, row, strip in zip(corners, (above, below), (0, rows // QUAD + 1), strict=True):
            value = pltpu.roll(corner, LANES - CORNER - 2 * CORNER * j, 1)
            value = jnp.where((lane < CORNER) | (lane >= LANES - CORNER), value, 0.0)
            if plane == PLANES:
                shared[strip, :, cols:] = value
            else:
                field[row, plane, :, cols:] = value
    inner = inner_ranges(rows)
    ranges = [
        [row for row in range(k, rows - k) if row not in inner[k + 4]] for k in range(-4, 1)
    ]
    totals = [totals_ref[k] for k in range(TOTALS)]
    strips = (0, rows // QUAD + 1)
    run(stages(field, shared, slope, store, rows, members, cols), totals, strips, ranges)
    sub = sublane_iota((members, LANES))
    row = jnp.zeros((members, LANES), F32)
    for k, total in enumerate(totals):
        row = row + jnp.where(lane == sub + members * k, jnp.sum(total, axis=1, keepdims=True), 0.0)
    row = jnp.sum(row, axis=0, keepdims=True)
    sums[...] = jnp.broadcast_to(row[None], sums.shape)


def final_kernel(parts, field, along, across, out, out_tiles, sems):
    high, _, members, wide = field.shape
    rows, cols = high - 2 * DEPTH, wide - LANES
    total = jnp.sum(parts[...], axis=0)
    spread = jnp.broadcast_to(total, (members, LANES))
    lane = lane_iota((members, LANES))
    sub = sublane_iota((members, LANES))
    norm, cross, square, power = (
        jnp.sum(jnp.where(lane == sub + members * k, spread, 0.0), axis=1, keepdims=True)
        for k in range(TOTALS)
    )
    k1, k2, k3 = cross / norm, square / norm, power / norm
    scale = 1.0 + k1
    first = 1.0 / scale
    beta = (k2 - k1 * k1) * first * first
    curve = (k1 * k1 * scale - 2.0 * k1 * (k1 + k2) + k3) * first * first - beta * beta * scale
    second = jnp.where(curve > 0.0, beta / jnp.where(curve > 0.0, curve, 1.0), 0.0)
    second = jnp.clip(second, 0.0, most_step)
    on_along = jnp.broadcast_to(first + second * (k1 * first + beta), (members, LANES))
    on_across = jnp.broadcast_to(second * first, (members, LANES))
    tiles = cols // LANES
    copies = []
    for b in range(rows // BLOCK):
        for t in range(tiles):
            place = slice(t * LANES, (t + 1) * LANES)
            for step in range(BLOCK):
                row = DEPTH + b * BLOCK + step
                for part in range(2):
                    out_tiles[t, b, pl.ds(part * BLOCK + step, members, stride=2 * BLOCK), :] = (
                        field[row, part, :, place]
                        + on_along * along[row, part, :, place]
                        - on_across * across[row, part, :, place]
                    )
            copies.append(
                pltpu.make_async_copy(
                    out_tiles.at[t, b].reshape(2 * members, BLOCK, LANES),
                    out.at[:, pl.ds(b * BLOCK, BLOCK), pl.ds(t * LANES, LANES)],
                    sems.at[b * tiles + t],
                )
            )
            copies[-1].start()
    for copy in copies:
        copy.wait()


def per_device(velocity_guess, friction, thickness, surface, ice_mask, grounded_mask):
    members, parts, rows, cols = velocity_guess.shape
    devices = lax.axis_size(("gx", "gy"))
    wide = cols + LANES
    high = rows + 2 * DEPTH
    tiles, blocks = cols // LANES, rows // BLOCK
    tiled = pltpu.VMEM((tiles, blocks, members * parts * BLOCK, LANES), F32)
    strip = vmem((rows // QUAD, members, LANES))
    quads = vmem((rows // QUAD + 2, members, wide))
    edge = vmem((len(edge_items()) * tiles, members, LANES))
    own, own_shared, side_inner, side_outer = call(
        pack_kernel,
        [vmem((high, PLANES, members, wide)), quads, strip, strip],
        ["hbm"] * 6,
        [
            tiled,
            pltpu.VMEM((members, rows, cols), friction.dtype),
            pltpu.VMEM((rows, cols), F32),
            pltpu.VMEM((rows, cols), F32),
            pltpu.VMEM((rows, cols), jnp.int32),
            pltpu.VMEM((rows, cols), jnp.int32),
            pltpu.VMEM((tiles, members * rows, LANES), F32),
            pltpu.SemaphoreType.DMA((5 + tiles * blocks,)),
        ],
        limit=60,
    )(velocity_guess.reshape(members * parts, rows, cols), friction, thickness, surface, ice_mask, grounded_mask)
    inner, outer = swaps("gy")
    side_inner = lax.ppermute(side_inner, "gy", inner)
    side_outer = lax.ppermute(side_outer, "gy", outer)
    inner, outer = row_swaps()
    edge_outer, edge_inner = call(edge_kernel, [edge, edge], ["vmem"] * 2)(own, own_shared)
    edge_outer = lax.ppermute(edge_outer, ("gx", "gy"), outer)
    edge_inner = lax.ppermute(edge_inner, ("gx", "gy"), inner)

    corner = vmem((members, LANES))
    corner_outer, corner_inner = call(corner_kernel, [corner, corner], ["vmem"] * 2)(side_inner, side_outer)
    corner_outer = lax.ppermute(corner_outer, ("gx", "gy"), outer)
    corner_inner = lax.ppermute(corner_inner, ("gx", "gy"), inner)

    one, two = vmem((high, members, wide)), vmem((high, 2, members, wide))
    held = [vmem((high, PLANES, members, wide)), quads, quads] + [one] * 7 + [two] * 4
    *held_now, totals = call(
        inner_kernel,
        held + [vmem((TOTALS, members, cols))],
        ["vmem"] * 4,
        flops=rows * members * wide * 10000,
        aliases={2: 0, 3: 1},
    )(side_inner, side_outer, own, own_shared)
    held_now[:2] = call(
        land_kernel,
        held[:2],
        ["vmem"] * 3,
        flops=rows * members * wide * 10000,
        aliases={1: 0, 2: 1},
    )(edge_inner, *held_now[:2])
    sums, *held_now = call(
        outer_kernel,
        [vmem((devices, 1, LANES))] + held,
        ["vmem"] * 18,
        aliases={4 + k: 1 + k for k in range(14)},
    )(edge_outer, corner_outer, corner_inner, totals, *held_now)
    shares = lax.all_to_all(sums, ("gx", "gy"), 0, 0, tiled=True)
    (out,) = call(
        final_kernel,
        [jax.ShapeDtypeStruct((members * parts, rows, cols), F32)],
        ["vmem"] * 4,
        [tiled, pltpu.SemaphoreType.DMA((tiles * blocks,))],
    )(shares, held_now[0], held_now[-2], held_now[-1])
    return out.reshape(members, parts, rows, cols)


def solution(mesh):
    placed = (
        P(None, None, "gx", "gy"),
        P(None, "gx", "gy"),
        P("gx", "gy"),
        P("gx", "gy"),
        P("gx", "gy"),
        P("gx", "gy"),
    )
    return jax.shard_map(
        per_device, mesh=mesh, in_specs=placed, out_specs=P(None, None, "gx", "gy"), check_vma=False
    )
```

```python
import functools

import jax
import jax.numpy as jnp
from jax import lax
from jax.experimental import pallas as pl
from jax.experimental.pallas import tpu as pltpu
from jax.sharding import PartitionSpec as P

strain_floor = 0.1
water_drag = 0.25
flow_power = 1.0 / 3.0
viscosity_factor = 0.5 * 4.0**flow_power

most_step = 1.0 + 2.5 * 2.25 * strain_floor**-flow_power / water_drag

F32 = jnp.float32
DEPTH = 5
SIDE = 8
CORNER = 4
BLOCK = 8
LANES = 128
PLANES = 3
GROUPS = LANES // SIDE
QUAD = 4
ITEMS = QUAD * PLANES + 1
MOVING = DEPTH
DRAGGED = DEPTH - 2
TOTALS = 4


def vmem(shape):
    return pltpu.VMEM(shape, F32)


def call(kernel, outs, ins, scratch=(), flops=0, limit=24, aliases=None):
    specs = [pl.BlockSpec(memory_space=pltpu.HBM if space == "hbm" else pltpu.VMEM) for space in ins]
    out_specs = [
        pl.BlockSpec(memory_space=pltpu.HBM if isinstance(o, jax.ShapeDtypeStruct) else pltpu.VMEM) for o in outs
    ]
    return pl.pallas_call(
        kernel,
        out_shape=outs,
        in_specs=specs,
        out_specs=out_specs,
        scratch_shapes=scratch,
        input_output_aliases=aliases or {},
        cost_estimate=pl.CostEstimate(flops=flops, bytes_accessed=flops // 8, transcendentals=0),
        compiler_params=pltpu.CompilerParams(vmem_limit_bytes=limit * 1024 * 1024),
    )


def lane_iota(shape):
    return lax.broadcasted_iota(jnp.int32, shape, len(shape) - 1)


def sublane_iota(shape):
    return lax.broadcasted_iota(jnp.int32, shape, len(shape) - 2)


def swaps(axis):
    count = lax.axis_size(axis)
    inner = [(i, i ^ 1) if i ^ 1 < count else (i, i) for i in range(count)]
    if count % 2:
        outer = [(i, i + 1) if i % 2 else (i, i - 1) if i else (i, i) for i in range(count)]
    else:
        outer = [(i, (i + 1) % count) if i % 2 else (i, (i - 1) % count) for i in range(count)]
    return inner, outer


def row_swaps():
    side = lax.axis_size("gy")
    inner, outer = swaps("gx")
    beside = dict(swaps("gy")[0])
    inner = [(i * side + k, j * side + k) for i, j in inner for k in range(side)]
    outer = [
        (i * side + k, j * side + k) if abs(i - j) == 1 else (i * side + k, i * side + beside[k])
        for i, j in outer
        for k in range(side)
    ]
    return inner, outer


def neighbours(axis):
    index, count = lax.axis_index(axis), lax.axis_size(axis)
    lower = lax.rem(index, 2) == 0
    inner = jnp.logical_or(jnp.logical_not(lower), index + 1 < count)
    outer = jnp.where(lower, index > 0, index + 1 < count)
    return lower, inner, outer


def either(flag, first, second):
    return jnp.where(flag, first, second)


def edge_items():
    moving = [(plane, k) for k in range(MOVING) for plane in (0, 1)]
    return moving + [(2, k) for k in range(DRAGGED)] + [(PLANES, 0)]


def edge_row(plane, k, rows, up):
    return k if up else rows - (MOVING, MOVING, DRAGGED, QUAD)[plane] + k


def pack_kernel(
    vel, fric, thick, surf, ice, ground, own, own_shared, to_inner, to_outer,
    vel_in, fric_in, thick_in, surf_in, ice_in, ground_in, friction32, sems,
):
    members, rows, cols = fric.shape
    tiles, blocks = cols // LANES, rows // BLOCK
    small = [
        pltpu.make_async_copy(source, target, sems.at[k])
        for k, (source, target) in enumerate(
            [(fric, fric_in), (ice, ice_in), (ground, ground_in), (thick, thick_in), (surf, surf_in)]
        )
    ]
    large = [
        [
            pltpu.make_async_copy(
                vel.at[:, pl.ds(b * BLOCK, BLOCK), pl.ds(t * LANES, LANES)],
                vel_in.at[t, b].reshape(2 * members, BLOCK, LANES),
                sems.at[len(small) + b * tiles + t],
            )
            for t in range(tiles)
        ]
        for b in range(blocks)
    ]
    for copy in small + sum(large, []):
        copy.start()
    lower, _, _ = neighbours("gy")
    group = lane_iota((members, LANES)) // SIDE
    sub = sublane_iota((members, LANES))
    for copy in small:
        copy.wait()
    for t in range(tiles):
        friction32[t] = fric_in[:, :, t * LANES : (t + 1) * LANES].astype(F32).reshape(members * rows, LANES)
    near = {}
    for b in range(blocks):
        for t in range(tiles):
            at = (slice(b * BLOCK, (b + 1) * BLOCK), slice(t * LANES, (t + 1) * LANES))
            icef = ice_in[at].astype(F32)
            near[b, t] = (icef, icef * ground_in[at].astype(F32), (viscosity_factor * icef) * thick_in[at], surf_in[at])
    strips = [[jnp.zeros((members, LANES), F32)] * 2 for _ in range(rows // QUAD)]

    def place(strip, item, t, value):
        if t == 0:
            head = pltpu.roll(value, item * SIDE, 1) if item else value
            strips[strip][0] = jnp.where(group == item, head, strips[strip][0])
        if t == tiles - 1:
            tail = pltpu.roll(value, (item + 1) * SIDE % LANES, 1)
            strips[strip][1] = jnp.where(group == item, tail, strips[strip][1])

    for strip in range(rows // QUAD):
        b, first = divmod(strip * QUAD, BLOCK)
        for t in range(tiles):
            part = slice(t * LANES, (t + 1) * LANES)
            icef, grounded, thin, top = near[b, t]
            shared = jnp.zeros((members, LANES), F32)
            for step in range(QUAD):
                row = strip * QUAD + step
                at = slice(first + step, first + step + 1)
                shared = jnp.where(sub == 2 * step, thin[at], jnp.where(sub == 2 * step + 1, top[at], shared))
                rough = friction32[t, pl.ds(row, members, stride=rows), :]
                drag = grounded[at] * rough + water_drag * icef[at]
                own[row + DEPTH, 2, :, part] = drag
                place(strip, step * PLANES + 2, t, drag)
            own_shared[strip + 1, :, part] = shared
            place(strip, ITEMS - 1, t, shared)
    for copy in sum(large, []):
        copy.wait()
    for b in range(blocks):
        for row in range(b * BLOCK, (b + 1) * BLOCK):
            strip, step = divmod(row, QUAD)
            at = row - b * BLOCK
            for t in range(tiles):
                icef = near[b, t][0][at : at + 1, :]
                for plane in range(2):
                    value = vel_in[t, b, pl.ds(plane * BLOCK + at, members, stride=2 * BLOCK), :] * icef
                    own[row + DEPTH, plane, :, t * LANES : (t + 1) * LANES] = value
                    place(strip, step * PLANES + plane, t, value)
            if step == QUAD - 1:
                heads, tails = strips[strip]
                to_inner[strip] = either(lower, tails, heads)
                to_outer[strip] = either(lower, heads, tails)


def edge_kernel(own, own_shared, edge_outer, edge_inner):
    high, _, _, wide = own.shape
    rows, tiles = high - 2 * DEPTH, wide // LANES - 1
    first, _, _ = neighbours("gx")

    def tile(up, plane, k, part):
        if plane == PLANES:
            return own_shared[1 if up else rows // QUAD, :, part]
        return own[edge_row(plane, k, rows, up) + DEPTH, plane, :, part]

    for j, (plane, k) in enumerate(edge_items()):
        for t in range(tiles):
            part = slice(t * LANES, (t + 1) * LANES)
            top, bottom = tile(True, plane, k, part), tile(False, plane, k, part)
            edge_inner[j * tiles + t] = either(first, bottom, top)
            edge_outer[j * tiles + t] = either(first, top, bottom)


def side_strips(from_inner, from_outer):
    lower, has_inner, has_outer = neighbours("gy")

    def strips(strip):
        inner = jnp.where(has_inner, from_inner[strip], 0.0)
        outer = jnp.where(has_outer, from_outer[strip], 0.0)
        return either(lower, outer, inner), either(lower, inner, outer)

    return strips


def unpacked(left, right, place, lane):
    if place:
        right = pltpu.roll(right, LANES - place * SIDE, 1)
    if place != GROUPS - 1:
        left = pltpu.roll(left, LANES - (place + 1) * SIDE, 1)
    return jnp.where(lane < SIDE, right, jnp.where(lane >= LANES - SIDE, left, 0.0))


def corner_kernel(from_inner, from_outer, to_outer, to_inner):
    strip_count, members, _ = from_inner.shape
    rows = strip_count * QUAD
    lane = lane_iota((members, LANES))
    strips = side_strips(from_inner, from_outer)
    first, _, _ = neighbours("gx")

    def item(up, plane, k, target):
        strip, step = divmod(edge_row(plane, k, rows, up), QUAD)
        left, right = strips(strip)
        place = SIDE * (ITEMS - 1 if plane == PLANES else step * PLANES + plane)
        left = pltpu.roll(left, (target - place - SIDE + CORNER) % LANES, 1)
        right = pltpu.roll(right, (target - place + CORNER) % LANES, 1)
        return jnp.where(lane % (2 * CORNER) < CORNER, left, right)

    top = jnp.zeros((members, LANES), F32)
    bottom = jnp.zeros((members, LANES), F32)
    for j, (plane, k) in enumerate(edge_items()):
        here = lane // (2 * CORNER) == j
        top = jnp.where(here, item(True, plane, k, 2 * CORNER * j), top)
        bottom = jnp.where(here, item(False, plane, k, 2 * CORNER * j), bottom)
    to_inner[...] = either(first, bottom, top)
    to_outer[...] = either(first, top, bottom)


def stages(field, shared, slope, store, rows, members, cols):
    visc, sx, sy, sz, tx, ty, tz, rest, inverse, along, across = store
    wide = cols + LANES

    def spread(ref, row, sub):
        strip, step = divmod(row + QUAD, QUAD)
        at = 2 * step + sub
        return jnp.broadcast_to(ref[strip, at : at + 1, :], (members, wide))

    lane = lane_iota((members, LANES))
    count = wide // LANES

    def split(value):
        return [value[:, t * LANES : (t + 1) * LANES] for t in range(count)]

    def after(value):
        parts = split(value)
        return jnp.concatenate(
            [
                pltpu.roll(jnp.where(lane == 0, parts[(t + 1) % count], parts[t]), LANES - 1, 1)
                for t in range(count)
            ],
            axis=1,
        )

    def before(value):
        parts = split(value)
        return jnp.concatenate(
            [
                pltpu.roll(jnp.where(lane == LANES - 1, parts[t - 1], parts[t]), 1, 1)
                for t in range(count)
            ],
            axis=1,
        )

    def incline(strip):
        value = shared[strip]
        slope[strip] = before(value) - after(value)

    def strains(ref, row):
        row = row + DEPTH
        u, v = ref[row, 0], ref[row, 1]
        return (
            ref[row + 1, 0] - ref[row - 1, 0],
            after(v) - before(v),
            (after(u) - before(u)) + (ref[row + 1, 1] - ref[row - 1, 1]),
        )

    def leans(strain_u, strain_v, strain_c):
        return strain_u + 0.5 * strain_v, strain_v + 0.5 * strain_u, 0.25 * strain_c

    def stress(x, y, z, row, nu, p, q, c):
        x[row + DEPTH] = nu * p
        y[row + DEPTH] = nu * q
        z[row + DEPTH] = nu * c

    def divergence(x, y, z, row):
        row = row + DEPTH
        shear, normal = z[row], y[row]
        return (
            (x[row + 1] - x[row - 1]) + (after(shear) - before(shear)),
            (after(normal) - before(normal)) + (z[row + 1] - z[row - 1]),
        )

    def viscosity(row):
        su, sv, sc = strains(field, row)
        p, q, c = leans(su, sv, sc)
        square = (su * p + sv * q + sc * c) + 4.0 * strain_floor
        nu = spread(shared, row, 0) * jnp.exp(-flow_power * jnp.log(square))
        visc[row + DEPTH] = nu
        stress(sx, sy, sz, row, nu, p, q, c)

    def reciprocal(value):
        guess = pltpu.reciprocal(value, approx=True)
        return guess * (2.0 - value * guess)

    def residual(row):
        div_u, div_v = divergence(sx, sy, sz, row)
        at = row + DEPTH
        drag = field[at, 2]
        on = drag > 0.0
        half = (0.5 / viscosity_factor) * spread(shared, row, 0)
        force_u = half * (spread(shared, row - 1, 1) - spread(shared, row + 1, 1))
        force_v = half * spread(slope, row, 1)
        res_u = force_u - (drag * field[at, 0] - jnp.where(on, div_u, 0.0))
        res_v = force_v - (drag * field[at, 1] - jnp.where(on, div_v, 0.0))
        nu = visc[at]
        near_rows = visc[at + 1] + visc[at - 1]
        near_cols = after(nu) + before(nu)
        inv_u = reciprocal(jnp.where(on, near_rows + 0.25 * near_cols + drag, 1.0))
        inv_v = reciprocal(jnp.where(on, near_cols + 0.25 * near_rows + drag, 1.0))
        rest[at, 0] = res_u
        rest[at, 1] = res_v
        inverse[at, 0] = inv_u
        inverse[at, 1] = inv_v
        along[at, 0] = res_u * inv_u
        along[at, 1] = res_v * inv_v

    def direction(row):
        su, sv, sc = strains(along, row)
        stress(tx, ty, tz, row, visc[row + DEPTH], *leans(su, sv, sc))

    def image(row, totals):
        div_u, div_v = divergence(tx, ty, tz, row)
        at = row + DEPTH
        drag = field[at, 2]
        on = drag > 0.0
        dir_u, dir_v = along[at, 0], along[at, 1]
        res_u, res_v = rest[at, 0], rest[at, 1]
        off_u = drag * dir_u - jnp.where(on, div_u, 0.0) - res_u
        off_v = drag * dir_v - jnp.where(on, div_v, 0.0) - res_v
        new_u = off_u * inverse[at, 0]
        new_v = off_v * inverse[at, 1]
        across[at, 0] = new_u
        across[at, 1] = new_v
        if 0 <= row < rows:
            totals[0] += (res_u * dir_u + res_v * dir_v)[:, :cols]
            totals[1] += (res_u * new_u + res_v * new_v)[:, :cols]
            totals[2] += (off_u * new_u + off_v * new_v)[:, :cols]

    def energy(row, totals):
        su, sv, sc = strains(across, row)
        at = row + DEPTH
        u, v = across[at, 0], across[at, 1]
        power = field[at, 2] * (u * u + v * v) + visc[at] * (su * (su + sv) + sv * sv + 0.25 * (sc * sc))
        totals[3] += power[:, :cols]

    return incline, viscosity, residual, direction, image, energy


def run(steps, totals, strips, ranges):
    incline, viscosity, residual, direction, image, energy = steps
    for strip in strips:
        incline(strip)
    for step, over in zip((viscosity, residual, direction), ranges[:3], strict=True):
        for row in over:
            step(row)
    for step, over in zip((image, energy), ranges[3:], strict=True):
        for row in over:
            step(row, totals)


def inner_ranges(rows):
    return [range(k, rows - k) for k in range(1, 6)]


def inner_kernel(from_inner, from_outer, _, __, field, shared, slope, *rest):
    store, totals_ref = rest[:11], rest[11]
    high, _, members, wide = field.shape
    rows, cols = high - 2 * DEPTH, wide - LANES
    lane = lane_iota((members, LANES))
    strips = side_strips(from_inner, from_outer)
    for strip in range(rows // QUAD):
        left, right = strips(strip)
        shared[strip + 1, :, cols:] = unpacked(left, right, ITEMS - 1, lane)
        for step in range(QUAD):
            row = strip * QUAD + step
            for plane in range(PLANES):
                field[row + DEPTH, plane, :, cols:] = unpacked(left, right, step * PLANES + plane, lane)
    totals = [jnp.zeros((members, cols), F32) for _ in range(TOTALS)]
    strips = range(1, rows // QUAD + 1)
    run(stages(field, shared, slope, store, rows, members, cols), totals, strips, inner_ranges(rows))
    for k, total in enumerate(totals):
        totals_ref[k] = total


def land(received, valid, below, field, shared):
    high, _, _, wide = field.shape
    rows, tiles = high - 2 * DEPTH, wide // LANES - 1
    for j, (plane, k) in enumerate(edge_items()):
        above = DEPTH - rows + edge_row(plane, k, rows, False)
        row = jnp.where(below, DEPTH + rows + edge_row(plane, k, rows, True), above)
        strip = jnp.where(below, rows // QUAD + 1, 0)
        for t in range(tiles):
            part = slice(t * LANES, (t + 1) * LANES)
            value = jnp.where(valid, received[j * tiles + t], 0.0)
            if plane == PLANES:
                shared[strip, :, part] = value
            else:
                field[row, plane, :, part] = value


def land_kernel(from_inner, _, __, field, shared):
    lower, has_inner, _ = neighbours("gx")
    land(from_inner, has_inner, lower, field, shared)


def outer_kernel(from_outer, corner_outer, corner_inner, totals_ref, *refs):
    sums, field, shared, slope, store = refs[14], refs[15], refs[16], refs[17], refs[18:29]
    high, _, members, wide = field.shape
    rows, cols = high - 2 * DEPTH, wide - LANES
    lane = lane_iota((members, LANES))
    lower, has_inner, has_outer = neighbours("gx")
    land(from_outer, has_outer, jnp.logical_not(lower), field, shared)
    inner = jnp.where(has_inner, corner_inner[...], 0.0)
    outer = jnp.where(has_outer, corner_outer[...], 0.0)
    corners = (either(lower, outer, inner), either(lower, inner, outer))
    for j, (plane, k) in enumerate(edge_items()):
        above = DEPTH - rows + edge_row(plane, k, rows, False)
        below = DEPTH + rows + edge_row(plane, k, rows, True)
        for corner, row, strip in zip(corners, (above, below), (0, rows // QUAD + 1), strict=True):
            value = pltpu.roll(corner, LANES - CORNER - 2 * CORNER * j, 1)
            value = jnp.where((lane < CORNER) | (lane >= LANES - CORNER), value, 0.0)
            if plane == PLANES:
                shared[strip, :, cols:] = value
            else:
                field[row, plane, :, cols:] = value
    inner = inner_ranges(rows)
    ranges = [
        [row for row in range(k, rows - k) if row not in inner[k + 4]] for k in range(-4, 1)
    ]
    totals = [totals_ref[k] for k in range(TOTALS)]
    strips = (0, rows // QUAD + 1)
    run(stages(field, shared, slope, store, rows, members, cols), totals, strips, ranges)
    sub = sublane_iota((members, LANES))
    row = jnp.zeros((members, LANES), F32)
    for k, total in enumerate(totals):
        row = row + jnp.where(lane == sub + members * k, jnp.sum(total, axis=1, keepdims=True), 0.0)
    row = jnp.sum(row, axis=0, keepdims=True)
    sums[...] = jnp.broadcast_to(row[None], sums.shape)


def final_kernel(parts, field, along, across, out, out_tiles, sems):
    high, _, members, wide = field.shape
    rows, cols = high - 2 * DEPTH, wide - LANES
    total = jnp.sum(parts[...], axis=0)
    spread = jnp.broadcast_to(total, (members, LANES))
    lane = lane_iota((members, LANES))
    sub = sublane_iota((members, LANES))
    norm, cross, square, power = (
        jnp.sum(jnp.where(lane == sub + members * k, spread, 0.0), axis=1, keepdims=True)
        for k in range(TOTALS)
    )
    k1, k2, k3 = cross / norm, square / norm, power / norm
    scale = 1.0 + k1
    first = 1.0 / scale
    beta = (k2 - k1 * k1) * first * first
    curve = (k1 * k1 * scale - 2.0 * k1 * (k1 + k2) + k3) * first * first - beta * beta * scale
    second = jnp.where(curve > 0.0, beta / jnp.where(curve > 0.0, curve, 1.0), 0.0)
    second = jnp.clip(second, 0.0, most_step)
    on_along = jnp.broadcast_to(first + second * (k1 * first + beta), (members, LANES))
    on_across = jnp.broadcast_to(second * first, (members, LANES))
    tiles = cols // LANES
    copies = []
    for b in range(rows // BLOCK):
        for t in range(tiles):
            place = slice(t * LANES, (t + 1) * LANES)
            for step in range(BLOCK):
                row = DEPTH + b * BLOCK + step
                for part in range(2):
                    out_tiles[t, b, pl.ds(part * BLOCK + step, members, stride=2 * BLOCK), :] = (
                        field[row, part, :, place]
                        + on_along * along[row, part, :, place]
                        - on_across * across[row, part, :, place]
                    )
            copies.append(
                pltpu.make_async_copy(
                    out_tiles.at[t, b].reshape(2 * members, BLOCK, LANES),
                    out.at[:, pl.ds(b * BLOCK, BLOCK), pl.ds(t * LANES, LANES)],
                    sems.at[b * tiles + t],
                )
            )
            copies[-1].start()
    for copy in copies:
        copy.wait()


def per_device(velocity_guess, friction, thickness, surface, ice_mask, grounded_mask):
    members, parts, rows, cols = velocity_guess.shape
    devices = lax.axis_size(("gx", "gy"))
    wide = cols + LANES
    high = rows + 2 * DEPTH
    tiles, blocks = cols // LANES, rows // BLOCK
    tiled = pltpu.VMEM((tiles, blocks, members * parts * BLOCK, LANES), F32)
    strip = vmem((rows // QUAD, members, LANES))
    quads = vmem((rows // QUAD + 2, members, wide))
    edge = vmem((len(edge_items()) * tiles, members, LANES))
    own, own_shared, side_inner, side_outer = call(
        pack_kernel,
        [vmem((high, PLANES, members, wide)), quads, strip, strip],
        ["hbm"] * 6,
        [
            tiled,
            pltpu.VMEM((members, rows, cols), friction.dtype),
            pltpu.VMEM((rows, cols), F32),
            pltpu.VMEM((rows, cols), F32),
            pltpu.VMEM((rows, cols), jnp.int32),
            pltpu.VMEM((rows, cols), jnp.int32),
            pltpu.VMEM((tiles, members * rows, LANES), F32),
            pltpu.SemaphoreType.DMA((5 + tiles * blocks,)),
        ],
        limit=60,
    )(velocity_guess.reshape(members * parts, rows, cols), friction, thickness, surface, ice_mask, grounded_mask)
    inner, outer = swaps("gy")
    side_inner = lax.ppermute(side_inner, "gy", inner)
    side_outer = lax.ppermute(side_outer, "gy", outer)
    inner, outer = row_swaps()
    edge_outer, edge_inner = call(edge_kernel, [edge, edge], ["vmem"] * 2)(own, own_shared)
    edge_outer = lax.ppermute(edge_outer, ("gx", "gy"), outer)
    edge_inner = lax.ppermute(edge_inner, ("gx", "gy"), inner)

    corner = vmem((members, LANES))
    corner_outer, corner_inner = call(corner_kernel, [corner, corner], ["vmem"] * 2)(side_inner, side_outer)
    corner_outer = lax.ppermute(corner_outer, ("gx", "gy"), outer)
    corner_inner = lax.ppermute(corner_inner, ("gx", "gy"), inner)

    one, two = vmem((high, members, wide)), vmem((high, 2, members, wide))
    held = [vmem((high, PLANES, members, wide)), quads, quads] + [one] * 7 + [two] * 4
    *held_now, totals = call(
        inner_kernel,
        held + [vmem((TOTALS, members, cols))],
        ["vmem"] * 4,
        flops=rows * members * wide * 10000,
        aliases={2: 0, 3: 1},
    )(side_inner, side_outer, own, own_shared)
    held_now[:2] = call(
        land_kernel,
        held[:2],
        ["vmem"] * 3,
        flops=rows * members * wide * 10000,
        aliases={1: 0, 2: 1},
    )(edge_inner, *held_now[:2])
    sums, *held_now = call(
        outer_kernel,
        [vmem((devices, 1, LANES))] + held,
        ["vmem"] * 18,
        aliases={4 + k: 1 + k for k in range(14)},
    )(edge_outer, corner_outer, corner_inner, totals, *held_now)
    shares = lax.all_to_all(sums, ("gx", "gy"), 0, 0, tiled=True)
    (out,) = call(
        final_kernel,
        [jax.ShapeDtypeStruct((members * parts, rows, cols), F32)],
        ["vmem"] * 4,
        [tiled, pltpu.SemaphoreType.DMA((tiles * blocks,))],
    )(shares, held_now[0], held_now[-2], held_now[-1])
    return out.reshape(members, parts, rows, cols)


def solution(mesh):
    placed = (
        P(None, None, "gx", "gy"),
        P(None, "gx", "gy"),
        P("gx", "gy"),
        P("gx", "gy"),
        P("gx", "gy"),
        P("gx", "gy"),
    )
    return jax.shard_map(
        per_device, mesh=mesh, in_specs=placed, out_specs=P(None, None, "gx", "gy"), check_vma=False
    )
```

```python
import functools

import jax
import jax.numpy as jnp
from jax import lax
from jax.experimental import pallas as pl
from jax.experimental.pallas import tpu as pltpu
from jax.sharding import PartitionSpec as P

strain_floor = 0.1
water_drag = 0.25
flow_power = 1.0 / 3.0
viscosity_factor = 0.5 * 4.0**flow_power

most_step = 1.0 + 2.5 * 2.25 * strain_floor**-flow_power / water_drag

F32 = jnp.float32
DEPTH = 5
SIDE = 8
CORNER = 4
BLOCK = 8
LANES = 128
PLANES = 3
GROUPS = LANES // SIDE
QUAD = 4
ITEMS = QUAD * PLANES + 1
MOVING = DEPTH
DRAGGED = DEPTH - 2
TOTALS = 4


def vmem(shape):
    return pltpu.VMEM(shape, F32)


def call(kernel, outs, ins, scratch=(), flops=0, limit=24, aliases=None):
    specs = [pl.BlockSpec(memory_space=pltpu.HBM if space == "hbm" else pltpu.VMEM) for space in ins]
    out_specs = [
        pl.BlockSpec(memory_space=pltpu.HBM if isinstance(o, jax.ShapeDtypeStruct) else pltpu.VMEM) for o in outs
    ]
    return pl.pallas_call(
        kernel,
        out_shape=outs,
        in_specs=specs,
        out_specs=out_specs,
        scratch_shapes=scratch,
        input_output_aliases=aliases or {},
        cost_estimate=pl.CostEstimate(flops=flops, bytes_accessed=flops // 8, transcendentals=0),
        compiler_params=pltpu.CompilerParams(vmem_limit_bytes=limit * 1024 * 1024),
    )


def lane_iota(shape):
    return lax.broadcasted_iota(jnp.int32, shape, len(shape) - 1)


def sublane_iota(shape):
    return lax.broadcasted_iota(jnp.int32, shape, len(shape) - 2)


def swaps(axis):
    count = lax.axis_size(axis)
    inner = [(i, i ^ 1) if i ^ 1 < count else (i, i) for i in range(count)]
    if count % 2:
        outer = [(i, i + 1) if i % 2 else (i, i - 1) if i else (i, i) for i in range(count)]
    else:
        outer = [(i, (i + 1) % count) if i % 2 else (i, (i - 1) % count) for i in range(count)]
    return inner, outer


def row_swaps():
    side = lax.axis_size("gy")
    inner, outer = swaps("gx")
    beside = dict(swaps("gy")[0])
    inner = [(i * side + k, j * side + k) for i, j in inner for k in range(side)]
    outer = [
        (i * side + k, j * side + k) if abs(i - j) == 1 else (i * side + k, i * side + beside[k])
        for i, j in outer
        for k in range(side)
    ]
    return inner, outer


def neighbours(axis):
    index, count = lax.axis_index(axis), lax.axis_size(axis)
    lower = lax.rem(index, 2) == 0
    inner = jnp.logical_or(jnp.logical_not(lower), index + 1 < count)
    outer = jnp.where(lower, index > 0, index + 1 < count)
    return lower, inner, outer


def either(flag, first, second):
    return jnp.where(flag, first, second)


def edge_items():
    moving = [(plane, k) for k in range(MOVING) for plane in (0, 1)]
    return moving + [(2, k) for k in range(DRAGGED)] + [(PLANES, 0)]


def edge_row(plane, k, rows, up):
    return k if up else rows - (MOVING, MOVING, DRAGGED, QUAD)[plane] + k


def pack_kernel(
    vel, fric, thick, surf, ice, ground, own, own_shared, to_inner, to_outer,
    vel_in, fric_in, thick_in, surf_in, ice_in, ground_in, friction32, sems,
):
    members, rows, cols = fric.shape
    tiles, blocks = cols // LANES, rows // BLOCK
    small = [
        pltpu.make_async_copy(source, target, sems.at[k])
        for k, (source, target) in enumerate(
            [(fric, fric_in), (ice, ice_in), (ground, ground_in), (thick, thick_in), (surf, surf_in)]
        )
    ]
    large = [
        [
            pltpu.make_async_copy(
                vel.at[:, pl.ds(b * BLOCK, BLOCK), pl.ds(t * LANES, LANES)],
                vel_in.at[t, b].reshape(2 * members, BLOCK, LANES),
                sems.at[len(small) + b * tiles + t],
            )
            for t in range(tiles)
        ]
        for b in range(blocks)
    ]
    for copy in small + sum(large, []):
        copy.start()
    lower, _, _ = neighbours("gy")
    group = lane_iota((members, LANES)) // SIDE
    sub = sublane_iota((members, LANES))
    for copy in small:
        copy.wait()
    for t in range(tiles):
        friction32[t] = fric_in[:, :, t * LANES : (t + 1) * LANES].astype(F32).reshape(members * rows, LANES)
    near = {}
    for b in range(blocks):
        for t in range(tiles):
            at = (slice(b * BLOCK, (b + 1) * BLOCK), slice(t * LANES, (t + 1) * LANES))
            icef = ice_in[at].astype(F32)
            near[b, t] = (icef, icef * ground_in[at].astype(F32), (viscosity_factor * icef) * thick_in[at], surf_in[at])
    strips = [[jnp.zeros((members, LANES), F32)] * 2 for _ in range(rows // QUAD)]

    def place(strip, item, t, value):
        if t == 0:
            head = pltpu.roll(value, item * SIDE, 1) if item else value
            strips[strip][0] = jnp.where(group == item, head, strips[strip][0])
        if t == tiles - 1:
            tail = pltpu.roll(value, (item + 1) * SIDE % LANES, 1)
            strips[strip][1] = jnp.where(group == item, tail, strips[strip][1])

    for strip in range(rows // QUAD):
        b, first = divmod(strip * QUAD, BLOCK)
        for t in range(tiles):
            part = slice(t * LANES, (t + 1) * LANES)
            icef, grounded, thin, top = near[b, t]
            shared = jnp.zeros((members, LANES), F32)
            for step in range(QUAD):
                row = strip * QUAD + step
                at = slice(first + step, first + step + 1)
                shared = jnp.where(sub == 2 * step, thin[at], jnp.where(sub == 2 * step + 1, top[at], shared))
                rough = friction32[t, pl.ds(row, members, stride=rows), :]
                drag = grounded[at] * rough + water_drag * icef[at]
                own[row + DEPTH, 2, :, part] = drag
                place(strip, step * PLANES + 2, t, drag)
            own_shared[strip + 1, :, part] = shared
            place(strip, ITEMS - 1, t, shared)
    for copy in sum(large, []):
        copy.wait()
    for b in range(blocks):
        for row in range(b * BLOCK, (b + 1) * BLOCK):
            strip, step = divmod(row, QUAD)
            at = row - b * BLOCK
            for t in range(tiles):
                icef = near[b, t][0][at : at + 1, :]
                for plane in range(2):
                    value = vel_in[t, b, pl.ds(plane * BLOCK + at, members, stride=2 * BLOCK), :] * icef
                    own[row + DEPTH, plane, :, t * LANES : (t + 1) * LANES] = value
                    place(strip, step * PLANES + plane, t, value)
            if step == QUAD - 1:
                heads, tails = strips[strip]
                to_inner[strip] = either(lower, tails, heads)
                to_outer[strip] = either(lower, heads, tails)


def edge_kernel(own, own_shared, edge_outer, edge_inner):
    high, _, _, wide = own.shape
    rows, tiles = high - 2 * DEPTH, wide // LANES - 1
    first, _, _ = neighbours("gx")

    def tile(up, plane, k, part):
        if plane == PLANES:
            return own_shared[1 if up else rows // QUAD, :, part]
        return own[edge_row(plane, k, rows, up) + DEPTH, plane, :, part]

    for j, (plane, k) in enumerate(edge_items()):
        for t in range(tiles):
            part = slice(t * LANES, (t + 1) * LANES)
            top, bottom = tile(True, plane, k, part), tile(False, plane, k, part)
            edge_inner[j * tiles + t] = either(first, bottom, top)
            edge_outer[j * tiles + t] = either(first, top, bottom)


def side_strips(from_inner, from_outer):
    lower, has_inner, has_outer = neighbours("gy")

    def strips(strip):
        inner = jnp.where(has_inner, from_inner[strip], 0.0)
        outer = jnp.where(has_outer, from_outer[strip], 0.0)
        return either(lower, outer, inner), either(lower, inner, outer)

    return strips


def unpacked(left, right, place, lane):
    if place:
        right = pltpu.roll(right, LANES - place * SIDE, 1)
    if place != GROUPS - 1:
        left = pltpu.roll(left, LANES - (place + 1) * SIDE, 1)
    return jnp.where(lane < SIDE, right, jnp.where(lane >= LANES - SIDE, left, 0.0))


def corner_kernel(from_inner, from_outer, to_outer, to_inner):
    strip_count, members, _ = from_inner.shape
    rows = strip_count * QUAD
    lane = lane_iota((members, LANES))
    strips = side_strips(from_inner, from_outer)
    first, _, _ = neighbours("gx")

    def item(up, plane, k, target):
        strip, step = divmod(edge_row(plane, k, rows, up), QUAD)
        left, right = strips(strip)
        place = SIDE * (ITEMS - 1 if plane == PLANES else step * PLANES + plane)
        left = pltpu.roll(left, (target - place - SIDE + CORNER) % LANES, 1)
        right = pltpu.roll(right, (target - place + CORNER) % LANES, 1)
        return jnp.where(lane % (2 * CORNER) < CORNER, left, right)

    top = jnp.zeros((members, LANES), F32)
    bottom = jnp.zeros((members, LANES), F32)
    for j, (plane, k) in enumerate(edge_items()):
        here = lane // (2 * CORNER) == j
        top = jnp.where(here, item(True, plane, k, 2 * CORNER * j), top)
        bottom = jnp.where(here, item(False, plane, k, 2 * CORNER * j), bottom)
    to_inner[...] = either(first, bottom, top)
    to_outer[...] = either(first, top, bottom)


def stages(field, shared, slope, store, rows, members, cols):
    visc, sx, sy, sz, tx, ty, tz, rest, inverse, along, across = store
    wide = cols + LANES

    def spread(ref, row, sub):
        strip, step = divmod(row + QUAD, QUAD)
        at = 2 * step + sub
        return jnp.broadcast_to(ref[strip, at : at + 1, :], (members, wide))

    lane = lane_iota((members, LANES))
    count = wide // LANES

    def split(value):
        return [value[:, t * LANES : (t + 1) * LANES] for t in range(count)]

    def after(value):
        parts = split(value)
        return jnp.concatenate(
            [
                pltpu.roll(jnp.where(lane == 0, parts[(t + 1) % count], parts[t]), LANES - 1, 1)
                for t in range(count)
            ],
            axis=1,
        )

    def before(value):
        parts = split(value)
        return jnp.concatenate(
            [
                pltpu.roll(jnp.where(lane == LANES - 1, parts[t - 1], parts[t]), 1, 1)
                for t in range(count)
            ],
            axis=1,
        )

    def incline(strip):
        value = shared[strip]
        slope[strip] = before(value) - after(value)

    def strains(ref, row):
        row = row + DEPTH
        u, v = ref[row, 0], ref[row, 1]
        return (
            ref[row + 1, 0] - ref[row - 1, 0],
            after(v) - before(v),
            (after(u) - before(u)) + (ref[row + 1, 1] - ref[row - 1, 1]),
        )

    def leans(strain_u, strain_v, strain_c):
        return strain_u + 0.5 * strain_v, strain_v + 0.5 * strain_u, 0.25 * strain_c

    def stress(x, y, z, row, nu, p, q, c, reach):
        x[row + DEPTH] = nu * p
        if -reach < row < rows - 1 + reach:
            y[row + DEPTH] = nu * q
        z[row + DEPTH] = nu * c

    def divergence(x, y, z, row):
        row = row + DEPTH
        shear, normal = z[row], y[row]
        return (
            (x[row + 1] - x[row - 1]) + (after(shear) - before(shear)),
            (after(normal) - before(normal)) + (z[row + 1] - z[row - 1]),
        )

    def viscosity(row):
        su, sv, sc = strains(field, row)
        p, q, c = leans(su, sv, sc)
        square = (su * p + sv * q + sc * c) + 4.0 * strain_floor
        nu = spread(shared, row, 0) * jnp.exp(-flow_power * jnp.log(square))
        visc[row + DEPTH] = nu
        stress(sx, sy, sz, row, nu, p, q, c, DEPTH - 1)

    def reciprocal(value):
        guess = pltpu.reciprocal(value, approx=True)
        return guess * (2.0 - value * guess)

    def residual(row):
        div_u, div_v = divergence(sx, sy, sz, row)
        at = row + DEPTH
        drag = field[at, 2]
        on = drag > 0.0
        half = (0.5 / viscosity_factor) * spread(shared, row, 0)
        force_u = half * (spread(shared, row - 1, 1) - spread(shared, row + 1, 1))
        force_v = half * spread(slope, row, 1)
        res_u = force_u - (drag * field[at, 0] - jnp.where(on, div_u, 0.0))
        res_v = force_v - (drag * field[at, 1] - jnp.where(on, div_v, 0.0))
        nu = visc[at]
        near_rows = visc[at + 1] + visc[at - 1]
        near_cols = after(nu) + before(nu)
        inv_u = reciprocal(jnp.where(on, near_rows + 0.25 * near_cols + drag, 1.0))
        inv_v = reciprocal(jnp.where(on, near_cols + 0.25 * near_rows + drag, 1.0))
        rest[at, 0] = res_u
        rest[at, 1] = res_v
        inverse[at, 0] = inv_u
        inverse[at, 1] = inv_v
        along[at, 0] = res_u * inv_u
        along[at, 1] = res_v * inv_v

    def direction(row):
        su, sv, sc = strains(along, row)
        stress(tx, ty, tz, row, visc[row + DEPTH], *leans(su, sv, sc), DEPTH - 3)

    def image(row, totals):
        div_u, div_v = divergence(tx, ty, tz, row)
        at = row + DEPTH
        drag = field[at, 2]
        on = drag > 0.0
        dir_u, dir_v = along[at, 0], along[at, 1]
        res_u, res_v = rest[at, 0], rest[at, 1]
        off_u = drag * dir_u - jnp.where(on, div_u, 0.0) - res_u
        off_v = drag * dir_v - jnp.where(on, div_v, 0.0) - res_v
        new_u = off_u * inverse[at, 0]
        new_v = off_v * inverse[at, 1]
        across[at, 0] = new_u
        across[at, 1] = new_v
        if 0 <= row < rows:
            totals[0] += (res_u * dir_u + res_v * dir_v)[:, :cols]
            totals[1] += (res_u * new_u + res_v * new_v)[:, :cols]
            totals[2] += (off_u * new_u + off_v * new_v)[:, :cols]

    def energy(row, totals):
        su, sv, sc = strains(across, row)
        at = row + DEPTH
        u, v = across[at, 0], across[at, 1]
        power = field[at, 2] * (u * u + v * v) + visc[at] * (su * (su + sv) + sv * sv + 0.25 * (sc * sc))
        totals[3] += power[:, :cols]

    return incline, viscosity, residual, direction, image, energy


def run(steps, totals, strips, ranges):
    incline, viscosity, residual, direction, image, energy = steps
    for strip in strips:
        incline(strip)
    for step, over in zip((viscosity, residual, direction), ranges[:3], strict=True):
        for row in over:
            step(row)
    for step, over in zip((image, energy), ranges[3:], strict=True):
        for row in over:
            step(row, totals)


def inner_ranges(rows):
    return [range(k, rows - k) for k in range(1, 6)]


def inner_kernel(from_inner, from_outer, _, __, field, shared, slope, *rest):
    store, totals_ref = rest[:11], rest[11]
    high, _, members, wide = field.shape
    rows, cols = high - 2 * DEPTH, wide - LANES
    lane = lane_iota((members, LANES))
    strips = side_strips(from_inner, from_outer)
    for strip in range(rows // QUAD):
        left, right = strips(strip)
        shared[strip + 1, :, cols:] = unpacked(left, right, ITEMS - 1, lane)
        for step in range(QUAD):
            row = strip * QUAD + step
            for plane in range(PLANES):
                field[row + DEPTH, plane, :, cols:] = unpacked(left, right, step * PLANES + plane, lane)
    totals = [jnp.zeros((members, cols), F32) for _ in range(TOTALS)]
    strips = range(1, rows // QUAD + 1)
    run(stages(field, shared, slope, store, rows, members, cols), totals, strips, inner_ranges(rows))
    for k, total in enumerate(totals):
        totals_ref[k] = total


def land(received, valid, below, field, shared):
    high, _, _, wide = field.shape
    rows, tiles = high - 2 * DEPTH, wide // LANES - 1
    for j, (plane, k) in enumerate(edge_items()):
        above = DEPTH - rows + edge_row(plane, k, rows, False)
        row = jnp.where(below, DEPTH + rows + edge_row(plane, k, rows, True), above)
        strip = jnp.where(below, rows // QUAD + 1, 0)
        for t in range(tiles):
            part = slice(t * LANES, (t + 1) * LANES)
            value = jnp.where(valid, received[j * tiles + t], 0.0)
            if plane == PLANES:
                shared[strip, :, part] = value
            else:
                field[row, plane, :, part] = value


def land_kernel(from_inner, _, __, field, shared):
    lower, has_inner, _ = neighbours("gx")
    land(from_inner, has_inner, lower, field, shared)


def outer_kernel(from_outer, corner_outer, corner_inner, totals_ref, *refs):
    sums, field, shared, slope, store = refs[14], refs[15], refs[16], refs[17], refs[18:29]
    high, _, members, wide = field.shape
    rows, cols = high - 2 * DEPTH, wide - LANES
    lane = lane_iota((members, LANES))
    lower, has_inner, has_outer = neighbours("gx")
    land(from_outer, has_outer, jnp.logical_not(lower), field, shared)
    inner = jnp.where(has_inner, corner_inner[...], 0.0)
    outer = jnp.where(has_outer, corner_outer[...], 0.0)
    corners = (either(lower, outer, inner), either(lower, inner, outer))
    for j, (plane, k) in enumerate(edge_items()):
        above = DEPTH - rows + edge_row(plane, k, rows, False)
        below = DEPTH + rows + edge_row(plane, k, rows, True)
        for corner, row, strip in zip(corners, (above, below), (0, rows // QUAD + 1), strict=True):
            value = pltpu.roll(corner, LANES - CORNER - 2 * CORNER * j, 1)
            value = jnp.where((lane < CORNER) | (lane >= LANES - CORNER), value, 0.0)
            if plane == PLANES:
                shared[strip, :, cols:] = value
            else:
                field[row, plane, :, cols:] = value
    inner = inner_ranges(rows)
    ranges = [
        [row for row in range(k, rows - k) if row not in inner[k + 4]] for k in range(-4, 1)
    ]
    totals = [totals_ref[k] for k in range(TOTALS)]
    strips = (0, rows // QUAD + 1)
    run(stages(field, shared, slope, store, rows, members, cols), totals, strips, ranges)
    sub = sublane_iota((members, LANES))
    row = jnp.zeros((members, LANES), F32)
    for k, total in enumerate(totals):
        row = row + jnp.where(lane == sub + members * k, jnp.sum(total, axis=1, keepdims=True), 0.0)
    row = jnp.sum(row, axis=0, keepdims=True)
    sums[...] = jnp.broadcast_to(row[None], sums.shape)


def final_kernel(parts, field, along, across, out, out_tiles, sems):
    high, _, members, wide = field.shape
    rows, cols = high - 2 * DEPTH, wide - LANES
    total = jnp.sum(parts[...], axis=0)
    spread = jnp.broadcast_to(total, (members, LANES))
    lane = lane_iota((members, LANES))
    sub = sublane_iota((members, LANES))
    norm, cross, square, power = (
        jnp.sum(jnp.where(lane == sub + members * k, spread, 0.0), axis=1, keepdims=True)
        for k in range(TOTALS)
    )
    k1, k2, k3 = cross / norm, square / norm, power / norm
    scale = 1.0 + k1
    first = 1.0 / scale
    beta = (k2 - k1 * k1) * first * first
    curve = (k1 * k1 * scale - 2.0 * k1 * (k1 + k2) + k3) * first * first - beta * beta * scale
    second = jnp.where(curve > 0.0, beta / jnp.where(curve > 0.0, curve, 1.0), 0.0)
    second = jnp.clip(second, 0.0, most_step)
    on_along = jnp.broadcast_to(first + second * (k1 * first + beta), (members, LANES))
    on_across = jnp.broadcast_to(second * first, (members, LANES))
    tiles = cols // LANES
    copies = []
    for b in range(rows // BLOCK):
        for t in range(tiles):
            place = slice(t * LANES, (t + 1) * LANES)
            for step in range(BLOCK):
                row = DEPTH + b * BLOCK + step
                for part in range(2):
                    out_tiles[t, b, pl.ds(part * BLOCK + step, members, stride=2 * BLOCK), :] = (
                        field[row, part, :, place]
                        + on_along * along[row, part, :, place]
                        - on_across * across[row, part, :, place]
                    )
            copies.append(
                pltpu.make_async_copy(
                    out_tiles.at[t, b].reshape(2 * members, BLOCK, LANES),
                    out.at[:, pl.ds(b * BLOCK, BLOCK), pl.ds(t * LANES, LANES)],
                    sems.at[b * tiles + t],
                )
            )
            copies[-1].start()
    for copy in copies:
        copy.wait()


def per_device(velocity_guess, friction, thickness, surface, ice_mask, grounded_mask):
    members, parts, rows, cols = velocity_guess.shape
    devices = lax.axis_size(("gx", "gy"))
    wide = cols + LANES
    high = rows + 2 * DEPTH
    tiles, blocks = cols // LANES, rows // BLOCK
    tiled = pltpu.VMEM((tiles, blocks, members * parts * BLOCK, LANES), F32)
    strip = vmem((rows // QUAD, members, LANES))
    quads = vmem((rows // QUAD + 2, members, wide))
    edge = vmem((len(edge_items()) * tiles, members, LANES))
    own, own_shared, side_inner, side_outer = call(
        pack_kernel,
        [vmem((high, PLANES, members, wide)), quads, strip, strip],
        ["hbm"] * 6,
        [
            tiled,
            pltpu.VMEM((members, rows, cols), friction.dtype),
            pltpu.VMEM((rows, cols), F32),
            pltpu.VMEM((rows, cols), F32),
            pltpu.VMEM((rows, cols), jnp.int32),
            pltpu.VMEM((rows, cols), jnp.int32),
            pltpu.VMEM((tiles, members * rows, LANES), F32),
            pltpu.SemaphoreType.DMA((5 + tiles * blocks,)),
        ],
        limit=60,
    )(velocity_guess.reshape(members * parts, rows, cols), friction, thickness, surface, ice_mask, grounded_mask)
    inner, outer = swaps("gy")
    side_inner = lax.ppermute(side_inner, "gy", inner)
    side_outer = lax.ppermute(side_outer, "gy", outer)
    inner, outer = row_swaps()
    edge_outer, edge_inner = call(edge_kernel, [edge, edge], ["vmem"] * 2)(own, own_shared)
    edge_outer = lax.ppermute(edge_outer, ("gx", "gy"), outer)
    edge_inner = lax.ppermute(edge_inner, ("gx", "gy"), inner)

    corner = vmem((members, LANES))
    corner_outer, corner_inner = call(corner_kernel, [corner, corner], ["vmem"] * 2)(side_inner, side_outer)
    corner_outer = lax.ppermute(corner_outer, ("gx", "gy"), outer)
    corner_inner = lax.ppermute(corner_inner, ("gx", "gy"), inner)

    one, two = vmem((high, members, wide)), vmem((high, 2, members, wide))
    held = [vmem((high, PLANES, members, wide)), quads, quads] + [one] * 7 + [two] * 4
    *held_now, totals = call(
        inner_kernel,
        held + [vmem((TOTALS, members, cols))],
        ["vmem"] * 4,
        flops=rows * members * wide * 10000,
        aliases={2: 0, 3: 1},
    )(side_inner, side_outer, own, own_shared)
    held_now[:2] = call(
        land_kernel,
        held[:2],
        ["vmem"] * 3,
        flops=rows * members * wide * 10000,
        aliases={1: 0, 2: 1},
    )(edge_inner, *held_now[:2])
    sums, *held_now = call(
        outer_kernel,
        [vmem((devices, 1, LANES))] + held,
        ["vmem"] * 18,
        aliases={4 + k: 1 + k for k in range(14)},
    )(edge_outer, corner_outer, corner_inner, totals, *held_now)
    shares = lax.all_to_all(sums, ("gx", "gy"), 0, 0, tiled=True)
    (out,) = call(
        final_kernel,
        [jax.ShapeDtypeStruct((members * parts, rows, cols), F32)],
        ["vmem"] * 4,
        [tiled, pltpu.SemaphoreType.DMA((tiles * blocks,))],
    )(shares, held_now[0], held_now[-2], held_now[-1])
    return out.reshape(members, parts, rows, cols)


def solution(mesh):
    placed = (
        P(None, None, "gx", "gy"),
        P(None, "gx", "gy"),
        P("gx", "gy"),
        P("gx", "gy"),
        P("gx", "gy"),
        P("gx", "gy"),
    )
    return jax.shard_map(
        per_device, mesh=mesh, in_specs=placed, out_specs=P(None, None, "gx", "gy"), check_vma=False
    )
```
